32 devices in a mesh: pipe: 2 (over core), expert: 16 (over z, y, x).
Axes of the slice: x: 2, y: 2, z: 4, core: 2. Of those that a mesh axis runs over, the one named last changes fastest.
Arguments:
- a_input: bfloat16 [2, 2048, 3584], P('pipe', 'expert'), may hold values from -6 to 6
- a_route: int32 [2, 2048, 1], P('pipe', 'expert'), may hold values from 0 to 3; in each aligned block of 128 rows (0 to 127, 128 to 255, ..., all dimensions but the last counted through in order) at most 34 rows name the same one
- b_saved: bfloat16 [2, 2048, 3584], P('pipe', 'expert'), may hold values from -6 to 6
- b_grad: bfloat16 [2, 2048, 3584], P('pipe', 'expert'), may hold values from -6 to 6
- b_route: int32 [2, 2048, 1], P('pipe', 'expert'), may hold values from 0 to 3; in each aligned block of 128 rows (0 to 127, 128 to 255, ..., all dimensions but the last counted through in order) at most 34 rows name the same one
- up_weight: bfloat16 [2, 3584, 4096], P('pipe', None, 'expert'), may hold values from -0.09375 to 0.09375
- down_weight: bfloat16 [2, 4096, 3584], P('pipe', 'expert'), may hold values from -0.1875 to 0.1875
- router: bfloat16 [2, 3584, 4], P('pipe'), may hold values from -0.09375 to 0.09375
Outputs:
- a_next: bfloat16 [2, 2048, 3584], P('pipe', 'expert')
- b_next: bfloat16 [2, 2048, 3584], P('pipe', 'expert')
- up_grad: bfloat16 [2, 3584, 4096], P('pipe', None, 'expert')
- down_grad: bfloat16 [2, 4096, 3584], P('pipe', 'expert')
The draws below stay inside these ranges and needn't reach their ends.
Inputs may be any that keep to these rules, and one draw needn't show every extreme that they name: `a_route`: within each device's 128 rows, no expert is named by more than 34 of the (token, choice) pairs, a bound that some block reaches. `b_route`: within each device's 128 rows, no expert is named by more than 34 of the (token, choice) pairs, a bound that some block reaches.
All inputs are finite; a program needn't handle non-finite values.
Results may differ from the reference program's by a relative error of at most 0.0067.
Values may be sent and summed in bfloat16 or wider, within the bound.
No kernel may reach another device: no remote copies, remote signals or barrier semaphores. Data moves between devices by JAX's collectives and lax.ppermute only.
A program may use at most 128 MiB of HBM per device.

```python
import math
import jax
import jax.numpy as jnp
import numpy as np
from jax import lax

D = 3584
FF = 1024
GROUP = 4
TOP = 1
TOK = 128
HID = 256
EXPERTS = 4
CAP = 34
TOKENS = 2048
N_PIPE = 2
N_EXPERT = 16


def level_of(key, dims, split, smallest, high):
    def one(axis_at, shards_of):
        heights = jax.random.uniform(jax.random.fold_in(jax.random.fold_in(key, 6), axis_at), (shards_of,), jnp.float32, smallest / len(split), high / len(split))
        return jnp.repeat(jnp.exp(heights), dims[axis_at] // shards_of).reshape((-1,) + (1,) * (len(dims) - axis_at - 1))

    level = one(*split[0])
    for cut in split[1:]:
        level = level * one(*cut)
    return level


def routed_block(own_key, own, number, rows, amount, top, most, skew):
    ranking = jax.random.permutation(own_key, amount)
    heavy_load, usual = load_shares(amount, rows * top, most, skew, True), load_shares(amount, rows * top, most, skew, False)
    places = jnp.arange(amount)

    def named(sizes, rotation):
        used = int((sizes > 0).sum())
        fixed = max(1, used // 4)
        moved = fixed + (places - fixed + rotation * (used - fixed)) % max(1, amount - fixed)
        return jnp.zeros((amount,), jnp.int32).at[ranking[jnp.where(places < fixed, places, moved)]].set(jnp.asarray(sizes, jnp.int32))

    sizes = jnp.where(number % 4 == 0, named(heavy_load, number // 4), named(usual, number - number // 4 - 1))
    mixed = jax.random.permutation(jax.random.fold_in(own, 3), amount)
    giver, receiver = mixed[0:amount // 2 * 2:2], mixed[1:amount // 2 * 2:2]
    margin = jnp.minimum(sizes[giver] - 1, most - sizes[receiver]) // 2
    margin = jnp.where((giver == ranking[0]) | (receiver == ranking[0]) | (sizes[receiver] == 0), 0, jnp.maximum(margin, 0))
    moved = jax.random.randint(jax.random.fold_in(own, 4), (amount // 2,), 0, 1 << 20) % (margin + 1)
    sizes = sizes.at[giver].add(-moved).at[receiver].add(moved)
    labels = jnp.searchsorted(jnp.cumsum(sizes), jnp.arange(rows * top), side="right").astype(jnp.int32)
    grid = labels.reshape(top, rows).T
    grid = grid[jax.random.permutation(jax.random.fold_in(own, 1), rows)]
    rotation = jax.random.randint(jax.random.fold_in(own, 2), (rows, 1), 0, top)
    return jnp.take_along_axis(grid, (jnp.arange(top)[None, :] + rotation) % top, axis=1)


def load_shares(number_of, total, bound, slope, full):
    loads = [(1 << 20) // math.isqrt(grade ** slope) + 1 for grade in range(1, number_of + 1)]
    largest = bound if full else min(bound, max(-(-total // number_of), total * loads[0] // sum(loads)))
    least = 1 if total - largest >= number_of - 1 else 0
    counts, rest = [largest] + [least] * (number_of - 1), total - largest - least * (number_of - 1)
    while rest > 0:
        movable = [i for i in range(1, number_of) if counts[i] < largest] or [i for i in range(1, number_of) if counts[i] < bound]
        mass, budget = sum([loads[i] for i in movable]), rest
        for i in movable:
            more = min(bound - counts[i], max(1, budget * loads[i] // mass), rest)
            counts[i] = counts[i] + more
            rest = rest - more
    return np.array(counts)


def bell_draw(rng, shape, scale, limit, pieces=(), kind=jnp.bfloat16):
    level = level_of(rng, shape, pieces, -0.22, 0.18) if pieces else 1.0
    result = jax.random.normal(rng, shape, jnp.float32) * scale * level
    return jnp.minimum(jnp.maximum(result, -limit), limit).astype(kind)


def setup_inputs(seed: int = 0) -> dict:
    keys = jax.random.split(jax.random.key(seed), 9)
    a_input = bell_draw(keys[0], (N_PIPE, TOKENS, D), 1.0, 6.0, ((0, 2), (1, 16)))
    a_route_keys = jax.random.split(jax.random.fold_in(keys[1], 1), N_PIPE * TOKENS // TOK)
    a_route_turns = jax.random.permutation(jax.random.fold_in(keys[1], 3), N_PIPE * TOKENS // TOK)
    a_route = jax.vmap(lambda own, number: routed_block(jax.random.fold_in(keys[1], 2), own, number, TOK, EXPERTS, TOP, CAP, 1))(a_route_keys, a_route_turns).reshape((N_PIPE, TOKENS, TOP))
    b_saved = bell_draw(keys[2], (N_PIPE, TOKENS, D), 1.0, 6.0, ((0, 2), (1, 16)))
    b_grad = bell_draw(keys[3], (N_PIPE, TOKENS, D), 1.0, 6.0, ((0, 2), (1, 16)))
    b_route_keys = jax.random.split(jax.random.fold_in(keys[4], 1), N_PIPE * TOKENS // TOK)
    b_route_turns = jax.random.permutation(jax.random.fold_in(keys[4], 3), N_PIPE * TOKENS // TOK)
    b_route = jax.vmap(lambda own, number: routed_block(jax.random.fold_in(keys[4], 2), own, number, TOK, EXPERTS, TOP, CAP, 1))(b_route_keys, b_route_turns).reshape((N_PIPE, TOKENS, TOP))
    up_weight = bell_draw(keys[5], (N_PIPE, D, EXPERTS * FF), D ** -0.5, 0.09375, ((0, 2), (2, 16)))
    down_weight = bell_draw(keys[6], (N_PIPE, EXPERTS * FF, D), FF ** -0.5, 0.1875, ((0, 2), (1, 16)))
    router = bell_draw(keys[7], (N_PIPE, D, EXPERTS), D ** -0.5, 0.09375, ((0, 2),))
    return dict(a_input=a_input, a_route=a_route, b_saved=b_saved, b_grad=b_grad, b_route=b_route, up_weight=up_weight, down_weight=down_weight, router=router)


EPS = 1e-06

def rounded(values):
    return lax.optimization_barrier(values.astype(jnp.bfloat16)).astype(jnp.float32)

def positions(route_ids):
    blocks = route_ids.reshape(N_EXPERT, TOK * TOP).astype(jnp.int32)
    onehot = (blocks[:, :, None] == jnp.arange(EXPERTS, dtype=jnp.int32)).astype(jnp.int32)
    slot_pos = lax.optimization_barrier(jnp.sum(onehot * (jnp.cumsum(onehot, axis=1) - 1), axis=2)).astype(jnp.int32)
    source = jnp.arange(N_EXPERT, dtype=jnp.int32)[:, None]
    return (blocks * (N_EXPERT * CAP) + source * CAP + slot_pos).reshape(-1).astype(jnp.int32)

def plan(features, route_ids, router_cols):
    feat_float = features.astype(jnp.float32)
    inv_scale = lax.rsqrt(lax.optimization_barrier(jnp.mean(feat_float * feat_float, axis=-1, keepdims=True)) + EPS)
    normed = (feat_float * inv_scale).astype(jnp.bfloat16)
    scores = jnp.dot(normed, router_cols, preferred_element_type=jnp.float32)
    gate_value = jax.nn.sigmoid(jnp.take_along_axis(scores, route_ids, axis=1))
    return (feat_float, inv_scale, normed, gate_value, positions(route_ids))

def spread(row_block, flat_index):
    buffer = jnp.zeros((EXPERTS * N_EXPERT * CAP, D), row_block.dtype).at[flat_index].set(row_block)
    return buffer.reshape(EXPERTS, N_EXPERT * CAP, D)

def section_weights(up_section, down_section):
    return (up_section.reshape(D, EXPERTS, FF).transpose(1, 0, 2), down_section.reshape(EXPERTS, FF, D))

def expert_forward(row_block, up_expert, down_expert):
    hidden = jnp.dot(row_block, up_expert, preferred_element_type=jnp.float32)
    sigma_vals = jax.nn.sigmoid(hidden)
    activated = (hidden * sigma_vals).astype(jnp.bfloat16)
    partial_value = jnp.einsum('rgh,ghd->grd', activated.reshape(-1, GROUP, HID).astype(jnp.float32), down_expert.reshape(GROUP, HID, D).astype(jnp.float32))
    return (hidden, sigma_vals, activated, partial_value.astype(jnp.bfloat16))

def forward_section(features, route_ids, up_section, down_section, router_cols):
    feat_float, inv_scale, normed, gate_value, flat_index = plan(features, route_ids, router_cols)
    buffers = spread(jnp.repeat(normed, TOP, axis=0), flat_index)
    ups, downs = section_weights(up_section, down_section)

    def one_expert(operands):
        partial_value = expert_forward(operands[0], operands[1], operands[2])[3]
        return lax.optimization_barrier(jnp.sum(partial_value.astype(jnp.float32), axis=0))
    expert_out = rounded(lax.map(one_expert, (buffers, ups, downs))).reshape(-1, D)
    token_out = expert_out[flat_index].reshape(TOKENS, TOP, D)
    return (feat_float + lax.optimization_barrier(jnp.sum(gate_value[:, :, None] * token_out, axis=1))).astype(jnp.bfloat16)

def backward_section(features, cotangent, route_ids, up_section, down_section, router_cols):
    feat_float, inv_scale, normed, gate_value, flat_index = plan(features, route_ids, router_cols)
    buffers = spread(jnp.repeat(normed, TOP, axis=0), flat_index)
    cot_rows = (gate_value[:, :, None] * cotangent.astype(jnp.float32)[:, None, :]).astype(jnp.bfloat16).reshape(-1, D)
    cot_buffers = spread(cot_rows, flat_index)
    ups, downs = section_weights(up_section, down_section)

    def one_expert(operands):
        row_block, cot_block, up_expert, down_expert = operands
        hidden, sigma_vals, activated, partial_value = expert_forward(row_block, up_expert, down_expert)
        gate_term = rounded(lax.optimization_barrier(jnp.sum(rounded(lax.optimization_barrier(jnp.sum(cot_block.astype(jnp.float32)[None] * partial_value.astype(jnp.float32), axis=2))), axis=0)))
        act_grad = jnp.dot(cot_block, down_expert.T, preferred_element_type=jnp.float32)
        hid_grad = (act_grad * sigma_vals * (1.0 + hidden * (1.0 - sigma_vals))).astype(jnp.bfloat16)
        grad_down = jnp.dot(activated.T, cot_block, preferred_element_type=jnp.float32).astype(jnp.bfloat16)
        grad_up = jnp.dot(row_block.T, hid_grad, preferred_element_type=jnp.float32).astype(jnp.bfloat16)
        up_groups = up_expert.reshape(D, GROUP, HID).transpose(1, 2, 0).astype(jnp.float32)
        input_part = jnp.einsum('rgh,ghd->grd', hid_grad.reshape(-1, GROUP, HID).astype(jnp.float32), up_groups)
        input_sum = rounded(lax.optimization_barrier(jnp.sum(rounded(input_part), axis=0)))
        return (grad_up, grad_down, input_sum, gate_term)
    grad_ups, grad_downs, input_sums, gate_terms = lax.map(one_expert, (buffers, cot_buffers, ups, downs))
    input_tok = lax.optimization_barrier(jnp.sum(input_sums.reshape(-1, D)[flat_index].reshape(TOKENS, TOP, D), axis=1))
    score_grad = gate_terms.reshape(-1)[flat_index].reshape(TOKENS, TOP) * (1.0 - gate_value)
    onehot = (route_ids[:, :, None] == jnp.arange(EXPERTS, dtype=jnp.int32)).astype(jnp.float32)
    full_grad = lax.optimization_barrier(jnp.sum(onehot * score_grad[:, :, None], axis=1))
    normed_grad = input_tok + jnp.dot(full_grad, router_cols.astype(jnp.float32).T, precision=lax.Precision.HIGHEST)
    cubed = inv_scale * inv_scale * inv_scale
    feature_grad = inv_scale * normed_grad - feat_float * cubed * lax.optimization_barrier(jnp.sum(normed_grad * feat_float, axis=-1, keepdims=True)) / D
    input_grad = (cotangent.astype(jnp.float32) + feature_grad).astype(jnp.bfloat16)
    up_full = grad_ups.transpose(1, 0, 2).reshape(D, EXPERTS * FF)
    down_full = grad_downs.reshape(EXPERTS * FF, D)
    return (input_grad, up_full, down_full)

def reference(a_input, a_route, b_saved, b_grad, b_route, up_weight, down_weight, router):
    a_outs = []
    b_outs = []
    up_grads = []
    down_grads = []
    for section_index in range(N_PIPE):
        a_outs.append(forward_section(a_input[section_index], a_route[section_index], up_weight[section_index], down_weight[section_index], router[section_index]))
        source = N_PIPE - 1 - section_index
        input_grad, up_full, down_full = backward_section(b_saved[source], b_grad[source], b_route[source], up_weight[section_index], down_weight[section_index], router[section_index])
        b_outs.append(input_grad)
        up_grads.append(up_full)
        down_grads.append(down_full)
    a_next = jnp.stack([a_outs[(j - 1) % N_PIPE] for j in range(N_PIPE)])
    b_next = jnp.stack([b_outs[(N_PIPE - j) % N_PIPE] for j in range(N_PIPE)])
    return (a_next, b_next, jnp.stack(up_grads), jnp.stack(down_grads))
```

```python
import jax
import jax.numpy as jnp
from jax import lax
from jax.sharding import PartitionSpec as P

EPS = 1e-06
F32 = jnp.float32
BF16 = jnp.bfloat16


def dot(a, b, dims=((1,), (0,))):
    return lax.dot_general(a, b, (dims, ((), ())), preferred_element_type=F32)


def pipe_move(array, target):
    count = lax.axis_size("pipe")
    pairs = [(i, target(i, count) % count) for i in range(count)]
    if all(a == b for a, b in pairs):
        return array
    return lax.ppermute(array, "pipe", pairs)


def plane_move(array, experts, bit):
    devices = lax.axis_size("expert")
    return lax.ppermute(array, "expert", [(i, i ^ bit) for i in range(devices)])


def depth_move(array, experts, k):
    devices = lax.axis_size("expert")
    group = devices // experts
    pairs = [(i, ((i // group) ^ k) * group + i % group) for i in range(devices)]
    return lax.ppermute(array, "expert", pairs)


class Layout:
    def __init__(self, experts, capacity):
        self.experts = experts
        self.main = capacity // 8 * 8
        self.rest = capacity - self.main
        self.tail = -(-experts * self.rest // 8) * 8
        self.rows = self.main + self.tail
        self.packed = experts * self.main + self.tail


def selectors(ids, layout, here):
    tokens = ids.shape[0]
    onehot = (ids[:, None] == jnp.arange(layout.experts, dtype=jnp.int32)).astype(jnp.int32)
    slot = jnp.sum(onehot * (jnp.cumsum(onehot, axis=0) - 1), axis=1)
    row = jnp.arange(layout.rows, dtype=jnp.int32)[:, None]
    picks = []
    for k in range(layout.experts):
        place = jnp.where(slot < layout.main, slot, slot + k * layout.rest)
        picks.append(((ids[None, :] == (here ^ k)) & (place[None, :] == row)).astype(BF16))
    return picks


def statistics(features):
    feat = features.astype(F32)
    scale = lax.rsqrt(jnp.mean(feat * feat, axis=-1, keepdims=True) + EPS)
    return feat, scale, (feat * scale).astype(BF16)


def gate_of(normed, ids, router):
    scores = dot(normed, router)
    onehot = ids[:, None] == jnp.arange(router.shape[1], dtype=jnp.int32)
    return jax.nn.sigmoid(jnp.sum(jnp.where(onehot, scores, 0.0), axis=1, keepdims=True))


def to_planes(rows, picks, layout):
    blocks = []
    for k, pick in enumerate(picks):
        block = dot(pick, rows).astype(BF16)
        blocks.append(depth_move(block, layout.experts, k) if k else block)
    return blocks


def pack(blocks, layout, cols):
    tail = blocks[0][layout.main :, cols]
    for block in blocks[1:]:
        tail = tail + block[layout.main :, cols]
    return jnp.concatenate([b[: layout.main, cols] for b in blocks] + [tail], axis=0)


def spread(blocks, layout, halves):
    e = layout.experts
    lo, hi = [pack(blocks, layout, cols) for cols in halves]
    x_lo, y_hi = plane_move(lo, e, 1), plane_move(hi, e, 2)
    x_hi, y_lo = plane_move(hi, e, 1), plane_move(lo, e, 2)
    d_lo, d_hi = plane_move(x_lo, e, 2), plane_move(y_hi, e, 1)
    return [(lo, hi), (x_lo, x_hi), (y_lo, y_hi), (d_lo, d_hi)]


def gather_back(part, layout):
    e = layout.experts
    s_lo = plane_move(part(3, 0).astype(BF16), e, 1)
    s_hi = plane_move(part(3, 1).astype(BF16), e, 2)
    x_lo = plane_move(part(1, 0).astype(BF16), e, 1)
    y_hi = plane_move(part(2, 1).astype(BF16), e, 2)
    x_hi = plane_move((part(1, 1) + s_hi.astype(F32)).astype(BF16), e, 1)
    y_lo = plane_move((part(2, 0) + s_lo.astype(F32)).astype(BF16), e, 2)
    lo = (part(0, 0) + x_lo.astype(F32) + y_lo.astype(F32)).astype(BF16)
    hi = (part(0, 1) + x_hi.astype(F32) + y_hi.astype(F32)).astype(BF16)
    return lo, hi


def to_tokens(total, picks, layout):
    lo, hi = total
    token_rows = 0.0
    for k, pick in enumerate(picks):
        rows = slice(k * layout.main, (k + 1) * layout.main)
        tail = slice(layout.experts * layout.main, layout.packed)
        block = jnp.concatenate(
            [
                jnp.concatenate([lo[rows], hi[rows]], axis=1),
                jnp.concatenate([lo[tail], hi[tail]], axis=1),
            ],
            axis=0,
        )
        if k:
            block = depth_move(block, layout.experts, k)
        token_rows = token_rows + dot(pick, block, ((0,), (0,)))
    return token_rows


def body(a_input, a_route, b_saved, b_grad, b_route, up_weight, down_weight, router):
    devices = lax.axis_size("expert")
    experts = router.shape[2]
    group = devices // experts
    tokens, width = a_input.shape[1], a_input.shape[2]
    layout = Layout(experts, tokens * a_route.shape[2] // experts + 2)
    here = lax.axis_index("expert") // group
    up, down, cols_r = up_weight[0], down_weight[0], router[0]
    half = width // 2
    halves = (slice(0, half), slice(half, width))

    b_ids = pipe_move(b_route[0].astype(BF16), lambda i, n: n - 1 - i).astype(jnp.int32)[:, 0]
    b_x = pipe_move(b_saved[0], lambda i, n: n - 1 - i)
    b_c = pipe_move(b_grad[0], lambda i, n: n - 1 - i)
    a_ids = a_route[0][:, 0]

    a_float, _, a_normed = statistics(a_input[0])
    a_picks = selectors(a_ids, layout, here)
    a_rows = spread(to_planes(a_normed, a_picks, layout), layout, halves)
    a_gate = gate_of(a_normed, a_ids, cols_r)

    b_float, b_scale, b_normed = statistics(b_x)
    b_picks = selectors(b_ids, layout, here)
    b_rows = spread(to_planes(b_normed, b_picks, layout), layout, halves)
    b_gate = gate_of(b_normed, b_ids, cols_r)
    cot = (b_gate * b_c.astype(F32)).astype(BF16)
    c_rows = spread(to_planes(cot, b_picks, layout), layout, halves)

    own_col = jnp.sum(
        jnp.where(jnp.arange(experts) == here, cols_r.astype(F32), 0.0), axis=1, keepdims=True
    ).astype(BF16)

    a_act = []
    for lo, hi in a_rows:
        hidden = dot(lo, up[:half]) + dot(hi, up[half:])
        a_act.append((hidden * jax.nn.sigmoid(hidden)).astype(BF16))
    a_total = gather_back(lambda j, h: dot(a_act[j], down[:, halves[h]]), layout)
    a_out = (a_float + a_gate * to_tokens(a_total, a_picks, layout)).astype(BF16)
    a_next = pipe_move(a_out, lambda i, n: i + 1)

    act, hid_grad, score_grad = [], [], []
    for (lo, hi), (c_lo, c_hi) in zip(b_rows, c_rows):
        hidden = dot(lo, up[:half]) + dot(hi, up[half:])
        score = dot(lo, own_col[:half]) + dot(hi, own_col[half:])
        sigma = jax.nn.sigmoid(hidden)
        active = hidden * sigma
        act_grad = dot(c_lo, down[:, :half], ((1,), (1,))) + dot(c_hi, down[:, half:], ((1,), (1,)))
        act.append(active.astype(BF16))
        hid_grad.append((act_grad * sigma * (1.0 + hidden * (1.0 - sigma))).astype(BF16))
        term = jnp.sum(active * act_grad, axis=1, keepdims=True)
        score_grad.append(term * jax.nn.sigmoid(-score))
    col_row = own_col.astype(F32).reshape(1, width)

    def input_part(j, h):
        return dot(hid_grad[j], up[halves[h]], ((1,), (1,))) + score_grad[j] * col_row[:, halves[h]]

    b_total = gather_back(input_part, layout)
    normed_grad = to_tokens(b_total, b_picks, layout)
    along = jnp.sum(normed_grad * b_float, axis=-1, keepdims=True) / width
    feature_grad = b_scale * normed_grad - b_float * (b_scale * b_scale * b_scale) * along
    b_out = (b_c.astype(F32) + feature_grad).astype(BF16)
    b_next = pipe_move(b_out, lambda i, n: n - i)

    acts, hids = jnp.concatenate(act, axis=0), jnp.concatenate(hid_grad, axis=0)
    down_parts, up_parts = [], []
    for h in range(2):
        b_all = jnp.concatenate([r[h] for r in b_rows], axis=0)
        c_all = jnp.concatenate([r[h] for r in c_rows], axis=0)
        up_parts.append(dot(b_all, hids, ((0,), (0,))).astype(BF16))
        down_parts.append(dot(acts, c_all, ((0,), (0,))).astype(BF16))
    up_grad = jnp.concatenate(up_parts, axis=0)
    down_grad = jnp.concatenate(down_parts, axis=1)
    return (a_next[None], b_next[None], up_grad[None], down_grad[None])


def solution(mesh):
    return jax.shard_map(
        body,
        mesh=mesh,
        in_specs=(
            P("pipe", "expert", None),
            P("pipe", "expert", None),
            P("pipe", "expert", None),
            P("pipe", "expert", None),
            P("pipe", "expert", None),
            P("pipe", None, "expert"),
            P("pipe", "expert", None),
            P("pipe", None, None),
        ),
        out_specs=(
            P("pipe", "expert", None),
            P("pipe", "expert", None),
            P("pipe", None, "expert"),
            P("pipe", "expert", None),
        ),
        check_vma=False,
    )
```

```python
import jax
import jax.numpy as jnp
from jax import lax
from jax.sharding import PartitionSpec as P

EPS = 1e-06
F32 = jnp.float32
BF16 = jnp.bfloat16


def dot(a, b, dims=((1,), (0,))):
    return lax.dot_general(a, b, (dims, ((), ())), preferred_element_type=F32)


def pipe_move(array, target):
    count = lax.axis_size("pipe")
    pairs = [(i, target(i, count) % count) for i in range(count)]
    if all(a == b for a, b in pairs):
        return array
    return lax.ppermute(array, "pipe", pairs)


def plane_move(array, experts, bit):
    devices = lax.axis_size("expert")
    return lax.ppermute(array, "expert", [(i, i ^ bit) for i in range(devices)])


def depth_move(array, experts, k):
    devices = lax.axis_size("expert")
    group = devices // experts
    pairs = [(i, ((i // group) ^ k) * group + i % group) for i in range(devices)]
    return lax.ppermute(array, "expert", pairs)


class Layout:
    def __init__(self, experts, capacity):
        self.experts = experts
        self.main = capacity // 8 * 8
        self.rest = capacity - self.main
        self.tail = -(-experts * self.rest // 8) * 8
        self.rows = self.main + self.tail
        self.packed = experts * self.main + self.tail


def selectors(ids, layout, here):
    tokens = ids.shape[0]
    onehot = (ids[:, None] == jnp.arange(layout.experts, dtype=jnp.int32)).astype(jnp.int32)
    slot = jnp.sum(onehot * (jnp.cumsum(onehot, axis=0) - 1), axis=1)
    row = jnp.arange(layout.rows, dtype=jnp.int32)[:, None]
    picks = []
    for k in range(layout.experts):
        place = jnp.where(slot < layout.main, slot, slot + k * layout.rest)
        picks.append(((ids[None, :] == (here ^ k)) & (place[None, :] == row)).astype(BF16))
    return picks


def statistics(features):
    feat = features.astype(F32)
    scale = lax.rsqrt(jnp.mean(feat * feat, axis=-1, keepdims=True) + EPS)
    return feat, scale, (feat * scale).astype(BF16)


def gate_of(normed, ids, router):
    scores = dot(normed, router)
    onehot = ids[:, None] == jnp.arange(router.shape[1], dtype=jnp.int32)
    return jax.nn.sigmoid(jnp.sum(jnp.where(onehot, scores, 0.0), axis=1, keepdims=True))


def to_planes(rows, picks, layout):
    blocks = []
    for k, pick in enumerate(picks):
        block = dot(pick, rows).astype(BF16)
        blocks.append(depth_move(block, layout.experts, k) if k else block)
    return blocks


def pack(blocks, layout, cols):
    tail = blocks[0][layout.main :, cols]
    for block in blocks[1:]:
        tail = tail + block[layout.main :, cols]
    return jnp.concatenate([b[: layout.main, cols] for b in blocks] + [tail], axis=0)


def planes_of(experts):
    devices = lax.axis_size("expert")
    group = devices // experts
    return [[e * group + m for m in range(group)] for e in range(experts)]


def spread(blocks, layout):
    mine = pack(blocks, layout, slice(None))
    groups = planes_of(layout.experts)
    return lax.all_gather(mine, "expert", axis=0, tiled=True, axis_index_groups=groups)


def gather_back(part, layout):
    e = layout.experts
    s_lo = plane_move(part(3, 0).astype(BF16), e, 1)
    s_hi = plane_move(part(3, 1).astype(BF16), e, 2)
    x_lo = plane_move(part(1, 0).astype(BF16), e, 1)
    y_hi = plane_move(part(2, 1).astype(BF16), e, 2)
    x_hi = plane_move((part(1, 1) + s_hi.astype(F32)).astype(BF16), e, 1)
    y_lo = plane_move((part(2, 0) + s_lo.astype(F32)).astype(BF16), e, 2)
    lo = (part(0, 0) + x_lo.astype(F32) + y_lo.astype(F32)).astype(BF16)
    hi = (part(0, 1) + x_hi.astype(F32) + y_hi.astype(F32)).astype(BF16)
    return lo, hi


def rows_of(values, layout, j):
    group = values.shape[0] // layout.packed
    member = (lax.axis_index("expert") % group) ^ j
    return lax.dynamic_slice_in_dim(values, member * layout.packed, layout.packed, axis=0)


def to_tokens(total, picks, layout):
    lo, hi = total
    token_rows = 0.0
    for k, pick in enumerate(picks):
        rows = slice(k * layout.main, (k + 1) * layout.main)
        tail = slice(layout.experts * layout.main, layout.packed)
        block = jnp.concatenate(
            [
                jnp.concatenate([lo[rows], hi[rows]], axis=1),
                jnp.concatenate([lo[tail], hi[tail]], axis=1),
            ],
            axis=0,
        )
        if k:
            block = depth_move(block, layout.experts, k)
        token_rows = token_rows + dot(pick, block, ((0,), (0,)))
    return token_rows


def body(a_input, a_route, b_saved, b_grad, b_route, up_weight, down_weight, router):
    devices = lax.axis_size("expert")
    experts = router.shape[2]
    group = devices // experts
    tokens, width = a_input.shape[1], a_input.shape[2]
    layout = Layout(experts, tokens * a_route.shape[2] // experts + 2)
    here = lax.axis_index("expert") // group
    up, down, cols_r = up_weight[0], down_weight[0], router[0]

    b_ids = pipe_move(b_route[0].astype(BF16), lambda i, n: n - 1 - i).astype(jnp.int32)[:, 0]
    b_x = pipe_move(b_saved[0], lambda i, n: n - 1 - i)
    b_c = pipe_move(b_grad[0], lambda i, n: n - 1 - i)
    a_ids = a_route[0][:, 0]

    a_float, _, a_normed = statistics(a_input[0])
    a_picks = selectors(a_ids, layout, here)
    a_rows = spread(to_planes(a_normed, a_picks, layout), layout)
    a_gate = gate_of(a_normed, a_ids, cols_r)

    b_float, b_scale, b_normed = statistics(b_x)
    b_picks = selectors(b_ids, layout, here)
    b_rows = spread(to_planes(b_normed, b_picks, layout), layout)
    b_gate = gate_of(b_normed, b_ids, cols_r)
    cot = (b_gate * b_c.astype(F32)).astype(BF16)
    c_rows = spread(to_planes(cot, b_picks, layout), layout)

    own_col = jnp.sum(
        jnp.where(jnp.arange(experts) == here, cols_r.astype(F32), 0.0), axis=1, keepdims=True
    ).astype(BF16)

    hidden = dot(a_rows, up)
    a_act = (hidden * jax.nn.sigmoid(hidden)).astype(BF16)
    half = width // 2
    halves = (slice(0, half), slice(half, width))
    a_parts = [rows_of(a_act, layout, j) for j in range(group)]
    a_total = gather_back(lambda j, h: dot(a_parts[j], down[:, halves[h]]), layout)
    a_out = (a_float + a_gate * to_tokens(a_total, a_picks, layout)).astype(BF16)
    a_next = pipe_move(a_out, lambda i, n: i + 1)

    hidden = dot(b_rows, up)
    score = dot(b_rows, own_col)
    sigma = jax.nn.sigmoid(hidden)
    active = hidden * sigma
    act_grad = dot(c_rows, down, ((1,), (1,)))
    act = active.astype(BF16)
    hid_grad = (act_grad * sigma * (1.0 + hidden * (1.0 - sigma))).astype(BF16)
    term = jnp.sum(active * act_grad, axis=1, keepdims=True)
    score_grad = term * jax.nn.sigmoid(-score)
    col_row = own_col.astype(F32).reshape(1, width)
    b_parts = [rows_of(hid_grad, layout, j) for j in range(group)]
    b_scores = [rows_of(score_grad, layout, j) for j in range(group)]

    def input_part(j, h):
        cols = halves[h]
        return dot(b_parts[j], up[cols], ((1,), (1,))) + b_scores[j] * col_row[:, cols]

    b_total = gather_back(input_part, layout)
    normed_grad = to_tokens(b_total, b_picks, layout)
    along = jnp.sum(normed_grad * b_float, axis=-1, keepdims=True) / width
    feature_grad = b_scale * normed_grad - b_float * (b_scale * b_scale * b_scale) * along
    b_out = (b_c.astype(F32) + feature_grad).astype(BF16)
    b_next = pipe_move(b_out, lambda i, n: n - i)

    up_grad = dot(b_rows, hid_grad, ((0,), (0,))).astype(BF16)
    down_grad = dot(act, c_rows, ((0,), (0,))).astype(BF16)
    return (a_next[None], b_next[None], up_grad[None], down_grad[None])


def solution(mesh):
    return jax.shard_map(
        body,
        mesh=mesh,
        in_specs=(
            P("pipe", "expert", None),
            P("pipe", "expert", None),
            P("pipe", "expert", None),
            P("pipe", "expert", None),
            P("pipe", "expert", None),
            P("pipe", None, "expert"),
            P("pipe", "expert", None),
            P("pipe", None, None),
        ),
        out_specs=(
            P("pipe", "expert", None),
            P("pipe", "expert", None),
            P("pipe", None, "expert"),
            P("pipe", "expert", None),
        ),
        check_vma=False,
    )
```

```python
import jax
import jax.numpy as jnp
from jax import lax
from jax.sharding import PartitionSpec as P

EPS = 1e-06
F32 = jnp.float32
BF16 = jnp.bfloat16


def dot(a, b, dims=((1,), (0,))):
    return lax.dot_general(a, b, (dims, ((), ())), preferred_element_type=F32)


def pipe_move(array, target):
    count = lax.axis_size("pipe")
    pairs = [(i, target(i, count) % count) for i in range(count)]
    if all(a == b for a, b in pairs):
        return array
    return lax.ppermute(array, "pipe", pairs)


def plane_move(array, experts, bit):
    devices = lax.axis_size("expert")
    return lax.ppermute(array, "expert", [(i, i ^ bit) for i in range(devices)])


def depth_exchange(blocks, experts):
    devices = lax.axis_size("expert")
    group = devices // experts
    columns = [[e * group + m for e in range(experts)] for m in range(group)]
    return lax.all_to_all(
        blocks, "expert", split_axis=0, concat_axis=0, tiled=True, axis_index_groups=columns
    )


class Layout:
    def __init__(self, experts, capacity):
        self.experts = experts
        self.main = capacity // 8 * 8
        self.rest = capacity - self.main
        self.tail = -(-experts * self.rest // 8) * 8
        self.rows = self.main + self.tail
        self.packed = experts * self.main + self.tail


def selector(ids, layout, here):
    onehot = (ids[:, None] == jnp.arange(layout.experts, dtype=jnp.int32)).astype(jnp.int32)
    slot = jnp.sum(onehot * (jnp.cumsum(onehot, axis=0) - 1), axis=1)
    place = jnp.where(slot < layout.main, slot, slot + here * layout.rest)
    row = jnp.arange(layout.experts * layout.rows, dtype=jnp.int32)[:, None]
    return ((ids * layout.rows + place)[None, :] == row).astype(BF16)


def packer(layout):
    packed = jnp.arange(layout.packed, dtype=jnp.int32)[:, None]
    row = jnp.arange(layout.experts * layout.rows, dtype=jnp.int32)[None, :]
    block, place = row // layout.rows, row % layout.rows
    target = jnp.where(
        place < layout.main,
        block * layout.main + place,
        layout.experts * layout.main + place - layout.main,
    )
    return (target == packed).astype(BF16)


def statistics(features):
    feat = features.astype(F32)
    scale = lax.rsqrt(jnp.mean(feat * feat, axis=-1, keepdims=True) + EPS)
    return feat, scale, (feat * scale).astype(BF16)


def gate_of(normed, ids, router):
    scores = dot(normed, router)
    onehot = ids[:, None] == jnp.arange(router.shape[1], dtype=jnp.int32)
    return jax.nn.sigmoid(jnp.sum(jnp.where(onehot, scores, 0.0), axis=1, keepdims=True))


def to_planes(rows, pick, layout):
    blocks = dot(pick, rows).astype(BF16).reshape(layout.experts, layout.rows, rows.shape[1])
    blocks = depth_exchange(blocks, layout.experts)
    blocks = blocks.reshape(layout.experts * layout.rows, rows.shape[1])
    return dot(packer(layout), blocks).astype(BF16)


def to_neighbours(mine, experts):
    return plane_move(mine, experts, 1), plane_move(mine, experts, 2)


def to_diagonal(from_x, from_y, experts, halves):
    return (
        plane_move(from_x[:, halves[0]], experts, 2),
        plane_move(from_y[:, halves[1]], experts, 1),
    )


def gather_back(part, layout):
    e = layout.experts
    s_lo = plane_move(part(3, 0).astype(BF16), e, 1)
    s_hi = plane_move(part(3, 1).astype(BF16), e, 2)
    x_lo = plane_move(part(1, 0).astype(BF16), e, 1)
    y_hi = plane_move(part(2, 1).astype(BF16), e, 2)
    x_hi = plane_move((part(1, 1) + s_hi.astype(F32)).astype(BF16), e, 1)
    y_lo = plane_move((part(2, 0) + s_lo.astype(F32)).astype(BF16), e, 2)
    lo = (part(0, 0) + x_lo.astype(F32) + y_lo.astype(F32)).astype(BF16)
    hi = (part(0, 1) + x_hi.astype(F32) + y_hi.astype(F32)).astype(BF16)
    return lo, hi


def to_tokens(total, pick, layout):
    blocks = [dot(packer(layout), t, ((0,), (0,))).astype(BF16) for t in total]
    blocks = jnp.concatenate(blocks, axis=1)
    blocks = blocks.reshape(layout.experts, layout.rows, blocks.shape[1])
    blocks = depth_exchange(blocks, layout.experts)
    blocks = blocks.reshape(layout.experts * layout.rows, blocks.shape[2])
    return dot(pick, blocks, ((0,), (0,)))


def body(a_input, a_route, b_saved, b_grad, b_route, up_weight, down_weight, router):
    devices = lax.axis_size("expert")
    experts = router.shape[2]
    group = devices // experts
    tokens, width = a_input.shape[1], a_input.shape[2]
    layout = Layout(experts, tokens * a_route.shape[2] // experts + 2)
    here = lax.axis_index("expert") // group
    up, down, cols_r = up_weight[0], down_weight[0], router[0]
    half = width // 2
    halves = (slice(0, half), slice(half, width))

    b_ids = pipe_move(b_route[0].astype(BF16), lambda i, n: n - 1 - i).astype(jnp.int32)[:, 0]
    b_x = pipe_move(b_saved[0], lambda i, n: n - 1 - i)
    b_c = pipe_move(b_grad[0], lambda i, n: n - 1 - i)
    a_ids = a_route[0][:, 0]

    a_float, _, a_normed = statistics(a_input[0])
    a_pick = selector(a_ids, layout, here)
    a_mine = to_planes(a_normed, a_pick, layout)
    a_gate = gate_of(a_normed, a_ids, cols_r)

    b_float, b_scale, b_normed = statistics(b_x)
    b_pick = selector(b_ids, layout, here)
    b_mine = to_planes(b_normed, b_pick, layout)
    b_gate = gate_of(b_normed, b_ids, cols_r)
    cot = (b_gate * b_c.astype(F32)).astype(BF16)
    c_mine = to_planes(cot, b_pick, layout)

    a_x, a_y = to_neighbours(a_mine, experts)
    b_mine, a_x, a_y = lax.optimization_barrier((b_mine, a_x, a_y))
    a_d = to_diagonal(a_x, a_y, experts, halves)
    b_nx, b_ny = to_neighbours(b_mine, experts)
    c_mine, b_nx, b_ny, a_d = lax.optimization_barrier((c_mine, b_nx, b_ny, a_d))
    b_d = to_diagonal(b_nx, b_ny, experts, halves)
    c_nx, c_ny = to_neighbours(c_mine, experts)
    a_rows = [(v[:, halves[0]], v[:, halves[1]]) for v in (a_mine, a_x, a_y)] + [a_d]

    own_col = jnp.sum(
        jnp.where(jnp.arange(experts) == here, cols_r.astype(F32), 0.0), axis=1, keepdims=True
    ).astype(BF16)

    a_act = []
    for lo, hi in a_rows:
        hidden = dot(lo, up[:half]) + dot(hi, up[half:])
        a_act.append((hidden * jax.nn.sigmoid(hidden)).astype(BF16))
    a_act, c_nx, c_ny, b_d = lax.optimization_barrier((a_act, c_nx, c_ny, b_d))
    c_d = to_diagonal(c_nx, c_ny, experts, halves)
    a_total = gather_back(lambda j, h: dot(a_act[j], down[:, halves[h]]), layout)
    a_out = (a_float + a_gate * to_tokens(a_total, a_pick, layout)).astype(BF16)
    a_next = pipe_move(a_out, lambda i, n: i + 1)

    b_rows = [(v[:, halves[0]], v[:, halves[1]]) for v in (b_mine, b_nx, b_ny)] + [b_d]
    c_rows = [(v[:, halves[0]], v[:, halves[1]]) for v in (c_mine, c_nx, c_ny)] + [c_d]
    act, hid_grad, score_grad = [], [], []
    for (lo, hi), (c_lo, c_hi) in zip(b_rows, c_rows):
        hidden = dot(lo, up[:half]) + dot(hi, up[half:])
        score = dot(lo, own_col[:half]) + dot(hi, own_col[half:])
        sigma = jax.nn.sigmoid(hidden)
        active = hidden * sigma
        act_grad = dot(c_lo, down[:, :half], ((1,), (1,))) + dot(c_hi, down[:, half:], ((1,), (1,)))
        act.append(active.astype(BF16))
        hid_grad.append((act_grad * sigma * (1.0 + hidden * (1.0 - sigma))).astype(BF16))
        term = jnp.sum(active * act_grad, axis=1, keepdims=True)
        score_grad.append(term * jax.nn.sigmoid(-score))
    col_row = own_col.astype(F32).reshape(1, width)

    def input_part(j, h):
        return dot(hid_grad[j], up[halves[h]], ((1,), (1,))) + score_grad[j] * col_row[:, halves[h]]

    b_total = gather_back(input_part, layout)
    normed_grad = to_tokens(b_total, b_pick, layout)
    along = jnp.sum(normed_grad * b_float, axis=-1, keepdims=True) / width
    feature_grad = b_scale * normed_grad - b_float * (b_scale * b_scale * b_scale) * along
    b_out = (b_c.astype(F32) + feature_grad).astype(BF16)
    b_next = pipe_move(b_out, lambda i, n: n - i)

    acts, hids = jnp.concatenate(act, axis=0), jnp.concatenate(hid_grad, axis=0)
    down_parts, up_parts = [], []
    for h in range(2):
        b_all = jnp.concatenate([r[h] for r in b_rows], axis=0)
        c_all = jnp.concatenate([r[h] for r in c_rows], axis=0)
        up_parts.append(dot(b_all, hids, ((0,), (0,))).astype(BF16))
        down_parts.append(dot(acts, c_all, ((0,), (0,))).astype(BF16))
    up_grad = jnp.concatenate(up_parts, axis=0)
    down_grad = jnp.concatenate(down_parts, axis=1)
    return (a_next[None], b_next[None], up_grad[None], down_grad[None])


def solution(mesh):
    return jax.shard_map(
        body,
        mesh=mesh,
        in_specs=(
            P("pipe", "expert", None),
            P("pipe", "expert", None),
            P("pipe", "expert", None),
            P("pipe", "expert", None),
            P("pipe", "expert", None),
            P("pipe", None, "expert"),
            P("pipe", "expert", None),
            P("pipe", None, None),
        ),
        out_specs=(
            P("pipe", "expert", None),
            P("pipe", "expert", None),
            P("pipe", None, "expert"),
            P("pipe", "expert", None),
        ),
        check_vma=False,
    )
```

```python
import jax
import jax.numpy as jnp
from jax import lax
from jax.sharding import PartitionSpec as P

EPS = 1e-06
F32 = jnp.float32
BF16 = jnp.bfloat16


def dot(a, b, dims=((1,), (0,))):
    return lax.dot_general(a, b, (dims, ((), ())), preferred_element_type=F32)


def pipe_move(array, target):
    count = lax.axis_size("pipe")
    pairs = [(i, target(i, count) % count) for i in range(count)]
    if all(a == b for a, b in pairs):
        return array
    return lax.ppermute(array, "pipe", pairs)


def plane_move(array, experts, bit):
    devices = lax.axis_size("expert")
    return lax.ppermute(array, "expert", [(i, i ^ bit) for i in range(devices)])


def depth_exchange(blocks, experts):
    devices = lax.axis_size("expert")
    group = devices // experts
    columns = [[e * group + m for e in range(experts)] for m in range(group)]
    return lax.all_to_all(
        blocks, "expert", split_axis=0, concat_axis=0, tiled=True, axis_index_groups=columns
    )


class Layout:
    def __init__(self, experts, capacity):
        self.experts = experts
        self.main = capacity // 8 * 8
        self.rest = capacity - self.main
        self.tail = -(-experts * self.rest // 8) * 8
        self.rows = self.main + self.tail
        self.packed = experts * self.main + self.tail


def selector(ids, layout, here):
    onehot = (ids[:, None] == jnp.arange(layout.experts, dtype=jnp.int32)).astype(jnp.int32)
    slot = jnp.sum(onehot * (jnp.cumsum(onehot, axis=0) - 1), axis=1)
    place = jnp.where(slot < layout.main, slot, slot + here * layout.rest)
    row = jnp.arange(layout.experts * layout.rows, dtype=jnp.int32)[:, None]
    return ((ids * layout.rows + place)[None, :] == row).astype(BF16)


def packer(layout):
    packed = jnp.arange(layout.packed, dtype=jnp.int32)[:, None]
    row = jnp.arange(layout.experts * layout.rows, dtype=jnp.int32)[None, :]
    block, place = row // layout.rows, row % layout.rows
    target = jnp.where(
        place < layout.main,
        block * layout.main + place,
        layout.experts * layout.main + place - layout.main,
    )
    return (target == packed).astype(BF16)


def statistics(features):
    feat = features.astype(F32)
    scale = lax.rsqrt(jnp.mean(feat * feat, axis=-1, keepdims=True) + EPS)
    return feat, scale, (feat * scale).astype(BF16)


def gate_of(normed, ids, router):
    scores = dot(normed, router)
    onehot = ids[:, None] == jnp.arange(router.shape[1], dtype=jnp.int32)
    return jax.nn.sigmoid(jnp.sum(jnp.where(onehot, scores, 0.0), axis=1, keepdims=True))


def select_rows(pick, rows, layout):
    return dot(pick, rows).astype(BF16).reshape(layout.experts, layout.rows, rows.shape[1])


def across_planes(blocks, layout):
    blocks = depth_exchange(blocks, layout.experts)
    blocks = blocks.reshape(layout.experts * layout.rows, blocks.shape[2])
    return dot(packer(layout), blocks).astype(BF16)


def to_neighbours(mine, experts):
    return plane_move(mine, experts, 1), plane_move(mine, experts, 2)


def to_diagonal(from_x, from_y, experts):
    cut = -(-from_x.shape[0] // 16) * 8
    return (
        plane_move(from_x[:cut], experts, 2),
        plane_move(from_y[cut:], experts, 1),
    )


def first_parts(part):
    return (
        jnp.concatenate([part(3, 0).astype(BF16), part(1, 0).astype(BF16)], axis=0),
        jnp.concatenate([part(3, 1).astype(BF16), part(2, 1).astype(BF16)], axis=0),
    )


def second_parts(part, got, rows):
    return (
        (part(1, 1) + got[1][:rows].astype(F32)).astype(BF16),
        (part(2, 0) + got[0][:rows].astype(F32)).astype(BF16),
    )


def swap_pair(pair, experts):
    return plane_move(pair[0], experts, 1), plane_move(pair[1], experts, 2)


def totals(part, first, second, rows):
    lo = part(0, 0) + first[0][rows:].astype(F32) + second[1].astype(F32)
    hi = part(0, 1) + first[1][rows:].astype(F32) + second[0].astype(F32)
    return lo.astype(BF16), hi.astype(BF16)


def for_tokens(total, layout):
    blocks = [dot(packer(layout), t, ((0,), (0,))).astype(BF16) for t in total]
    blocks = jnp.concatenate(blocks, axis=1)
    return blocks.reshape(layout.experts, layout.rows, blocks.shape[1])


def at_tokens(blocks, pick, layout):
    blocks = depth_exchange(blocks, layout.experts)
    blocks = blocks.reshape(layout.experts * layout.rows, blocks.shape[2])
    return dot(pick, blocks, ((0,), (0,)))


def body(a_input, a_route, b_saved, b_grad, b_route, up_weight, down_weight, router):
    devices = lax.axis_size("expert")
    experts = router.shape[2]
    group = devices // experts
    tokens, width = a_input.shape[1], a_input.shape[2]
    layout = Layout(experts, tokens * a_route.shape[2] // experts + 2)
    here = lax.axis_index("expert") // group
    up, down, cols_r = up_weight[0], down_weight[0], router[0]
    half = width // 2
    halves = (slice(0, half), slice(half, width))

    b_ids = pipe_move(b_route[0].astype(BF16), lambda i, n: n - 1 - i).astype(jnp.int32)[:, 0]
    b_x = pipe_move(b_saved[0], lambda i, n: n - 1 - i)
    b_c = pipe_move(b_grad[0], lambda i, n: n - 1 - i)
    a_ids = a_route[0][:, 0]

    after = lax.optimization_barrier
    rows = layout.packed

    own_col = jnp.sum(
        jnp.where(jnp.arange(experts) == here, cols_r.astype(F32), 0.0), axis=1, keepdims=True
    ).astype(BF16)
    col_row = own_col.astype(F32).reshape(1, width)

    a_float, _, a_normed = statistics(a_input[0])
    a_pick = selector(a_ids, layout, here)
    a_mine = across_planes(select_rows(a_pick, a_normed, layout), layout)

    b_float, b_scale, b_normed = statistics(b_x)
    b_pick = selector(b_ids, layout, here)
    b_send = select_rows(b_pick, b_normed, layout)
    b_send, a_mine = after((b_send, a_mine))
    a_near = to_neighbours(a_mine, experts)
    b_mine = across_planes(b_send, layout)

    b_gate = gate_of(b_normed, b_ids, cols_r)
    cot = (b_gate * b_c.astype(F32)).astype(BF16)
    c_send = select_rows(b_pick, cot, layout)
    c_send, a_near, b_mine = after((c_send, a_near, b_mine))
    c_mine = across_planes(c_send, layout)
    a_far = to_diagonal(a_near[0], a_near[1], experts)
    b_near = to_neighbours(b_mine, experts)

    def forward_act(block):
        hidden = dot(block, up)
        return (hidden * jax.nn.sigmoid(hidden)).astype(BF16)

    a_act = [forward_act(v) for v in (a_mine,) + a_near]
    a_act.append(jnp.concatenate([forward_act(v) for v in a_far], axis=0))

    def a_part(j, h):
        return dot(a_act[j], down[:, halves[h]])

    a_first = first_parts(a_part)
    a_first, b_near = after((a_first, b_near))
    a_first = swap_pair(a_first, experts)
    b_far = to_diagonal(b_near[0], b_near[1], experts)
    a_first, c_mine = after((a_first, c_mine))
    c_near = to_neighbours(c_mine, experts)
    a_second = second_parts(a_part, a_first, rows)
    a_second, b_far, c_near = after((a_second, b_far, c_near))
    c_far = to_diagonal(c_near[0], c_near[1], experts)
    a_second = swap_pair(a_second, experts)
    a_back = for_tokens(totals(a_part, a_first, a_second, rows), layout)

    act, hid_grad, score_grad = [], [], []
    for block, cots in zip((b_mine,) + b_near + b_far, (c_mine,) + c_near + c_far):
        hidden = dot(block, up)
        score = dot(block, own_col)
        sigma = jax.nn.sigmoid(hidden)
        active = hidden * sigma
        act_grad = dot(cots, down, ((1,), (1,)))
        act.append(active.astype(BF16))
        hid_grad.append((act_grad * sigma * (1.0 + hidden * (1.0 - sigma))).astype(BF16))
        term = jnp.sum(active * act_grad, axis=1, keepdims=True)
        score_grad.append(term * jax.nn.sigmoid(-score))
    parts_g = hid_grad[:3] + [jnp.concatenate(hid_grad[3:], axis=0)]
    scores = score_grad[:3] + [jnp.concatenate(score_grad[3:], axis=0)]

    def b_part(j, h):
        cols = halves[h]
        return dot(parts_g[j], up[cols], ((1,), (1,))) + scores[j] * col_row[:, cols]

    b_first, a_back = after((first_parts(b_part), a_back))
    b_first = swap_pair(b_first, experts)
    a_gate = gate_of(a_normed, a_ids, cols_r)
    a_out = (a_float + a_gate * at_tokens(a_back, a_pick, layout)).astype(BF16)
    a_next = pipe_move(a_out, lambda i, n: i + 1)
    b_second = swap_pair(second_parts(b_part, b_first, rows), experts)
    b_back = for_tokens(totals(b_part, b_first, b_second, rows), layout)
    normed_grad = at_tokens(b_back, b_pick, layout)
    along = jnp.sum(normed_grad * b_float, axis=-1, keepdims=True) / width
    feature_grad = b_scale * normed_grad - b_float * (b_scale * b_scale * b_scale) * along
    b_out = (b_c.astype(F32) + feature_grad).astype(BF16)
    b_next = pipe_move(b_out, lambda i, n: n - i)

    acts, hids = jnp.concatenate(act, axis=0), jnp.concatenate(hid_grad, axis=0)
    b_all = jnp.concatenate((b_mine,) + b_near + b_far, axis=0)
    c_all = jnp.concatenate((c_mine,) + c_near + c_far, axis=0)
    up_grad = dot(b_all, hids, ((0,), (0,))).astype(BF16)
    down_grad = dot(acts, c_all, ((0,), (0,))).astype(BF16)
    return (a_next[None], b_next[None], up_grad[None], down_grad[None])


def solution(mesh):
    return jax.shard_map(
        body,
        mesh=mesh,
        in_specs=(
            P("pipe", "expert", None),
            P("pipe", "expert", None),
            P("pipe", "expert", None),
            P("pipe", "expert", None),
            P("pipe", "expert", None),
            P("pipe", None, "expert"),
            P("pipe", "expert", None),
            P("pipe", None, None),
        ),
        out_specs=(
            P("pipe", "expert", None),
            P("pipe", "expert", None),
            P("pipe", None, "expert"),
            P("pipe", "expert", None),
        ),
        check_vma=False,
    )
```

```python
import jax
import jax.numpy as jnp
from jax import lax
from jax.sharding import PartitionSpec as P

EPS = 1e-06
F32 = jnp.float32
BF16 = jnp.bfloat16


def dot(a, b, dims=((1,), (0,))):
    return lax.dot_general(a, b, (dims, ((), ())), preferred_element_type=F32)


def pipe_move(array, target):
    count = lax.axis_size("pipe")
    pairs = [(i, target(i, count) % count) for i in range(count)]
    if all(a == b for a, b in pairs):
        return array
    return lax.ppermute(array, "pipe", pairs)


def plane_move(array, experts, bit):
    devices = lax.axis_size("expert")
    return lax.ppermute(array, "expert", [(i, i ^ bit) for i in range(devices)])


def depth_exchange(blocks, experts):
    devices = lax.axis_size("expert")
    group = devices // experts
    columns = [[e * group + m for e in range(experts)] for m in range(group)]
    return lax.all_to_all(
        blocks, "expert", split_axis=0, concat_axis=0, tiled=True, axis_index_groups=columns
    )


class Layout:
    def __init__(self, experts, capacity):
        self.experts = experts
        self.main = capacity // 8 * 8
        self.rest = capacity - self.main
        self.tail = -(-experts * self.rest // 8) * 8
        self.rows = self.main + self.tail
        self.packed = experts * self.main + self.tail


def selector(ids, layout, here):
    onehot = (ids[:, None] == jnp.arange(layout.experts, dtype=jnp.int32)).astype(jnp.int32)
    slot = jnp.sum(onehot * (jnp.cumsum(onehot, axis=0) - 1), axis=1)
    place = jnp.where(slot < layout.main, slot, slot + here * layout.rest)
    row = jnp.arange(layout.experts * layout.rows, dtype=jnp.int32)[:, None]
    return ((ids * layout.rows + place)[None, :] == row).astype(BF16)


def packer(layout):
    packed = jnp.arange(layout.packed, dtype=jnp.int32)[:, None]
    row = jnp.arange(layout.experts * layout.rows, dtype=jnp.int32)[None, :]
    block, place = row // layout.rows, row % layout.rows
    target = jnp.where(
        place < layout.main,
        block * layout.main + place,
        layout.experts * layout.main + place - layout.main,
    )
    return (target == packed).astype(BF16)


def statistics(features):
    feat = features.astype(F32)
    scale = lax.rsqrt(jnp.mean(feat * feat, axis=-1, keepdims=True) + EPS)
    return feat, scale, (feat * scale).astype(BF16)


def gate_of(normed, ids, router):
    scores = dot(normed, router)
    onehot = ids[:, None] == jnp.arange(router.shape[1], dtype=jnp.int32)
    return jax.nn.sigmoid(jnp.sum(jnp.where(onehot, scores, 0.0), axis=1, keepdims=True))


def select_rows(pick, rows, layout):
    return dot(pick, rows).astype(BF16).reshape(layout.experts, layout.rows, rows.shape[1])


def pack_rows(blocks, layout):
    return dot(
        packer(layout), blocks.reshape(layout.experts * layout.rows, blocks.shape[2])
    ).astype(BF16)


def across_planes(blocks, layout):
    return pack_rows(depth_exchange(blocks, layout.experts), layout)


def swap_pair(pair, experts):
    return plane_move(pair[0], experts, 1), plane_move(pair[1], experts, 2)


def to_diagonal(from_x, from_y, experts):
    cut = -(-from_x.shape[0] // 16) * 8
    return (
        plane_move(from_x[:cut], experts, 2),
        plane_move(from_y[cut:], experts, 1),
    )


def add(value, *got):
    for term in got:
        value = value + term.astype(F32)
    return value.astype(BF16)


def for_tokens(total, layout):
    total = jnp.concatenate(total, axis=1)
    blocks = dot(packer(layout), total, ((0,), (0,))).astype(BF16)
    return blocks.reshape(layout.experts, layout.rows, blocks.shape[1])


def at_tokens(blocks, pick, layout):
    blocks = depth_exchange(blocks, layout.experts)
    blocks = blocks.reshape(layout.experts * layout.rows, blocks.shape[2])
    return dot(pick, blocks, ((0,), (0,)))


def body(a_input, a_route, b_saved, b_grad, b_route, up_weight, down_weight, router):
    devices = lax.axis_size("expert")
    experts = router.shape[2]
    group = devices // experts
    tokens, width = a_input.shape[1], a_input.shape[2]
    layout = Layout(experts, tokens * a_route.shape[2] // experts + 2)
    here = lax.axis_index("expert") // group
    up, down, cols_r = up_weight[0], down_weight[0], router[0]
    half = width // 2
    halves = (slice(0, half), slice(half, width))

    b_ids = pipe_move(b_route[0].astype(BF16), lambda i, n: n - 1 - i).astype(jnp.int32)[:, 0]
    b_x = pipe_move(b_saved[0], lambda i, n: n - 1 - i)
    b_c = pipe_move(b_grad[0], lambda i, n: n - 1 - i)
    a_ids = a_route[0][:, 0]

    after = lax.optimization_barrier
    rows = layout.packed

    own_col = jnp.sum(
        jnp.where(jnp.arange(experts) == here, cols_r.astype(F32), 0.0), axis=1, keepdims=True
    ).astype(BF16)
    col_row = own_col.astype(F32).reshape(1, width)

    a_float, _, a_normed = statistics(a_input[0])
    a_pick = selector(a_ids, layout, here)
    a_mine = [
        across_planes(select_rows(a_pick, a_normed[:, cols], layout), layout) for cols in halves
    ]
    a_x, a_y = [None, None], [None, None]
    a_x[0], a_y[0] = swap_pair((a_mine[0], a_mine[0]), experts)

    b_float, b_scale, b_normed = statistics(b_x)
    b_pick = selector(b_ids, layout, here)
    b_send = select_rows(b_pick, b_normed, layout)
    b_send, a_mine = after((b_send, a_mine))
    a_x[1], a_y[1] = swap_pair((a_mine[1], a_mine[1]), experts)
    a_far = plane_move(a_x[0], experts, 2), plane_move(a_y[1], experts, 1)
    b_got = depth_exchange(b_send, experts)

    def forward_act(block):
        hidden = dot(block[0], up[:half]) + dot(block[1], up[half:])
        return (hidden * jax.nn.sigmoid(hidden)).astype(BF16)

    a_act = [forward_act(v) for v in (a_mine, a_x, a_y, a_far)]

    def a_part(j, h):
        return dot(a_act[j], down[:, halves[h]])

    a_first = tuple(
        dot(jnp.concatenate([a_act[3], a_act[1 + h]], axis=0), down[:, halves[h]]).astype(BF16)
        for h in range(2)
    )
    a_first, b_got = after((a_first, b_got))
    a_first = swap_pair(a_first, experts)
    b_mine = pack_rows(b_got, layout)
    b_near = swap_pair((b_mine, b_mine), experts)

    b_gate = gate_of(b_normed, b_ids, cols_r)
    cot = (b_gate * b_c.astype(F32)).astype(BF16)
    c_send = select_rows(b_pick, cot, layout)
    c_send, b_mine = after((c_send, b_mine))
    c_mine = across_planes(c_send, layout)

    a_second = (
        add(a_part(1, 1), a_first[1][:rows]),
        add(a_part(2, 0), a_first[0][:rows]),
    )
    a_second, b_near = after((a_second, b_near))
    b_far = to_diagonal(b_near[0], b_near[1], experts)
    a_second = swap_pair(a_second, experts)
    c_mine, a_second = after((c_mine, a_second))
    c_near = swap_pair((c_mine, c_mine), experts)
    a_back = for_tokens(
        [
            add(a_part(0, 0), a_first[0][rows:], a_second[1]),
            add(a_part(0, 1), a_first[1][rows:], a_second[0]),
        ],
        layout,
    )
    c_near, b_far, a_back = after((c_near, b_far, a_back))
    c_far = to_diagonal(c_near[0], c_near[1], experts)

    def backward(block, cots):
        hidden = dot(block, up)
        score = dot(block, own_col)
        sigma = jax.nn.sigmoid(hidden)
        active = hidden * sigma
        act_grad = dot(cots, down, ((1,), (1,)))
        hid_grad = (act_grad * sigma * (1.0 + hidden * (1.0 - sigma))).astype(BF16)
        term = jnp.sum(active * act_grad, axis=1, keepdims=True)
        return active.astype(BF16), hid_grad, term * jax.nn.sigmoid(-score)

    done = [backward(v, w) for v, w in zip((b_mine,) + b_near, (c_mine,) + c_near)]
    quarter = half // 2

    def piece(c, side):
        begin = c * half + side * quarter
        return slice(begin, begin + quarter)

    def b_part(j, c, side):
        cols = piece(c, side)
        return dot(done[j][1], up[cols], ((1,), (1,))) + done[j][2] * col_row[:, cols]

    b_plain = [tuple(add(b_part(1 + side, c, side)) for side in range(2)) for c in range(2)]
    b_plain = [swap_pair(pair, experts) for pair in b_plain]
    ends = [backward(v, w) for v, w in zip(b_far, c_far)]
    done.append(tuple(jnp.concatenate(pair, axis=0) for pair in zip(*ends)))

    a_gate = gate_of(a_normed, a_ids, cols_r)
    a_out = (a_float + a_gate * at_tokens(a_back, a_pick, layout)).astype(BF16)
    a_next = pipe_move(a_out, lambda i, n: i + 1)

    b_relay = [tuple(add(b_part(3, c, side)) for side in range(2)) for c in range(2)]
    b_relay[0], b_plain[0] = after((b_relay[0], b_plain[0]))
    b_relay = [swap_pair(pair, experts) for pair in b_relay]
    b_second = [
        swap_pair(
            (
                add(b_part(1, c, 1), b_relay[c][1]),
                add(b_part(2, c, 0), b_relay[c][0]),
            ),
            experts,
        )
        for c in range(2)
    ]
    pieces = []
    for c in range(2):
        total = [
            add(b_part(0, c, 0), b_plain[c][0], b_second[c][1]),
            add(b_part(0, c, 1), b_plain[c][1], b_second[c][0]),
        ]
        pieces.append(at_tokens(for_tokens(total, layout), b_pick, layout))
    normed_grad = jnp.concatenate(pieces, axis=1)
    along = jnp.sum(normed_grad * b_float, axis=-1, keepdims=True) / width
    feature_grad = b_scale * normed_grad - b_float * (b_scale * b_scale * b_scale) * along
    b_out = (b_c.astype(F32) + feature_grad).astype(BF16)
    b_next = pipe_move(b_out, lambda i, n: n - i)

    acts, hids = [jnp.concatenate([d[i] for d in done], axis=0) for i in range(2)]
    b_all = jnp.concatenate((b_mine,) + b_near + b_far, axis=0)
    c_all = jnp.concatenate((c_mine,) + c_near + c_far, axis=0)
    up_grad = dot(b_all, hids, ((0,), (0,))).astype(BF16)
    down_grad = dot(acts, c_all, ((0,), (0,))).astype(BF16)
    return (a_next[None], b_next[None], up_grad[None], down_grad[None])


def solution(mesh):
    return jax.shard_map(
        body,
        mesh=mesh,
        in_specs=(
            P("pipe", "expert", None),
            P("pipe", "expert", None),
            P("pipe", "expert", None),
            P("pipe", "expert", None),
            P("pipe", "expert", None),
            P("pipe", None, "expert"),
            P("pipe", "expert", None),
            P("pipe", None, None),
        ),
        out_specs=(
            P("pipe", "expert", None),
            P("pipe", "expert", None),
            P("pipe", None, "expert"),
            P("pipe", "expert", None),
        ),
        check_vma=False,
    )
```

```python
import jax
import jax.numpy as jnp
from jax import lax
from jax.experimental import pallas as pl
from jax.experimental.pallas import tpu as pltpu
from jax.sharding import PartitionSpec as P

EPS = 1e-06
F32 = jnp.float32
BF16 = jnp.bfloat16


def dot(a, b, dims=((1,), (0,))):
    return lax.dot_general(a, b, (dims, ((), ())), preferred_element_type=F32)


def pipe_move(array, target):
    count = lax.axis_size("pipe")
    pairs = [(i, target(i, count) % count) for i in range(count)]
    if all(a == b for a, b in pairs):
        return array
    return lax.ppermute(array, "pipe", pairs)


def plane_move(array, experts, bit):
    devices = lax.axis_size("expert")
    return lax.ppermute(array, "expert", [(i, i ^ bit) for i in range(devices)])


def depth_exchange(blocks, experts):
    devices = lax.axis_size("expert")
    group = devices // experts
    columns = [[e * group + m for e in range(experts)] for m in range(group)]
    return lax.all_to_all(
        blocks, "expert", split_axis=0, concat_axis=0, tiled=True, axis_index_groups=columns
    )


class Layout:
    def __init__(self, experts, capacity):
        self.experts = experts
        self.main = capacity // 8 * 8
        self.rest = capacity - self.main
        self.tail = -(-experts * self.rest // 8) * 8
        self.rows = self.main + self.tail
        self.packed = experts * self.main + self.tail


def selector(ids, layout, here):
    onehot = (ids[:, None] == jnp.arange(layout.experts, dtype=jnp.int32)).astype(jnp.int32)
    slot = jnp.sum(onehot * (jnp.cumsum(onehot, axis=0) - 1), axis=1)
    place = jnp.where(slot < layout.main, slot, slot + here * layout.rest)
    row = jnp.arange(layout.experts * layout.rows, dtype=jnp.int32)[:, None]
    return ((ids * layout.rows + place)[None, :] == row).astype(BF16)


def packer(layout):
    packed = jnp.arange(layout.packed, dtype=jnp.int32)[:, None]
    row = jnp.arange(layout.experts * layout.rows, dtype=jnp.int32)[None, :]
    block, place = row // layout.rows, row % layout.rows
    target = jnp.where(
        place < layout.main,
        block * layout.main + place,
        layout.experts * layout.main + place - layout.main,
    )
    return (target == packed).astype(BF16)


def on_core(name, work, outs, *args):
    def kernel(*refs):
        work(refs[: len(args)], refs[len(args) :])

    space = pl.BlockSpec(memory_space=pltpu.VMEM)
    return pl.pallas_call(
        kernel,
        out_shape=[jax.ShapeDtypeStruct(shape, kind) for shape, kind in outs],
        in_specs=[space] * len(args),
        out_specs=[space] * len(outs),
        compiler_params=pltpu.CompilerParams(vmem_limit_bytes=40 * 2**20),
        cost_estimate=pl.CostEstimate(flops=10**6, bytes_accessed=10**5, transcendentals=0),
        name=name,
    )(*args)


NT = ((1,), (1,))
TN = ((0,), (0,))


def pack_halves(blocks, select):
    rows, half = select.shape[0], blocks.shape[1] // 2

    def work(ins, outs):
        for h in range(2):
            outs[h][...] = dot(ins[1][...], ins[0][:, h * half : (h + 1) * half]).astype(BF16)

    return on_core("pack", work, [((rows, half), BF16)] * 2, blocks, select)


def a_near_rows(blocks, up):
    half, hidden_units = up.shape[0] // 2, up.shape[1]
    rows = blocks[0][0].shape[0]

    def work(ins, outs):
        for j in range(3):
            hidden = dot(ins[2 * j][...], ins[6][:half]) + dot(ins[2 * j + 1][...], ins[6][half:])
            outs[0][j] = (hidden * jax.nn.sigmoid(hidden)).astype(BF16)

    flat = [half_block for block in blocks for half_block in block]
    return on_core("a_near", work, [((3, rows, hidden_units), BF16)], *flat, up)[0]


def a_far_rows(block, act, up, down):
    half, rows = up.shape[0] // 2, act.shape[1]

    def work(ins, outs):
        lo, hi, acts, up_ref, down_ref = ins
        hidden = dot(lo[...], up_ref[:half]) + dot(hi[...], up_ref[half:])
        far = (hidden * jax.nn.sigmoid(hidden)).astype(BF16)
        for h in range(2):
            weights = down_ref[:, h * half : (h + 1) * half]
            outs[h][0] = dot(far, weights).astype(BF16)
            outs[h][1] = dot(acts[1 + h], weights).astype(BF16)

    return on_core("a_far", work, [((2, rows, half), BF16)] * 2, *block, act, up, down)


def a_second_rows(act, down, got):
    half, rows = down.shape[1] // 2, act.shape[1]

    def work(ins, outs):
        acts, down_ref, by_x, by_y = ins
        outs[0][...] = (dot(acts[1], down_ref[:, half:]) + by_y[0].astype(F32)).astype(BF16)
        outs[1][...] = (dot(acts[2], down_ref[:, :half]) + by_x[0].astype(F32)).astype(BF16)

    return on_core("a_second", work, [((rows, half), BF16)] * 2, act, down, *got)


def a_total_rows(act, down, first, second, place):
    half = down.shape[1] // 2

    def work(ins, outs):
        acts, down_ref, first_x, first_y, second_x, second_y, place_ref = ins
        for h, (one, two) in enumerate(((first_x, second_y), (first_y, second_x))):
            cols = slice(h * half, (h + 1) * half)
            total = dot(acts[0], down_ref[:, cols]) + one[1].astype(F32) + two[...].astype(F32)
            outs[0][:, cols] = dot(place_ref[...], total.astype(BF16)).astype(BF16)

    outs = [((place.shape[0], 2 * half), BF16)]
    return on_core("a_total", work, outs, act, down, *first, *second, place)[0]


def back_rows(x_lo, x_hi, c_lo, c_hi, up_ref, down_ref, col_ref):
    half = x_lo.shape[1]
    hidden = dot(x_lo, up_ref[:half]) + dot(x_hi, up_ref[half:])
    score = (dot(x_lo, col_ref[:half]) + dot(x_hi, col_ref[half:]))[:, :1]
    act_grad = dot(c_lo, down_ref[:, :half], NT) + dot(c_hi, down_ref[:, half:], NT)
    sigma = jax.nn.sigmoid(hidden)
    active = hidden * sigma
    hid_grad = (act_grad * sigma * (1.0 + hidden * (1.0 - sigma))).astype(BF16)
    term = jnp.sum(active * act_grad, axis=1, keepdims=True) * jax.nn.sigmoid(-score)
    return active.astype(BF16), hid_grad, term


def grad_rows(hid_grad, term, up_ref, line_ref, cols):
    return dot(hid_grad, up_ref[cols], NT) + term * line_ref[:, cols]


def piece(c, side, half):
    begin = c * half + side * (half // 2)
    return slice(begin, begin + half // 2)


def b_near_rows(blocks, cots, up, down, col, line):
    half, units, rows = up.shape[0] // 2, up.shape[1], blocks[0][0].shape[0]

    def work(ins, outs):
        up_ref, down_ref, col_ref, line_ref = ins[12:]
        for j in range(3):
            act, hid, term = back_rows(
                ins[2 * j][...],
                ins[2 * j + 1][...],
                ins[6 + 2 * j][...],
                ins[7 + 2 * j][...],
                up_ref,
                down_ref,
                col_ref,
            )
            outs[0][j], outs[1][j] = act, hid
            outs[2][j] = jnp.broadcast_to(term, (rows, 128))
            if j:
                for c in range(2):
                    cols = piece(c, j - 1, half)
                    part = grad_rows(hid, term, up_ref, line_ref, cols)
                    outs[2 + j][c] = part.astype(BF16)

    flat = [v for block in blocks for v in block] + [v for block in cots for v in block]
    outs = [((3, rows, units), BF16)] * 2 + [((3, rows, 128), F32)]
    outs += [((2, rows, half // 2), BF16)] * 2
    act, hid, term, by_x, by_y = on_core("b_near", work, outs, *flat, up, down, col, line)
    return (act, hid, term), (by_x, by_y)


def b_far_rows(block, cots, up, down, col, line):
    half, units, rows = up.shape[0] // 2, up.shape[1], block[0].shape[0]

    def work(ins, outs):
        up_ref, down_ref, col_ref, line_ref = ins[4:]
        values = [ref[...] for ref in ins[:4]]
        act, hid, term = back_rows(*values, up_ref, down_ref, col_ref)
        outs[0][...], outs[1][...] = act, hid
        for c in range(2):
            for side in range(2):
                part = grad_rows(hid, term, up_ref, line_ref, piece(c, side, half))
                outs[2 + 2 * c + side][...] = part.astype(BF16)

    outs = [((rows, units), BF16)] * 2 + [((rows, half // 2), BF16)] * 4
    act, hid, x0, y0, x1, y1 = on_core("b_far", work, outs, *block, *cots, up, down, col, line)
    return (act, hid), [(x0, y0), (x1, y1)]


def b_second_rows(near, up, line, got, c):
    half, rows = up.shape[0] // 2, got[0].shape[0]

    def work(ins, outs):
        hids, terms, up_ref, line_ref, by_x, by_y = ins
        for side, ref in enumerate((by_y, by_x)):
            j, cols = 1 + side, piece(c, 1 - side, half)
            part = grad_rows(hids[j], terms[j][:, :1], up_ref, line_ref, cols)
            outs[side][...] = (part + ref[...].astype(F32)).astype(BF16)

    outs = [((rows, half // 2), BF16)] * 2
    return on_core("b_second", work, outs, near[1], near[2], up, line, *got)


def b_total_rows(near, up, line, plain, second, place, c):
    half = up.shape[0] // 2
    quarter = half // 2

    def work(ins, outs):
        hids, terms, up_ref, line_ref, plain_x, plain_y, second_x, second_y, place_ref = ins
        for side, (one, two) in enumerate(((plain_x, second_y), (plain_y, second_x))):
            part = grad_rows(hids[0], terms[0][:, :1], up_ref, line_ref, piece(c, side, half))
            total = (part + one[c].astype(F32) + two[...].astype(F32)).astype(BF16)
            cols = slice(side * quarter, (side + 1) * quarter)
            outs[0][:, cols] = dot(place_ref[...], total).astype(BF16)

    outs = [((place.shape[0], half), BF16)]
    return on_core("b_total", work, outs, near[1], near[2], up, line, *plain, *second, place)[0]


def weight_grads(blocks, cots, near, far):
    half, units = blocks[0][0].shape[1], far[0].shape[1]
    tile = 256

    def work(ins, outs):
        xs, cs = ins[0:8], ins[8:16]
        acts = [ins[16][j] for j in range(3)] + [ins[18][...]]
        hids = [ins[17][j] for j in range(3)] + [ins[19][...]]
        for h in range(2):
            for begin in range(0, half, tile):
                cols, out = slice(begin, begin + tile), slice(h * half + begin, h * half + begin + tile)
                up_sum, down_sum = 0.0, 0.0
                for j in range(4):
                    up_sum = up_sum + dot(xs[2 * j + h][:, cols], hids[j], TN)
                    down_sum = down_sum + dot(acts[j], cs[2 * j + h][:, cols], TN)
                outs[0][out, :] = up_sum.astype(BF16)
                outs[1][:, out] = down_sum.astype(BF16)

    flat = [v for block in blocks for v in block] + [v for block in cots for v in block]
    outs = [((2 * half, units), BF16), ((units, 2 * half), BF16)]
    return on_core("weight_grads", work, outs, *flat, near[0], near[1], *far)


def statistics(features):
    feat = features.astype(F32)
    scale = lax.rsqrt(jnp.mean(feat * feat, axis=-1, keepdims=True) + EPS)
    return feat, scale, (feat * scale).astype(BF16)


def gate_of(normed, ids, router):
    scores = dot(normed, router)
    onehot = ids[:, None] == jnp.arange(router.shape[1], dtype=jnp.int32)
    return jax.nn.sigmoid(jnp.sum(jnp.where(onehot, scores, 0.0), axis=1, keepdims=True))


def select_rows(pick, rows, layout):
    return dot(pick, rows).astype(BF16).reshape(layout.experts, layout.rows, rows.shape[1])


def across_planes(blocks, layout):
    blocks = depth_exchange(blocks, layout.experts)
    return blocks.reshape(layout.experts * layout.rows, blocks.shape[2])


def swap_pair(pair, experts):
    return plane_move(pair[0], experts, 1), plane_move(pair[1], experts, 2)


def at_tokens(blocks, pick, layout):
    blocks = blocks.reshape(layout.experts, layout.rows, blocks.shape[1])
    return dot(pick, across_planes(blocks, layout), TN)


def spread_halves(mine, experts):
    x_lo, y_hi = swap_pair(mine, experts)
    x_hi, y_lo = swap_pair((mine[1], mine[0]), experts)
    return (x_lo, x_hi), (y_lo, y_hi)


def relay_halves(near, experts):
    return plane_move(near[0][0], experts, 2), plane_move(near[1][1], experts, 1)


def body(a_input, a_route, b_saved, b_grad, b_route, up_weight, down_weight, router):
    devices = lax.axis_size("expert")
    experts = router.shape[2]
    group = devices // experts
    tokens, width = a_input.shape[1], a_input.shape[2]
    layout = Layout(experts, tokens * a_route.shape[2] // experts + 2)
    here = lax.axis_index("expert") // group
    up, down, cols_r = up_weight[0], down_weight[0], router[0]
    half = width // 2

    b_ids = pipe_move(b_route[0].astype(BF16), lambda i, n: n - 1 - i).astype(jnp.int32)[:, 0]
    b_x = pipe_move(b_saved[0], lambda i, n: n - 1 - i)
    b_c = pipe_move(b_grad[0], lambda i, n: n - 1 - i)
    a_ids = a_route[0][:, 0]

    after = lax.optimization_barrier
    own = jnp.where(jnp.arange(experts) == here, cols_r.astype(F32), 0.0)
    own = jnp.sum(own, axis=1, keepdims=True)
    line = own.reshape(1, width)
    col = jnp.where(jnp.arange(128)[None, :] == 0, own, 0.0).astype(BF16)
    select = packer(layout)
    place = select.T

    a_float, _, a_normed = statistics(a_input[0])
    a_pick = selector(a_ids, layout, here)
    a_blocks = across_planes(select_rows(a_pick, a_normed, layout), layout)
    a_mine = tuple(pack_halves(a_blocks, select))

    b_float, b_scale, b_normed = statistics(b_x)
    b_pick = selector(b_ids, layout, here)
    b_send = select_rows(b_pick, b_normed, layout)
    b_send, a_mine = after((b_send, a_mine))
    a_near = spread_halves(a_mine, experts)
    a_far = relay_halves(a_near, experts)
    b_blocks = across_planes(b_send, layout)

    act = a_near_rows((a_mine,) + a_near, up)
    a_first = a_far_rows(a_far, act, up, down)
    a_first, b_blocks = after((a_first, b_blocks))
    a_first = swap_pair(a_first, experts)
    b_mine = tuple(pack_halves(b_blocks, select))

    b_gate = gate_of(b_normed, b_ids, cols_r)
    cot = (b_gate * b_c.astype(F32)).astype(BF16)
    c_send = select_rows(b_pick, cot, layout)
    c_send, b_mine = after((c_send, b_mine))
    b_near = spread_halves(b_mine, experts)
    b_far = relay_halves(b_near, experts)
    c_blocks = across_planes(c_send, layout)

    a_second = a_second_rows(act, down, a_first)
    a_second, c_blocks = after((a_second, c_blocks))
    a_second = swap_pair(a_second, experts)
    c_mine = tuple(pack_halves(c_blocks, select))
    c_near = spread_halves(c_mine, experts)
    c_far = relay_halves(c_near, experts)
    a_back = a_total_rows(act, down, a_first, a_second, place)
    a_gate = gate_of(a_normed, a_ids, cols_r)
    a_out = (a_float + a_gate * at_tokens(a_back, a_pick, layout)).astype(BF16)
    a_next = pipe_move(a_out, lambda i, n: i + 1)

    near, b_plain = b_near_rows((b_mine,) + b_near, (c_mine,) + c_near, up, down, col, line)
    b_plain = swap_pair(b_plain, experts)
    far, b_relay = b_far_rows(b_far, c_far, up, down, col, line)
    b_relay = [swap_pair(pair, experts) for pair in b_relay]
    pieces = []
    for c in range(2):
        second = swap_pair(b_second_rows(near, up, line, b_relay[c], c), experts)
        b_back = b_total_rows(near, up, line, b_plain, second, place, c)
        pieces.append(at_tokens(b_back, b_pick, layout))
    normed_grad = jnp.concatenate(pieces, axis=1)
    along = jnp.sum(normed_grad * b_float, axis=-1, keepdims=True) / width
    feature_grad = b_scale * normed_grad - b_float * (b_scale * b_scale * b_scale) * along
    b_out = (b_c.astype(F32) + feature_grad).astype(BF16)
    b_next = pipe_move(b_out, lambda i, n: n - i)

    up_grad, down_grad = weight_grads(
        (b_mine,) + b_near + (b_far,), (c_mine,) + c_near + (c_far,), near, far
    )
    return (a_next[None], b_next[None], up_grad[None], down_grad[None])


def solution(mesh):
    return jax.shard_map(
        body,
        mesh=mesh,
        in_specs=(
            P("pipe", "expert", None),
            P("pipe", "expert", None),
            P("pipe", "expert", None),
            P("pipe", "expert", None),
            P("pipe", "expert", None),
            P("pipe", None, "expert"),
            P("pipe", "expert", None),
            P("pipe", None, None),
        ),
        out_specs=(
            P("pipe", "expert", None),
            P("pipe", "expert", None),
            P("pipe", None, "expert"),
            P("pipe", "expert", None),
        ),
        check_vma=False,
    )
```

```python
import jax
import jax.numpy as jnp
from jax import lax
from jax.experimental import pallas as pl
from jax.experimental.pallas import tpu as pltpu
from jax.sharding import PartitionSpec as P

EPS = 1e-06
F32 = jnp.float32
BF16 = jnp.bfloat16


def dot(a, b, dims=((1,), (0,))):
    return lax.dot_general(a, b, (dims, ((), ())), preferred_element_type=F32)


def pipe_move(array, target):
    count = lax.axis_size("pipe")
    pairs = [(i, target(i, count) % count) for i in range(count)]
    if all(a == b for a, b in pairs):
        return array
    return lax.ppermute(array, "pipe", pairs)


def plane_move(array, experts, bit):
    devices = lax.axis_size("expert")
    return lax.ppermute(array, "expert", [(i, i ^ bit) for i in range(devices)])


def depth_exchange(blocks, experts):
    devices = lax.axis_size("expert")
    group = devices // experts
    columns = [[e * group + m for e in range(experts)] for m in range(group)]
    return lax.all_to_all(
        blocks, "expert", split_axis=0, concat_axis=0, tiled=True, axis_index_groups=columns
    )


class Layout:
    def __init__(self, experts, capacity):
        self.experts = experts
        self.main = capacity // 8 * 8
        self.rest = capacity - self.main
        self.tail = -(-experts * self.rest // 8) * 8
        self.rows = self.main + self.tail
        self.packed = experts * self.main + self.tail


def selector(ids, layout, here):
    onehot = (ids[:, None] == jnp.arange(layout.experts, dtype=jnp.int32)).astype(jnp.int32)
    slot = jnp.sum(onehot * (jnp.cumsum(onehot, axis=0) - 1), axis=1)
    place = jnp.where(slot < layout.main, slot, slot + here * layout.rest)
    row = jnp.arange(layout.experts * layout.rows, dtype=jnp.int32)[:, None]
    return ((ids * layout.rows + place)[None, :] == row).astype(BF16)


def packer(layout):
    packed = jnp.arange(layout.packed, dtype=jnp.int32)[:, None]
    row = jnp.arange(layout.experts * layout.rows, dtype=jnp.int32)[None, :]
    block, place = row // layout.rows, row % layout.rows
    target = jnp.where(
        place < layout.main,
        block * layout.main + place,
        layout.experts * layout.main + place - layout.main,
    )
    return (target == packed).astype(BF16)


def on_core(name, work, outs, *args):
    def kernel(*refs):
        work(refs[: len(args)], refs[len(args) :])

    space = pl.BlockSpec(memory_space=pltpu.VMEM)
    return pl.pallas_call(
        kernel,
        out_shape=[jax.ShapeDtypeStruct(shape, kind) for shape, kind in outs],
        in_specs=[space] * len(args),
        out_specs=[space] * len(outs),
        compiler_params=pltpu.CompilerParams(vmem_limit_bytes=16 * 2**20),
        cost_estimate=pl.CostEstimate(flops=10**6, bytes_accessed=10**5, transcendentals=0),
        name=name,
    )(*args)


NT = ((1,), (1,))
TN = ((0,), (0,))


def pack_part(blocks, select):
    def work(ins, outs):
        outs[0][...] = dot(ins[1][...], ins[0][...]).astype(BF16)

    return on_core("pack", work, [((select.shape[0], blocks.shape[1]), BF16)], blocks, select)[0]


def pack_halves(blocks, select):
    rows, half = select.shape[0], blocks.shape[1] // 2

    def work(ins, outs):
        for h in range(2):
            outs[h][...] = dot(ins[1][...], ins[0][:, h * half : (h + 1) * half]).astype(BF16)

    return tuple(on_core("pack", work, [((rows, half), BF16)] * 2, blocks, select))


def a_near_rows(blocks, up, down):
    half, units, rows = up.shape[0] // 2, up.shape[1], blocks[0][0].shape[0]

    def work(ins, outs):
        up_ref, down_ref = ins[6:]
        for j in range(3):
            hidden = dot(ins[2 * j][...], up_ref[:half]) + dot(ins[2 * j + 1][...], up_ref[half:])
            act = (hidden * jax.nn.sigmoid(hidden)).astype(BF16)
            outs[0][j] = act
            if j:
                cols = slice((j - 1) * half, j * half)
                outs[j][...] = dot(act, down_ref[:, cols]).astype(BF16)

    flat = [v for block in blocks for v in block]
    outs = [((3, rows, units), BF16)] + [((rows, half), BF16)] * 2
    act, by_x, by_y = on_core("a_near", work, outs, *flat, up, down)
    return act, (by_x, by_y)


def a_far_rows(block, act, up, down):
    half, rows = up.shape[0] // 2, act.shape[1]

    def work(ins, outs):
        lo, hi, _, up_ref, down_ref = ins
        hidden = dot(lo[...], up_ref[:half]) + dot(hi[...], up_ref[half:])
        far = (hidden * jax.nn.sigmoid(hidden)).astype(BF16)
        for h in range(2):
            outs[h][...] = dot(far, down_ref[:, h * half : (h + 1) * half]).astype(BF16)

    return tuple(on_core("a_far", work, [((rows, half), BF16)] * 2, *block, act, up, down))


def a_second_rows(act, down, got):
    half, rows = down.shape[1] // 2, act.shape[1]

    def work(ins, outs):
        acts, down_ref, by_x, by_y = ins
        outs[0][...] = (dot(acts[1], down_ref[:, half:]) + by_y[...].astype(F32)).astype(BF16)
        outs[1][...] = (dot(acts[2], down_ref[:, :half]) + by_x[...].astype(F32)).astype(BF16)

    return tuple(on_core("a_second", work, [((rows, half), BF16)] * 2, act, down, *got))


def a_total_rows(act, down, plain, second, place):
    half = down.shape[1] // 2

    def work(ins, outs):
        acts, down_ref, plain_x, plain_y, second_x, second_y, place_ref = ins
        for h, (one, two) in enumerate(((plain_x, second_y), (plain_y, second_x))):
            cols = slice(h * half, (h + 1) * half)
            total = dot(acts[0], down_ref[:, cols]) + one[...].astype(F32) + two[...].astype(F32)
            outs[0][:, cols] = dot(place_ref[...], total.astype(BF16)).astype(BF16)

    outs = [((place.shape[0], 2 * half), BF16)]
    return on_core("a_total", work, outs, act, down, *plain, *second, place)[0]


def b_hidden_rows(blocks, up, col):
    half, units, rows = up.shape[0] // 2, up.shape[1], blocks[0][0].shape[0]

    def work(ins, outs):
        up_ref, col_ref = ins[8:]
        for j in range(4):
            lo, hi = ins[2 * j][...], ins[2 * j + 1][...]
            outs[0][j] = dot(lo, up_ref[:half]) + dot(hi, up_ref[half:])
            outs[1][j] = dot(lo, col_ref[:half]) + dot(hi, col_ref[half:])

    flat = [v for block in blocks for v in block]
    outs = [((4, rows, units), F32), ((4, rows, 128), F32)]
    return tuple(on_core("b_hidden", work, outs, *flat, up, col))


def back_rows(hidden, score, c_lo, c_hi, down_ref):
    half = c_lo.shape[1]
    act_grad = dot(c_lo, down_ref[:half]) + dot(c_hi, down_ref[half:])
    sigma = jax.nn.sigmoid(hidden)
    active = hidden * sigma
    hid_grad = (act_grad * sigma * (1.0 + hidden * (1.0 - sigma))).astype(BF16)
    term = jnp.sum(active * act_grad, axis=1, keepdims=True) * jax.nn.sigmoid(-score[:, :1])
    return active.astype(BF16), hid_grad, term


def grad_rows(hid_grad, term, up_ref, line_ref, cols):
    return dot(hid_grad, up_ref[:, cols]) + term * line_ref[:, cols]


def piece(c, side, half):
    begin = c * half + side * (half // 2)
    return slice(begin, begin + half // 2)


def b_near_rows(cots, early, up, down, line):
    half, units, rows = up.shape[1] // 2, up.shape[0], cots[0][0].shape[0]

    def work(ins, outs):
        hidden, score, up_ref, down_ref, line_ref = ins[6:]
        for j in range(3):
            lo, hi = ins[2 * j][...], ins[2 * j + 1][...]
            act, hid, term = back_rows(hidden[j], score[j], lo, hi, down_ref)
            outs[0][j], outs[1][j] = act, hid
            outs[2][j] = jnp.broadcast_to(term, (rows, 128))
            if j:
                for c in range(2):
                    cols = piece(c, j - 1, half)
                    part = grad_rows(hid, term, up_ref, line_ref, cols)
                    outs[2 + j][c] = part.astype(BF16)

    flat = [v for block in cots for v in block]
    outs = [((3, rows, units), BF16)] * 2 + [((3, rows, 128), F32)]
    outs += [((2, rows, half // 2), BF16)] * 2
    act, hid, term, by_x, by_y = on_core("b_near", work, outs, *flat, *early, up, down, line)
    return (act, hid, term), (by_x, by_y)


def b_far_rows(cots, early, near, up, down, line):
    half, units, rows = up.shape[1] // 2, up.shape[0], cots[0].shape[0]

    def work(ins, outs):
        lo, hi, hidden, score, _, up_ref, down_ref, line_ref = ins
        act, hid, term = back_rows(hidden[3], score[3], lo[...], hi[...], down_ref)
        outs[0][...], outs[1][...] = act, hid
        for c in range(2):
            for side in range(2):
                part = grad_rows(hid, term, up_ref, line_ref, piece(c, side, half))
                outs[2 + 2 * c + side][...] = part.astype(BF16)

    outs = [((rows, units), BF16)] * 2 + [((rows, half // 2), BF16)] * 4
    args = (*cots, *early, near[2], up, down, line)
    act, hid, x0, y0, x1, y1 = on_core("b_far", work, outs, *args)
    return (act, hid), [(x0, y0), (x1, y1)]


def b_second_rows(near, up, line, got, c):
    half, rows = up.shape[1] // 2, got[0].shape[0]

    def work(ins, outs):
        hids, terms, up_ref, line_ref, by_x, by_y = ins
        for side, ref in enumerate((by_y, by_x)):
            j, cols = 1 + side, piece(c, 1 - side, half)
            part = grad_rows(hids[j], terms[j][:, :1], up_ref, line_ref, cols)
            outs[side][...] = (part + ref[...].astype(F32)).astype(BF16)

    outs = [((rows, half // 2), BF16)] * 2
    return on_core("b_second", work, outs, near[1], near[2], up, line, *got)


def b_total_rows(near, up, line, plain, second, place, c):
    half = up.shape[1] // 2
    quarter = half // 2

    def work(ins, outs):
        hids, terms, up_ref, line_ref, plain_x, plain_y, second_x, second_y, place_ref = ins
        for side, (one, two) in enumerate(((plain_x, second_y), (plain_y, second_x))):
            part = grad_rows(hids[0], terms[0][:, :1], up_ref, line_ref, piece(c, side, half))
            total = (part + one[c].astype(F32) + two[...].astype(F32)).astype(BF16)
            cols = slice(side * quarter, (side + 1) * quarter)
            outs[0][:, cols] = dot(place_ref[...], total).astype(BF16)

    outs = [((place.shape[0], half), BF16)]
    return on_core("b_total", work, outs, near[1], near[2], up, line, *plain, *second, place)[0]


def weight_grads(blocks, cots, near, far):
    half, units = blocks[0][0].shape[1], far[0].shape[1]
    tile = 256

    def work(ins, outs):
        xs, cs = ins[0:8], ins[8:16]
        acts = [ins[16][j] for j in range(3)] + [ins[18][...]]
        hids = [ins[17][j] for j in range(3)] + [ins[19][...]]
        for h in range(2):
            for begin in range(0, half, tile):
                cols, out = slice(begin, begin + tile), slice(h * half + begin, h * half + begin + tile)
                up_sum, down_sum = 0.0, 0.0
                for j in range(4):
                    up_sum = up_sum + dot(xs[2 * j + h][:, cols], hids[j], TN)
                    down_sum = down_sum + dot(acts[j], cs[2 * j + h][:, cols], TN)
                outs[0][out, :] = up_sum.astype(BF16)
                outs[1][:, out] = down_sum.astype(BF16)

    flat = [v for block in blocks for v in block] + [v for block in cots for v in block]
    outs = [((2 * half, units), BF16), ((units, 2 * half), BF16)]
    return on_core("weight_grads", work, outs, *flat, near[0], near[1], *far)


def statistics(features):
    feat = features.astype(F32)
    scale = lax.rsqrt(jnp.mean(feat * feat, axis=-1, keepdims=True) + EPS)
    return feat, scale, (feat * scale).astype(BF16)


def gate_of(normed, ids, router):
    scores = dot(normed, router)
    onehot = ids[:, None] == jnp.arange(router.shape[1], dtype=jnp.int32)
    return jax.nn.sigmoid(jnp.sum(jnp.where(onehot, scores, 0.0), axis=1, keepdims=True))


def select_rows(pick, rows, layout):
    return dot(pick, rows).astype(BF16).reshape(layout.experts, layout.rows, rows.shape[1])


def across_planes(blocks, layout):
    blocks = depth_exchange(blocks, layout.experts)
    return blocks.reshape(layout.experts * layout.rows, blocks.shape[2])


def swap_pair(pair, experts):
    return plane_move(pair[0], experts, 1), plane_move(pair[1], experts, 2)


def at_tokens(blocks, pick, layout):
    blocks = blocks.reshape(layout.experts, layout.rows, blocks.shape[1])
    return dot(pick, across_planes(blocks, layout), TN)


def spread_halves(mine, experts):
    x_lo, y_hi = swap_pair(mine, experts)
    x_hi, y_lo = swap_pair((mine[1], mine[0]), experts)
    return (x_lo, x_hi), (y_lo, y_hi)


def relay_halves(near, experts):
    return plane_move(near[0][0], experts, 2), plane_move(near[1][1], experts, 1)


def body(a_input, a_route, b_saved, b_grad, b_route, up_weight, down_weight, router):
    devices = lax.axis_size("expert")
    experts = router.shape[2]
    group = devices // experts
    tokens, width = a_input.shape[1], a_input.shape[2]
    layout = Layout(experts, tokens * a_route.shape[2] // experts + 2)
    here = lax.axis_index("expert") // group
    up, down, cols_r = up_weight[0], down_weight[0], router[0]
    half = width // 2

    b_ids = pipe_move(b_route[0].astype(BF16), lambda i, n: n - 1 - i).astype(jnp.int32)[:, 0]
    b_x = pipe_move(b_saved[0], lambda i, n: n - 1 - i)
    b_c = pipe_move(b_grad[0], lambda i, n: n - 1 - i)
    a_ids = a_route[0][:, 0]

    after = lax.optimization_barrier
    own = jnp.where(jnp.arange(experts) == here, cols_r.astype(F32), 0.0)
    own = jnp.sum(own, axis=1, keepdims=True)
    line = own.reshape(1, width)
    col = jnp.where(jnp.arange(128)[None, :] == 0, own, 0.0).astype(BF16)
    select = packer(layout)
    place = select.T

    a_float, _, a_normed = statistics(a_input[0])
    a_pick = selector(a_ids, layout, here)
    a_mine = []
    for h in range(2):
        send = select_rows(a_pick, a_normed[:, h * half : (h + 1) * half], layout)
        a_mine.append(pack_part(across_planes(send, layout), select))
    a_mine = tuple(a_mine)

    b_float, b_scale, b_normed = statistics(b_x)
    b_pick = selector(b_ids, layout, here)
    b_send = select_rows(b_pick, b_normed, layout)
    a_x_lo, a_y_lo = swap_pair((a_mine[0], a_mine[0]), experts)
    up_turned, down_turned = up.T, down.T
    b_send, a_mine, up_turned, down_turned = after((b_send, a_mine, up_turned, down_turned))
    a_x_hi, a_y_hi = swap_pair((a_mine[1], a_mine[1]), experts)
    a_near = ((a_x_lo, a_x_hi), (a_y_lo, a_y_hi))
    a_far = relay_halves(a_near, experts)
    b_blocks = across_planes(b_send, layout)

    act, a_plain = a_near_rows((a_mine,) + a_near, up, down)
    a_plain = swap_pair(a_plain, experts)
    a_relay = a_far_rows(a_far, act, up, down)
    a_relay, a_plain, b_blocks = after((a_relay, a_plain, b_blocks))
    a_relay = swap_pair(a_relay, experts)
    b_mine = pack_halves(b_blocks, select)

    b_gate = gate_of(b_normed, b_ids, cols_r)
    cot = (b_gate * b_c.astype(F32)).astype(BF16)
    c_send = select_rows(b_pick, cot, layout)
    b_near = spread_halves(b_mine, experts)
    c_send, _, a_relay = after((c_send, b_mine, a_relay))
    b_far = relay_halves(b_near, experts)
    c_blocks = across_planes(c_send, layout)

    a_second = a_second_rows(act, down, a_relay)
    a_second, c_blocks = after((a_second, c_blocks))
    a_second = swap_pair(a_second, experts)
    c_mine = pack_halves(c_blocks, select)
    c_near = spread_halves(c_mine, experts)
    c_far = relay_halves(c_near, experts)
    a_back = a_total_rows(act, down, a_plain, a_second, place)
    a_gate = gate_of(a_normed, a_ids, cols_r)
    a_out = (a_float + a_gate * at_tokens(a_back, a_pick, layout)).astype(BF16)
    a_next = pipe_move(a_out, lambda i, n: i + 1)

    early = b_hidden_rows((b_mine,) + b_near + (b_far,), up, col)
    near, b_plain = b_near_rows((c_mine,) + c_near, early, up_turned, down_turned, line)
    b_plain = swap_pair(b_plain, experts)
    far, b_relay = b_far_rows(c_far, early, near, up_turned, down_turned, line)
    b_relay[1], b_plain = after((b_relay[1], b_plain))
    b_relay = [swap_pair(pair, experts) for pair in b_relay]
    backs = []
    for c in range(2):
        second = swap_pair(b_second_rows(near, up_turned, line, b_relay[c], c), experts)
        backs.append(b_total_rows(near, up_turned, line, b_plain, second, place, c))
    backs[1], far = after((backs[1], far))
    normed_grad = jnp.concatenate([at_tokens(back, b_pick, layout) for back in backs], axis=1)
    along = jnp.sum(normed_grad * b_float, axis=-1, keepdims=True) / width
    feature_grad = b_scale * normed_grad - b_float * (b_scale * b_scale * b_scale) * along
    b_out = (b_c.astype(F32) + feature_grad).astype(BF16)
    b_next = pipe_move(b_out, lambda i, n: n - i)

    up_grad, down_grad = weight_grads(
        (b_mine,) + b_near + (b_far,), (c_mine,) + c_near + (c_far,), near, far
    )
    return (a_next[None], b_next[None], up_grad[None], down_grad[None])


def solution(mesh):
    return jax.shard_map(
        body,
        mesh=mesh,
        in_specs=(
            P("pipe", "expert", None),
            P("pipe", "expert", None),
            P("pipe", "expert", None),
            P("pipe", "expert", None),
            P("pipe", "expert", None),
            P("pipe", None, "expert"),
            P("pipe", "expert", None),
            P("pipe", None, None),
        ),
        out_specs=(
            P("pipe", "expert", None),
            P("pipe", "expert", None),
            P("pipe", None, "expert"),
            P("pipe", "expert", None),
        ),
        check_vma=False,
    )
```

```python
import jax
import jax.numpy as jnp
import numpy as np
from jax import lax
from jax.experimental import pallas as pl
from jax.experimental.pallas import tpu as pltpu
from jax.sharding import PartitionSpec as P

EPS = 1e-06
F32 = jnp.float32
BF16 = jnp.bfloat16


def dot(a, b, dims=((1,), (0,))):
    return lax.dot_general(a, b, (dims, ((), ())), preferred_element_type=F32)


def pipe_move(array, target):
    count = lax.axis_size("pipe")
    pairs = [(i, target(i, count) % count) for i in range(count)]
    if all(a == b for a, b in pairs):
        return array
    return lax.ppermute(array, "pipe", pairs)


def plane_move(array, experts, bit):
    devices = lax.axis_size("expert")
    return lax.ppermute(array, "expert", [(i, i ^ bit) for i in range(devices)])


def depth_exchange(blocks, experts):
    devices = lax.axis_size("expert")
    group = devices // experts
    columns = [[e * group + m for e in range(experts)] for m in range(group)]
    return lax.all_to_all(
        blocks, "expert", split_axis=0, concat_axis=0, tiled=True, axis_index_groups=columns
    )


class Layout:
    cuts = 4

    def __init__(self, experts, capacity):
        self.experts = experts
        self.slots = capacity
        self.block = self.cuts * capacity
        self.sent = experts * self.block
        self.packed = experts * capacity

    def places(self):
        packed = np.arange(self.packed)
        found = np.zeros((self.cuts, self.sent, self.packed), np.float32)
        for c in range(self.cuts):
            row = packed // self.slots * self.block + c * self.slots + packed % self.slots
            found[c, row, packed] = 1.0
        return jnp.asarray(found, BF16), jnp.asarray(found.transpose(0, 2, 1), BF16)


def target_rows(ids, layout):
    onehot = (ids[:, None] == jnp.arange(layout.experts, dtype=jnp.int32)).astype(jnp.int32)
    slot = jnp.sum(onehot * (jnp.cumsum(onehot, axis=0) - 1), axis=1)
    first = (ids * layout.block + slot)[:, None]
    return first + layout.slots * jnp.arange(layout.cuts, dtype=jnp.int32)[None, :]


def on_core(name, work, outs, *args):
    def kernel(*refs):
        work(refs[: len(args)], refs[len(args) :])

    space = pl.BlockSpec(memory_space=pltpu.VMEM)
    return pl.pallas_call(
        kernel,
        out_shape=[jax.ShapeDtypeStruct(shape, kind) for shape, kind in outs],
        in_specs=[space] * len(args),
        out_specs=[space] * len(outs),
        compiler_params=pltpu.CompilerParams(vmem_limit_bytes=16 * 2**20),
        cost_estimate=pl.CostEstimate(flops=10**6, bytes_accessed=10**5, transcendentals=0),
        name=name,
    )(*args)


NT = ((1,), (1,))
TN = ((0,), (0,))


TOKEN = ((8, 128), F32)


def sent_rows(values, target, sent):
    cuts, tokens = target.shape
    part = values.shape[1] // cuts
    rows = lax.broadcasted_iota(jnp.int32, (sent, tokens), 0)
    total = 0.0
    for c in range(cuts):
        pick = jnp.where(rows == target[c : c + 1, :], 1.0, 0.0).astype(BF16)
        total = total + dot(pick, values[:, c * part : (c + 1) * part])
    return total.astype(BF16)


def token_rows(ref, target):
    tokens, cuts = target.shape
    rows = lax.broadcasted_iota(jnp.int32, (tokens, ref.shape[0]), 1)
    parts = []
    for c in range(cuts):
        pick = jnp.where(rows == target[:, c : c + 1], 1.0, 0.0).astype(BF16)
        parts.append(dot(pick, ref[...]))
    return jnp.concatenate(parts, axis=1)


def send_normed(x, ids, router, target, layout, after=()):
    tokens, width = x.shape

    def work(ins, outs):
        x_ref, ids_ref, router_ref, target_ref = ins[:4]
        feat = x_ref[...].astype(F32)
        scale = lax.rsqrt(jnp.mean(feat * feat, axis=1, keepdims=True) + EPS)
        normed = (feat * scale).astype(BF16)
        outs[0][...] = sent_rows(normed, target_ref[...], layout.sent)
        scores = dot(normed, router_ref[...])
        expert = lax.broadcasted_iota(jnp.int32, scores.shape, 1)
        score = jnp.sum(jnp.where(expert == ids_ref[...], scores, 0.0), axis=1, keepdims=True)
        outs[1][...] = jnp.broadcast_to(jax.nn.sigmoid(score), (tokens, 128))

    outs = [((layout.sent, width // layout.cuts), BF16), ((tokens, 128), F32)]
    return on_core("send_normed", work, outs, x, ids, router, target.T, *after)


def send_cotangents(cot, gate, target, layout, after=()):
    def work(ins, outs):
        values = (ins[1][:, :1] * ins[0][...].astype(F32)).astype(BF16)
        outs[0][...] = sent_rows(values, ins[2][...], layout.sent)
        outs[1][...] = jnp.zeros(TOKEN[0], F32)

    outs = [((layout.sent, cot.shape[1] // layout.cuts), BF16), TOKEN]
    return on_core("send_cotangents", work, outs, cot, gate, target.T, *after)


def forward_out(x, gate, back, target):
    def work(ins, outs):
        rows = token_rows(ins[2], ins[3][...])
        outs[0][...] = (ins[0][...].astype(F32) + ins[1][:, :1] * rows).astype(BF16)

    return on_core("forward_out", work, [(x.shape, BF16)], x, gate, back, target)[0]


def backward_out(x, cot, back, target):
    width = x.shape[1]

    def work(ins, outs):
        feat = ins[0][...].astype(F32)
        scale = lax.rsqrt(jnp.mean(feat * feat, axis=1, keepdims=True) + EPS)
        normed_grad = token_rows(ins[2], ins[3][...])
        along = jnp.sum(normed_grad * feat, axis=1, keepdims=True) / width
        feature_grad = scale * normed_grad - feat * (scale * scale * scale) * along
        outs[0][...] = (ins[1][...].astype(F32) + feature_grad).astype(BF16)

    return on_core("backward_out", work, [(x.shape, BF16)], x, cot, back, target)[0]


def pack_halves(blocks, select, after=()):
    cuts, rows, _ = select.shape
    part = blocks.shape[1]
    half = cuts * part // 2

    def work(ins, outs):
        for c in range(cuts):
            begin = c * part % half
            outs[c * part // half][:, begin : begin + part] = dot(ins[1][c], ins[0][...]).astype(
                BF16
            )
        outs[2][...] = jnp.zeros(TOKEN[0], F32)

    lo, hi, token = on_core(
        "pack", work, [((rows, half), BF16)] * 2 + [TOKEN], blocks, select, *after
    )
    return (lo, hi), token


def placed(parts, place_ref):
    cuts = place_ref.shape[0]
    part = 2 * parts[0].shape[1] // cuts
    rows = 0.0
    for c in range(cuts):
        begin = c * part % parts[0].shape[1]
        rows = rows + dot(
            place_ref[c], parts[c * part // parts[0].shape[1]][:, begin : begin + part]
        )
    return rows.astype(BF16)


def a_near_rows(blocks, up, after):
    half, hidden_units = up.shape[0] // 2, up.shape[1]
    rows = blocks[0][0].shape[0]

    def work(ins, outs):
        for j in range(3):
            hidden = dot(ins[2 * j][...], ins[6][:half]) + dot(ins[2 * j + 1][...], ins[6][half:])
            outs[0][j] = (hidden * jax.nn.sigmoid(hidden)).astype(BF16)

    flat = [half_block for block in blocks for half_block in block]
    return on_core("a_near", work, [((3, rows, hidden_units), BF16)], *flat, up, after)[0]


def a_far_rows(block, act, up, down):
    half, rows = up.shape[0] // 2, act.shape[1]

    def work(ins, outs):
        lo, hi, acts, up_ref, down_ref = ins
        hidden = dot(lo[...], up_ref[:half]) + dot(hi[...], up_ref[half:])
        far = (hidden * jax.nn.sigmoid(hidden)).astype(BF16)
        for h in range(2):
            weights = down_ref[:, h * half : (h + 1) * half]
            outs[h][0] = dot(far, weights).astype(BF16)
            outs[h][1] = dot(acts[1 + h], weights).astype(BF16)
        outs[2][...] = jnp.zeros(TOKEN[0], F32)

    outs = [((2, rows, half), BF16)] * 2 + [TOKEN]
    by_x, by_y, token = on_core("a_far", work, outs, *block, act, up, down)
    return (by_x, by_y), token


def a_second_rows(act, down, got, after):
    half, rows = down.shape[1] // 2, act.shape[1]

    def work(ins, outs):
        acts, down_ref, by_x, by_y = ins[:4]
        outs[0][...] = (dot(acts[1], down_ref[:, half:]) + by_y[0].astype(F32)).astype(BF16)
        outs[1][...] = (dot(acts[2], down_ref[:, :half]) + by_x[0].astype(F32)).astype(BF16)
        outs[2][...] = jnp.zeros(TOKEN[0], F32)

    outs = [((rows, half), BF16)] * 2 + [TOKEN]
    by_x, by_y, token = on_core("a_second", work, outs, act, down, *got, after)
    return (by_x, by_y), token


def a_total_rows(act, down, first, second, place):
    half = down.shape[1] // 2

    def work(ins, outs):
        acts, down_ref, first_x, first_y, second_x, second_y, place_ref = ins
        parts = []
        for h, (one, two) in enumerate(((first_x, second_y), (first_y, second_x))):
            cols = slice(h * half, (h + 1) * half)
            total = dot(acts[0], down_ref[:, cols]) + one[1].astype(F32) + two[...].astype(F32)
            parts.append(total.astype(BF16))
        outs[0][...] = placed(parts, place_ref)
        outs[1][...] = jnp.zeros(TOKEN[0], F32)

    outs = [((place.shape[1], 2 * half // place.shape[0]), BF16), TOKEN]
    return on_core("a_total", work, outs, act, down, *first, *second, place)


def b_hidden_rows(blocks, up, col, after):
    half, units, rows = up.shape[0] // 2, up.shape[1], blocks[0][0].shape[0]

    def work(ins, outs):
        up_ref, col_ref = ins[8:10]
        for j in range(4):
            lo, hi = ins[2 * j][...], ins[2 * j + 1][...]
            outs[0][j] = dot(lo, up_ref[:half]) + dot(hi, up_ref[half:])
            outs[1][j] = dot(lo, col_ref[:half]) + dot(hi, col_ref[half:])

    flat = [v for block in blocks for v in block]
    outs = [((4, rows, units), F32), ((4, rows, 128), F32)]
    return tuple(on_core("b_hidden", work, outs, *flat, up, col, after))


def back_rows(hidden, score, c_lo, c_hi, down_ref):
    half = c_lo.shape[1]
    act_grad = dot(c_lo, down_ref[:half]) + dot(c_hi, down_ref[half:])
    sigma = jax.nn.sigmoid(hidden)
    active = hidden * sigma
    hid_grad = (act_grad * sigma * (1.0 + hidden * (1.0 - sigma))).astype(BF16)
    term = jnp.sum(active * act_grad, axis=1, keepdims=True) * jax.nn.sigmoid(-score[:, :1])
    return active.astype(BF16), hid_grad, term


def grad_rows(hid_grad, term, up_ref, line_ref, cols):
    return dot(hid_grad, up_ref[:, cols]) + term * line_ref[:, cols]


def b_near_rows(cots, early, up, down, line):
    half, units, rows = up.shape[1] // 2, up.shape[0], cots[0][0].shape[0]

    def work(ins, outs):
        hidden, score, up_ref, down_ref, line_ref = ins[6:]
        for j in range(3):
            lo, hi = ins[2 * j][...], ins[2 * j + 1][...]
            act, hid, term = back_rows(hidden[j], score[j], lo, hi, down_ref)
            outs[0][j], outs[1][j] = act, hid
            outs[2][j] = jnp.broadcast_to(term, (rows, 128))
            if j:
                cols = slice((j - 1) * half, j * half)
                outs[2 + j][...] = grad_rows(hid, term, up_ref, line_ref, cols).astype(BF16)

    flat = [v for block in cots for v in block]
    outs = [((3, rows, units), BF16)] * 2 + [((3, rows, 128), F32)]
    outs += [((rows, half), BF16)] * 2
    act, hid, term, by_x, by_y = on_core("b_near", work, outs, *flat, *early, up, down, line)
    return (act, hid, term), (by_x, by_y)


def b_far_rows(cots, early, near, up, down, line):
    half, units, rows = up.shape[1] // 2, up.shape[0], cots[0].shape[0]

    def work(ins, outs):
        lo, hi, hidden, score, _, up_ref, down_ref, line_ref = ins
        act, hid, term = back_rows(hidden[3], score[3], lo[...], hi[...], down_ref)
        outs[0][...], outs[1][...] = act, hid
        for h in range(2):
            part = grad_rows(hid, term, up_ref, line_ref, slice(h * half, (h + 1) * half))
            outs[2 + h][...] = part.astype(BF16)

    outs = [((rows, units), BF16)] * 2 + [((rows, half), BF16)] * 2
    args = (*cots, *early, near[2], up, down, line)
    act, hid, by_x, by_y = on_core("b_far", work, outs, *args)
    return (act, hid), (by_x, by_y)


def b_second_rows(near, up, line, got, plain):
    half, rows = up.shape[1] // 2, got[0].shape[0]

    def work(ins, outs):
        hids, terms, up_ref, line_ref, by_x, by_y = ins[:6]
        for side, ref in enumerate((by_y, by_x)):
            j, cols = 1 + side, slice((1 - side) * half, (2 - side) * half)
            part = grad_rows(hids[j], terms[j][:, :1], up_ref, line_ref, cols)
            outs[side][...] = (part + ref[...].astype(F32)).astype(BF16)

    outs = [((rows, half), BF16)] * 2
    return on_core("b_second", work, outs, near[1], near[2], up, line, *got, *plain)


def b_total_rows(near, up, line, plain, second, place):
    half = up.shape[1] // 2

    def work(ins, outs):
        hids, terms, up_ref, line_ref, plain_x, plain_y, second_x, second_y, place_ref = ins
        parts = []
        for h, (one, two) in enumerate(((plain_x, second_y), (plain_y, second_x))):
            cols = slice(h * half, (h + 1) * half)
            part = grad_rows(hids[0], terms[0][:, :1], up_ref, line_ref, cols)
            parts.append((part + one[...].astype(F32) + two[...].astype(F32)).astype(BF16))
        outs[0][...] = placed(parts, place_ref)
        outs[1][...] = jnp.zeros(TOKEN[0], F32)

    outs = [((place.shape[1], 2 * half // place.shape[0]), BF16), TOKEN]
    return on_core("b_total", work, outs, near[1], near[2], up, line, *plain, *second, place)


def weight_grads(blocks, cots, near, far, after):
    half, units = blocks[0][0].shape[1], far[0].shape[1]
    tile = 256

    def work(ins, outs):
        xs, cs = ins[0:8], ins[8:16]
        acts = [ins[16][j] for j in range(3)] + [ins[18][...]]
        hids = [ins[17][j] for j in range(3)] + [ins[19][...]]
        for h in range(2):
            for begin in range(0, half, tile):
                cols, out = slice(begin, begin + tile), slice(h * half + begin, h * half + begin + tile)
                up_sum, down_sum = 0.0, 0.0
                for j in range(4):
                    up_sum = up_sum + dot(xs[2 * j + h][:, cols], hids[j], TN)
                    down_sum = down_sum + dot(acts[j], cs[2 * j + h][:, cols], TN)
                outs[0][out, :] = up_sum.astype(BF16)
                outs[1][:, out] = down_sum.astype(BF16)

    flat = [v for block in blocks for v in block] + [v for block in cots for v in block]
    outs = [((2 * half, units), BF16), ((units, 2 * half), BF16)]
    return on_core("weight_grads", work, outs, *flat, near[0], near[1], *far, after)


def across_planes(rows, layout):
    blocks = rows.reshape(layout.experts, layout.block, rows.shape[1])
    return depth_exchange(blocks, layout.experts).reshape(rows.shape)


def swap_pair(pair, experts):
    return plane_move(pair[0], experts, 1), plane_move(pair[1], experts, 2)


def spread_halves(mine, experts):
    x_lo, y_hi = swap_pair(mine, experts)
    x_hi, y_lo = swap_pair((mine[1], mine[0]), experts)
    return (x_lo, x_hi), (y_lo, y_hi)


def relay_halves(near, experts):
    return plane_move(near[0][0], experts, 2), plane_move(near[1][1], experts, 1)


def body(a_input, a_route, b_saved, b_grad, b_route, up_weight, down_weight, router):
    devices = lax.axis_size("expert")
    experts = router.shape[2]
    group = devices // experts
    tokens, width = a_input.shape[1], a_input.shape[2]
    layout = Layout(experts, tokens * a_route.shape[2] // experts + 2)
    here = lax.axis_index("expert") // group
    up, down, cols_r = up_weight[0], down_weight[0], router[0]
    b_ids = pipe_move(b_route[0].astype(BF16), lambda i, n: n - 1 - i).astype(jnp.int32)
    b_x = pipe_move(b_saved[0], lambda i, n: n - 1 - i)
    b_c = pipe_move(b_grad[0], lambda i, n: n - 1 - i)
    a_ids = a_route[0]
    own = jnp.where(jnp.arange(experts) == here, cols_r.astype(F32), 0.0)
    own = jnp.sum(own, axis=1, keepdims=True)
    line = own.reshape(1, width)
    col = jnp.where(jnp.arange(128)[None, :] == 0, own, 0.0).astype(BF16)
    place, select = layout.places()
    a_target, b_target = target_rows(a_ids[:, 0], layout), target_rows(b_ids[:, 0], layout)

    a_send, a_gate = send_normed(a_input[0], a_ids, cols_r, a_target, layout)
    a_mine, a_packed = pack_halves(across_planes(a_send, layout), select)
    b_send, b_gate = send_normed(b_x, b_ids, cols_r, b_target, layout, (a_packed,))
    a_near = spread_halves(a_mine, experts)
    a_far = relay_halves(a_near, experts)
    b_blocks = across_planes(b_send, layout)

    act = a_near_rows((a_mine,) + a_near, up, b_gate)
    a_first, a_ready = a_far_rows(a_far, act, up, down)
    a_first = swap_pair(a_first, experts)
    b_mine, b_packed = pack_halves(b_blocks, select, (a_ready,))
    b_near = spread_halves(b_mine, experts)
    b_far = relay_halves(b_near, experts)
    c_send, c_sent = send_cotangents(b_c, b_gate, b_target, layout, (b_packed,))
    c_blocks = across_planes(c_send, layout)

    a_second, a_done = a_second_rows(act, down, a_first, c_sent)
    a_second = swap_pair(a_second, experts)
    c_mine, _ = pack_halves(c_blocks, select, (a_done,))
    c_near = spread_halves(c_mine, experts)
    c_far = relay_halves(c_near, experts)
    a_total, a_summed = a_total_rows(act, down, a_first, a_second, place)
    a_back = across_planes(a_total, layout)
    a_out = forward_out(a_input[0], a_gate, a_back, a_target)
    a_next = pipe_move(a_out, lambda i, n: i + 1)

    up_turned, down_turned = up.T, down.T
    early = b_hidden_rows((b_mine,) + b_near + (b_far,), up, col, a_summed)
    near, b_plain = b_near_rows((c_mine,) + c_near, early, up_turned, down_turned, line)
    b_plain = swap_pair(b_plain, experts)
    far, b_relay = b_far_rows(c_far, early, near, up_turned, down_turned, line)
    b_relay = swap_pair(b_relay, experts)
    b_second = b_second_rows(near, up_turned, line, b_relay, b_plain)
    b_second = swap_pair(b_second, experts)
    b_total, b_done = b_total_rows(near, up_turned, line, b_plain, b_second, place)
    b_out = backward_out(b_x, b_c, across_planes(b_total, layout), b_target)
    b_next = pipe_move(b_out, lambda i, n: n - i)
    up_grad, down_grad = weight_grads(
        (b_mine,) + b_near + (b_far,), (c_mine,) + c_near + (c_far,), near, far, b_done
    )
    return (a_next[None], b_next[None], up_grad[None], down_grad[None])


def solution(mesh):
    return jax.shard_map(
        body,
        mesh=mesh,
        in_specs=(
            P("pipe", "expert", None),
            P("pipe", "expert", None),
            P("pipe", "expert", None),
            P("pipe", "expert", None),
            P("pipe", "expert", None),
            P("pipe", None, "expert"),
            P("pipe", "expert", None),
            P("pipe", None, None),
        ),
        out_specs=(
            P("pipe", "expert", None),
            P("pipe", "expert", None),
            P("pipe", None, "expert"),
            P("pipe", "expert", None),
        ),
        check_vma=False,
    )
```

```python
import jax
import jax.numpy as jnp
import numpy as np
from jax import lax
from jax.experimental import pallas as pl
from jax.experimental.pallas import tpu as pltpu
from jax.sharding import PartitionSpec as P

EPS = 1e-06
F32 = jnp.float32
BF16 = jnp.bfloat16


def dot(a, b, dims=((1,), (0,))):
    return lax.dot_general(a, b, (dims, ((), ())), preferred_element_type=F32)


def pipe_move(array, target):
    count = lax.axis_size("pipe")
    pairs = [(i, target(i, count) % count) for i in range(count)]
    if all(a == b for a, b in pairs):
        return array
    return lax.ppermute(array, "pipe", pairs)


def plane_move(array, experts, bit):
    devices = lax.axis_size("expert")
    return lax.ppermute(array, "expert", [(i, i ^ bit) for i in range(devices)])


def depth_exchange(blocks, experts):
    devices = lax.axis_size("expert")
    group = devices // experts
    columns = [[e * group + m for e in range(experts)] for m in range(group)]
    return lax.all_to_all(
        blocks, "expert", split_axis=0, concat_axis=0, tiled=True, axis_index_groups=columns
    )


class Layout:
    cuts = 4

    def __init__(self, experts, capacity):
        self.experts = experts
        self.slots = capacity
        self.block = self.cuts * capacity
        self.sent = experts * self.block
        self.packed = experts * capacity

    def places(self):
        packed = np.arange(self.packed)
        found = np.zeros((self.cuts, self.sent, self.packed), np.float32)
        for c in range(self.cuts):
            row = packed // self.slots * self.block + c * self.slots + packed % self.slots
            found[c, row, packed] = 1.0
        return jnp.asarray(found, BF16), jnp.asarray(found.transpose(0, 2, 1), BF16)


def target_rows(ids, layout):
    onehot = (ids[:, None] == jnp.arange(layout.experts, dtype=jnp.int32)).astype(jnp.int32)
    slot = jnp.sum(onehot * (jnp.cumsum(onehot, axis=0) - 1), axis=1)
    first = (ids * layout.block + slot)[:, None]
    return first + layout.slots * jnp.arange(layout.cuts, dtype=jnp.int32)[None, :]


def on_core(name, work, outs, *args, after=()):
    first_out = len(args) + len(after)

    def kernel(*refs):
        work(refs[: len(args)], refs[first_out:])

    space = pl.BlockSpec(memory_space=pltpu.VMEM)
    return pl.pallas_call(
        kernel,
        out_shape=[jax.ShapeDtypeStruct(shape, kind) for shape, kind in outs],
        in_specs=[space] * len(args) + [pl.BlockSpec(memory_space=pl.ANY)] * len(after),
        out_specs=[space] * len(outs),
        compiler_params=pltpu.CompilerParams(vmem_limit_bytes=16 * 2**20),
        cost_estimate=pl.CostEstimate(flops=10**6, bytes_accessed=10**5, transcendentals=0),
        name=name,
    )(*args, *after)


NT = ((1,), (1,))
TN = ((0,), (0,))


TOKEN = ((8, 128), F32)


def sent_rows(values, target, sent):
    cuts, tokens = target.shape
    part = values.shape[1] // cuts
    rows = lax.broadcasted_iota(jnp.int32, (sent, tokens), 0)
    total = 0.0
    for c in range(cuts):
        pick = jnp.where(rows == target[c : c + 1, :], 1.0, 0.0).astype(BF16)
        total = total + dot(pick, values[:, c * part : (c + 1) * part])
    return total.astype(BF16)


def token_rows(ref, target):
    tokens, cuts = target.shape
    rows = lax.broadcasted_iota(jnp.int32, (tokens, ref.shape[0]), 1)
    parts = []
    for c in range(cuts):
        pick = jnp.where(rows == target[:, c : c + 1], 1.0, 0.0).astype(BF16)
        parts.append(dot(pick, ref[...]))
    return jnp.concatenate(parts, axis=1)


def send_normed(x, ids, router, target, layout, after=()):
    tokens, width = x.shape

    def work(ins, outs):
        x_ref, ids_ref, router_ref, target_ref = ins[:4]
        feat = x_ref[...].astype(F32)
        scale = lax.rsqrt(jnp.mean(feat * feat, axis=1, keepdims=True) + EPS)
        normed = (feat * scale).astype(BF16)
        outs[0][...] = sent_rows(normed, target_ref[...], layout.sent)
        scores = dot(normed, router_ref[...])
        expert = lax.broadcasted_iota(jnp.int32, scores.shape, 1)
        score = jnp.sum(jnp.where(expert == ids_ref[...], scores, 0.0), axis=1, keepdims=True)
        outs[1][...] = jnp.broadcast_to(jax.nn.sigmoid(score), (tokens, 128))

    outs = [((layout.sent, width // layout.cuts), BF16), ((tokens, 128), F32)]
    return on_core("send_normed", work, outs, x, ids, router, target.T, after=after)


def send_cotangents(cot, gate, target, layout, after=()):
    def work(ins, outs):
        values = (ins[1][:, :1] * ins[0][...].astype(F32)).astype(BF16)
        outs[0][...] = sent_rows(values, ins[2][...], layout.sent)
        outs[1][...] = jnp.zeros(TOKEN[0], F32)

    outs = [((layout.sent, cot.shape[1] // layout.cuts), BF16), TOKEN]
    return on_core("send_cotangents", work, outs, cot, gate, target.T, after=after)


def forward_out(x, gate, back, target):
    def work(ins, outs):
        rows = token_rows(ins[2], ins[3][...])
        outs[0][...] = (ins[0][...].astype(F32) + ins[1][:, :1] * rows).astype(BF16)

    return on_core("forward_out", work, [(x.shape, BF16)], x, gate, back, target)[0]


def backward_out(x, cot, back, target):
    width = x.shape[1]

    def work(ins, outs):
        feat = ins[0][...].astype(F32)
        scale = lax.rsqrt(jnp.mean(feat * feat, axis=1, keepdims=True) + EPS)
        normed_grad = token_rows(ins[2], ins[3][...])
        along = jnp.sum(normed_grad * feat, axis=1, keepdims=True) / width
        feature_grad = scale * normed_grad - feat * (scale * scale * scale) * along
        outs[0][...] = (ins[1][...].astype(F32) + feature_grad).astype(BF16)

    return on_core("backward_out", work, [(x.shape, BF16)], x, cot, back, target)[0]


def pack_halves(blocks, select, after=()):
    cuts, rows, _ = select.shape
    part = blocks.shape[1]
    half = cuts * part // 2

    def work(ins, outs):
        for c in range(cuts):
            begin = c * part % half
            outs[c * part // half][:, begin : begin + part] = dot(ins[1][c], ins[0][...]).astype(
                BF16
            )
        outs[2][...] = jnp.zeros(TOKEN[0], F32)

    lo, hi, token = on_core(
        "pack", work, [((rows, half), BF16)] * 2 + [TOKEN], blocks, select, after=after
    )
    return (lo, hi), token


def placed(parts, place_ref):
    cuts = place_ref.shape[0]
    part = 2 * parts[0].shape[1] // cuts
    rows = 0.0
    for c in range(cuts):
        begin = c * part % parts[0].shape[1]
        rows = rows + dot(
            place_ref[c], parts[c * part // parts[0].shape[1]][:, begin : begin + part]
        )
    return rows.astype(BF16)


def a_near_rows(blocks, up, after):
    half, hidden_units = up.shape[0] // 2, up.shape[1]
    rows = blocks[0][0].shape[0]

    def work(ins, outs):
        for j in range(3):
            hidden = dot(ins[2 * j][...], ins[6][:half]) + dot(ins[2 * j + 1][...], ins[6][half:])
            outs[0][j] = (hidden * jax.nn.sigmoid(hidden)).astype(BF16)

    flat = [half_block for block in blocks for half_block in block]
    return on_core("a_near", work, [((3, rows, hidden_units), BF16)], *flat, up, after=(after,))[0]


def a_far_rows(block, act, up, down):
    half, rows = up.shape[0] // 2, act.shape[1]

    def work(ins, outs):
        lo, hi, acts, up_ref, down_ref = ins
        hidden = dot(lo[...], up_ref[:half]) + dot(hi[...], up_ref[half:])
        far = (hidden * jax.nn.sigmoid(hidden)).astype(BF16)
        for h in range(2):
            weights = down_ref[:, h * half : (h + 1) * half]
            outs[h][0] = dot(far, weights).astype(BF16)
            outs[h][1] = dot(acts[1 + h], weights).astype(BF16)
        outs[2][...] = jnp.zeros(TOKEN[0], F32)

    outs = [((2, rows, half), BF16)] * 2 + [TOKEN]
    by_x, by_y, token = on_core("a_far", work, outs, *block, act, up, down)
    return (by_x, by_y), token


def a_second_rows(act, down, got, after=()):
    half, rows = down.shape[1] // 2, act.shape[1]

    def work(ins, outs):
        acts, down_ref, by_x, by_y = ins
        outs[0][...] = (dot(acts[1], down_ref[:, half:]) + by_y[0].astype(F32)).astype(BF16)
        outs[1][...] = (dot(acts[2], down_ref[:, :half]) + by_x[0].astype(F32)).astype(BF16)
        outs[2][...] = jnp.zeros(TOKEN[0], F32)

    outs = [((rows, half), BF16)] * 2 + [TOKEN]
    by_x, by_y, token = on_core("a_second", work, outs, act, down, *got, after=after)
    return (by_x, by_y), token


def a_total_rows(act, down, first, second, place, after):
    half = down.shape[1] // 2

    def work(ins, outs):
        acts, down_ref, first_x, first_y, second_x, second_y, place_ref = ins
        parts = []
        for h, (one, two) in enumerate(((first_x, second_y), (first_y, second_x))):
            cols = slice(h * half, (h + 1) * half)
            total = dot(acts[0], down_ref[:, cols]) + one[1].astype(F32) + two[...].astype(F32)
            parts.append(total.astype(BF16))
        outs[0][...] = placed(parts, place_ref)
        outs[1][...] = jnp.zeros(TOKEN[0], F32)

    outs = [((place.shape[1], 2 * half // place.shape[0]), BF16), TOKEN]
    return on_core("a_total", work, outs, act, down, *first, *second, place, after=after)


def b_hidden_rows(blocks, up, col):
    half, units, rows = up.shape[0] // 2, up.shape[1], blocks[0][0].shape[0]

    def work(ins, outs):
        up_ref, col_ref = ins[8:]
        for j in range(4):
            lo, hi = ins[2 * j][...], ins[2 * j + 1][...]
            outs[0][j] = dot(lo, up_ref[:half]) + dot(hi, up_ref[half:])
            outs[1][j] = dot(lo, col_ref[:half]) + dot(hi, col_ref[half:])

        outs[2][...] = jnp.zeros(TOKEN[0], F32)

    flat = [v for block in blocks for v in block]
    outs = [((4, rows, units), F32), ((4, rows, 128), F32), TOKEN]
    hidden, score, token = on_core("b_hidden", work, outs, *flat, up, col)
    return (hidden, score), token


def back_rows(hidden, score, c_lo, c_hi, down_ref):
    half = c_lo.shape[1]
    act_grad = dot(c_lo, down_ref[:half]) + dot(c_hi, down_ref[half:])
    sigma = jax.nn.sigmoid(hidden)
    active = hidden * sigma
    hid_grad = (act_grad * sigma * (1.0 + hidden * (1.0 - sigma))).astype(BF16)
    term = jnp.sum(active * act_grad, axis=1, keepdims=True) * jax.nn.sigmoid(-score[:, :1])
    return active.astype(BF16), hid_grad, term


def grad_rows(hid_grad, term, up_ref, line_ref, cols):
    return dot(hid_grad, up_ref[:, cols]) + term * line_ref[:, cols]


def b_near_rows(cots, early, up, down, line, after):
    half, units, rows = up.shape[1] // 2, up.shape[0], cots[0][0].shape[0]

    def work(ins, outs):
        hidden, score, up_ref, down_ref, line_ref = ins[6:]
        for j in range(3):
            lo, hi = ins[2 * j][...], ins[2 * j + 1][...]
            act, hid, term = back_rows(hidden[j], score[j], lo, hi, down_ref)
            outs[0][j], outs[1][j] = act, hid
            outs[2][j] = jnp.broadcast_to(term, (rows, 128))
            if j:
                cols = slice((j - 1) * half, j * half)
                outs[2 + j][...] = grad_rows(hid, term, up_ref, line_ref, cols).astype(BF16)

    flat = [v for block in cots for v in block]
    outs = [((3, rows, units), BF16)] * 2 + [((3, rows, 128), F32)]
    outs += [((rows, half), BF16)] * 2
    act, hid, term, by_x, by_y = on_core("b_near", work, outs, *flat, *early, up, down, line, after=after)
    return (act, hid, term), (by_x, by_y)


def b_far_rows(cots, early, near, up, down, line):
    half, units, rows = up.shape[1] // 2, up.shape[0], cots[0].shape[0]

    def work(ins, outs):
        lo, hi, hidden, score, up_ref, down_ref, line_ref = ins
        act, hid, term = back_rows(hidden[3], score[3], lo[...], hi[...], down_ref)
        outs[0][...], outs[1][...] = act, hid
        for h in range(2):
            part = grad_rows(hid, term, up_ref, line_ref, slice(h * half, (h + 1) * half))
            outs[2 + h][...] = part.astype(BF16)

    outs = [((rows, units), BF16)] * 2 + [((rows, half), BF16)] * 2
    args = (*cots, *early, up, down, line)
    act, hid, by_x, by_y = on_core("b_far", work, outs, *args, after=(near[2],))
    return (act, hid), (by_x, by_y)


def b_second_rows(near, up, line, got, plain):
    half, rows = up.shape[1] // 2, got[0].shape[0]

    def work(ins, outs):
        hids, terms, up_ref, line_ref, by_x, by_y = ins
        for side, ref in enumerate((by_y, by_x)):
            j, cols = 1 + side, slice((1 - side) * half, (2 - side) * half)
            part = grad_rows(hids[j], terms[j][:, :1], up_ref, line_ref, cols)
            outs[side][...] = (part + ref[...].astype(F32)).astype(BF16)

    outs = [((rows, half), BF16)] * 2
    return on_core("b_second", work, outs, near[1], near[2], up, line, *got, after=plain)


def b_total_rows(near, up, line, plain, second, place):
    half = up.shape[1] // 2

    def work(ins, outs):
        hids, terms, up_ref, line_ref, plain_x, plain_y, second_x, second_y, place_ref = ins
        parts = []
        for h, (one, two) in enumerate(((plain_x, second_y), (plain_y, second_x))):
            cols = slice(h * half, (h + 1) * half)
            part = grad_rows(hids[0], terms[0][:, :1], up_ref, line_ref, cols)
            parts.append((part + one[...].astype(F32) + two[...].astype(F32)).astype(BF16))
        outs[0][...] = placed(parts, place_ref)
        outs[1][...] = jnp.zeros(TOKEN[0], F32)

    outs = [((place.shape[1], 2 * half // place.shape[0]), BF16), TOKEN]
    return on_core("b_total", work, outs, near[1], near[2], up, line, *plain, *second, place)


def weight_grads(blocks, cots, near, far, after):
    half, units = blocks[0][0].shape[1], far[0].shape[1]
    tile = 256

    def work(ins, outs):
        xs, cs = ins[0:8], ins[8:16]
        acts = [ins[16][j] for j in range(3)] + [ins[18][...]]
        hids = [ins[17][j] for j in range(3)] + [ins[19][...]]
        for h in range(2):
            for begin in range(0, half, tile):
                cols, out = slice(begin, begin + tile), slice(h * half + begin, h * half + begin + tile)
                up_sum, down_sum = 0.0, 0.0
                for j in range(4):
                    up_sum = up_sum + dot(xs[2 * j + h][:, cols], hids[j], TN)
                    down_sum = down_sum + dot(acts[j], cs[2 * j + h][:, cols], TN)
                outs[0][out, :] = up_sum.astype(BF16)
                outs[1][:, out] = down_sum.astype(BF16)

    flat = [v for block in blocks for v in block] + [v for block in cots for v in block]
    outs = [((2 * half, units), BF16), ((units, 2 * half), BF16)]
    return on_core("weight_grads", work, outs, *flat, near[0], near[1], *far, after=(after,))


def across_planes(rows, layout):
    blocks = rows.reshape(layout.experts, layout.block, rows.shape[1])
    return depth_exchange(blocks, layout.experts).reshape(rows.shape)


def swap_pair(pair, experts):
    return plane_move(pair[0], experts, 1), plane_move(pair[1], experts, 2)


def spread_halves(mine, experts):
    x_lo, y_hi = swap_pair(mine, experts)
    x_hi, y_lo = swap_pair((mine[1], mine[0]), experts)
    return (x_lo, x_hi), (y_lo, y_hi)


def relay_halves(near, experts):
    return plane_move(near[0][0], experts, 2), plane_move(near[1][1], experts, 1)


def body(a_input, a_route, b_saved, b_grad, b_route, up_weight, down_weight, router):
    devices = lax.axis_size("expert")
    experts = router.shape[2]
    group = devices // experts
    tokens, width = a_input.shape[1], a_input.shape[2]
    layout = Layout(experts, tokens * a_route.shape[2] // experts + 2)
    here = lax.axis_index("expert") // group
    up, down, cols_r = up_weight[0], down_weight[0], router[0]
    b_ids = pipe_move(b_route[0].astype(BF16), lambda i, n: n - 1 - i).astype(jnp.int32)
    b_x = pipe_move(b_saved[0], lambda i, n: n - 1 - i)
    b_c = pipe_move(b_grad[0], lambda i, n: n - 1 - i)
    a_ids = a_route[0]
    own = jnp.where(jnp.arange(experts) == here, cols_r.astype(F32), 0.0)
    own = jnp.sum(own, axis=1, keepdims=True)
    line = own.reshape(1, width)
    col = jnp.where(jnp.arange(128)[None, :] == 0, own, 0.0).astype(BF16)
    place, select = layout.places()
    a_target, b_target = target_rows(a_ids[:, 0], layout), target_rows(b_ids[:, 0], layout)

    a_send, a_gate = send_normed(a_input[0], a_ids, cols_r, a_target, layout)
    up_turned, down_turned = up.T, down.T
    a_blocks = across_planes(a_send, layout)
    a_mine, _ = pack_halves(a_blocks, select, (up_turned, down_turned))
    a_near = spread_halves(a_mine, experts)
    a_far = relay_halves(a_near, experts)
    b_send, b_gate = send_normed(b_x, b_ids, cols_r, b_target, layout, (a_near[0][0],))
    b_blocks = across_planes(b_send, layout)

    act = a_near_rows((a_mine,) + a_near, up, b_gate)
    a_first, a_ready = a_far_rows(a_far, act, up, down)
    a_first = swap_pair(a_first, experts)
    b_mine, _ = pack_halves(b_blocks, select, (a_ready,))
    b_near = spread_halves(b_mine, experts)
    b_far = relay_halves(b_near, experts)

    a_second, a_done = a_second_rows(act, down, a_first)
    a_second = swap_pair(a_second, experts)
    c_send, _ = send_cotangents(b_c, b_gate, b_target, layout, (a_done,))
    c_blocks = across_planes(c_send, layout)
    c_mine, _ = pack_halves(c_blocks, select)
    c_near = spread_halves(c_mine, experts)
    c_far = relay_halves(c_near, experts)
    early, b_ready = b_hidden_rows((b_mine,) + b_near + (b_far,), up, col)
    a_total, a_summed = a_total_rows(act, down, a_first, a_second, place, (b_ready,))
    a_back = across_planes(a_total, layout)
    a_out = forward_out(a_input[0], a_gate, a_back, a_target)
    a_next = pipe_move(a_out, lambda i, n: i + 1)

    cots = (c_mine,) + c_near
    near, b_plain = b_near_rows(cots, early, up_turned, down_turned, line, (a_summed,))
    b_plain = swap_pair(b_plain, experts)
    far, b_relay = b_far_rows(c_far, early, near, up_turned, down_turned, line)
    b_relay = swap_pair(b_relay, experts)
    b_second = b_second_rows(near, up_turned, line, b_relay, b_plain)
    b_second = swap_pair(b_second, experts)
    b_total, b_done = b_total_rows(near, up_turned, line, b_plain, b_second, place)
    b_out = backward_out(b_x, b_c, across_planes(b_total, layout), b_target)
    b_next = pipe_move(b_out, lambda i, n: n - i)
    up_grad, down_grad = weight_grads(
        (b_mine,) + b_near + (b_far,), (c_mine,) + c_near + (c_far,), near, far, b_done
    )
    return (a_next[None], b_next[None], up_grad[None], down_grad[None])


def solution(mesh):
    return jax.shard_map(
        body,
        mesh=mesh,
        in_specs=(
            P("pipe", "expert", None),
            P("pipe", "expert", None),
            P("pipe", "expert", None),
            P("pipe", "expert", None),
            P("pipe", "expert", None),
            P("pipe", None, "expert"),
            P("pipe", "expert", None),
            P("pipe", None, None),
        ),
        out_specs=(
            P("pipe", "expert", None),
            P("pipe", "expert", None),
            P("pipe", None, "expert"),
            P("pipe", "expert", None),
        ),
        check_vma=False,
    )
```

```python
import jax
import jax.numpy as jnp
import numpy as np
from jax import lax
from jax.experimental import pallas as pl
from jax.experimental.pallas import tpu as pltpu
from jax.sharding import PartitionSpec as P

EPS = 1e-06
F32 = jnp.float32
BF16 = jnp.bfloat16


def dot(a, b, dims=((1,), (0,))):
    return lax.dot_general(a, b, (dims, ((), ())), preferred_element_type=F32)


def pipe_move(array, target):
    count = lax.axis_size("pipe")
    pairs = [(i, target(i, count) % count) for i in range(count)]
    if all(a == b for a, b in pairs):
        return array
    return lax.ppermute(array, "pipe", pairs)


def plane_move(array, experts, bit):
    devices = lax.axis_size("expert")
    return lax.ppermute(array, "expert", [(i, i ^ bit) for i in range(devices)])


def depth_exchange(blocks, experts):
    devices = lax.axis_size("expert")
    group = devices // experts
    columns = [[e * group + m for e in range(experts)] for m in range(group)]
    return lax.all_to_all(
        blocks, "expert", split_axis=0, concat_axis=0, tiled=True, axis_index_groups=columns
    )


class Layout:
    cuts = 4

    def __init__(self, experts, capacity):
        self.experts = experts
        self.slots = capacity
        self.block = self.cuts * capacity
        self.sent = experts * self.block
        self.packed = experts * capacity

    def places(self):
        packed = np.arange(self.packed)
        found = np.zeros((self.cuts, self.sent, self.packed), np.float32)
        for c in range(self.cuts):
            row = packed // self.slots * self.block + c * self.slots + packed % self.slots
            found[c, row, packed] = 1.0
        return jnp.asarray(found, BF16), jnp.asarray(found.transpose(0, 2, 1), BF16)


def target_rows(ids, layout):
    onehot = (ids[:, None] == jnp.arange(layout.experts, dtype=jnp.int32)).astype(jnp.int32)
    slot = jnp.sum(onehot * (jnp.cumsum(onehot, axis=0) - 1), axis=1)
    first = (ids * layout.block + slot)[:, None]
    return first + layout.slots * jnp.arange(layout.cuts, dtype=jnp.int32)[None, :]


def on_core(name, work, outs, *args, after=()):
    first_out = len(args) + len(after)

    def kernel(*refs):
        work(refs[: len(args)], refs[first_out:])

    space = pl.BlockSpec(memory_space=pltpu.VMEM)
    return pl.pallas_call(
        kernel,
        out_shape=[jax.ShapeDtypeStruct(shape, kind) for shape, kind in outs],
        in_specs=[space] * len(args) + [pl.BlockSpec(memory_space=pl.ANY)] * len(after),
        out_specs=[space] * len(outs),
        compiler_params=pltpu.CompilerParams(vmem_limit_bytes=16 * 2**20),
        cost_estimate=pl.CostEstimate(flops=10**6, bytes_accessed=10**5, transcendentals=0),
        name=name,
    )(*args, *after)


NT = ((1,), (1,))
TN = ((0,), (0,))


TOKEN = ((8, 128), F32)


def sent_rows(values, target, sent):
    cuts, tokens = target.shape
    part = values.shape[1] // cuts
    rows = lax.broadcasted_iota(jnp.int32, (sent, tokens), 0)
    total = 0.0
    for c in range(cuts):
        pick = jnp.where(rows == target[c : c + 1, :], 1.0, 0.0).astype(BF16)
        total = total + dot(pick, values[:, c * part : (c + 1) * part])
    return total.astype(BF16)


def token_rows(ref, target):
    tokens, cuts = target.shape
    rows = lax.broadcasted_iota(jnp.int32, (tokens, ref.shape[0]), 1)
    parts = []
    for c in range(cuts):
        pick = jnp.where(rows == target[:, c : c + 1], 1.0, 0.0).astype(BF16)
        parts.append(dot(pick, ref[...]))
    return jnp.concatenate(parts, axis=1)


def send_normed(x, ids, router, target, layout, after=()):
    tokens, width = x.shape

    def work(ins, outs):
        x_ref, ids_ref, router_ref, target_ref = ins[:4]
        feat = x_ref[...].astype(F32)
        scale = lax.rsqrt(jnp.mean(feat * feat, axis=1, keepdims=True) + EPS)
        normed = (feat * scale).astype(BF16)
        outs[0][...] = sent_rows(normed, target_ref[...], layout.sent)
        scores = dot(normed, router_ref[...])
        expert = lax.broadcasted_iota(jnp.int32, scores.shape, 1)
        score = jnp.sum(jnp.where(expert == ids_ref[...], scores, 0.0), axis=1, keepdims=True)
        outs[1][...] = jnp.broadcast_to(jax.nn.sigmoid(score), (tokens, 128))

    outs = [((layout.sent, width // layout.cuts), BF16), ((tokens, 128), F32)]
    return on_core("send_normed", work, outs, x, ids, router, target.T, after=after)


def send_cotangents(cot, gate, target, layout, after=()):
    def work(ins, outs):
        values = (ins[1][:, :1] * ins[0][...].astype(F32)).astype(BF16)
        outs[0][...] = sent_rows(values, ins[2][...], layout.sent)
        outs[1][...] = jnp.zeros(TOKEN[0], F32)

    outs = [((layout.sent, cot.shape[1] // layout.cuts), BF16), TOKEN]
    return on_core("send_cotangents", work, outs, cot, gate, target.T, after=after)


def forward_out(x, gate, back, target):
    def work(ins, outs):
        rows = token_rows(ins[2], ins[3][...])
        outs[0][...] = (ins[0][...].astype(F32) + ins[1][:, :1] * rows).astype(BF16)

    return on_core("forward_out", work, [(x.shape, BF16)], x, gate, back, target)[0]


def backward_out(x, cot, back, target):
    width = x.shape[1]

    def work(ins, outs):
        feat = ins[0][...].astype(F32)
        scale = lax.rsqrt(jnp.mean(feat * feat, axis=1, keepdims=True) + EPS)
        normed_grad = token_rows(ins[2], ins[3][...])
        along = jnp.sum(normed_grad * feat, axis=1, keepdims=True) / width
        feature_grad = scale * normed_grad - feat * (scale * scale * scale) * along
        outs[0][...] = (ins[1][...].astype(F32) + feature_grad).astype(BF16)

    return on_core("backward_out", work, [(x.shape, BF16)], x, cot, back, target)[0]


def pack_halves(blocks, select, after=()):
    cuts, rows, _ = select.shape
    part = blocks.shape[1]
    half = cuts * part // 2

    def work(ins, outs):
        for c in range(cuts):
            begin = c * part % half
            outs[c * part // half][:, begin : begin + part] = dot(ins[1][c], ins[0][...]).astype(
                BF16
            )
        outs[2][...] = jnp.zeros(TOKEN[0], F32)

    lo, hi, token = on_core(
        "pack", work, [((rows, half), BF16)] * 2 + [TOKEN], blocks, select, after=after
    )
    return (lo, hi), token


def placed(parts, place_ref):
    cuts = place_ref.shape[0]
    part = 2 * parts[0].shape[1] // cuts
    rows = 0.0
    for c in range(cuts):
        begin = c * part % parts[0].shape[1]
        rows = rows + dot(
            place_ref[c], parts[c * part // parts[0].shape[1]][:, begin : begin + part]
        )
    return rows.astype(BF16)


def a_near_rows(blocks, up, after):
    half, hidden_units = up.shape[0] // 2, up.shape[1]
    rows = blocks[0][0].shape[0]

    def work(ins, outs):
        for j in range(3):
            hidden = dot(ins[2 * j][...], ins[6][:half]) + dot(ins[2 * j + 1][...], ins[6][half:])
            outs[0][j] = (hidden * jax.nn.sigmoid(hidden)).astype(BF16)

    flat = [half_block for block in blocks for half_block in block]
    return on_core("a_near", work, [((3, rows, hidden_units), BF16)], *flat, up, after=(after,))[0]


def a_far_rows(block, act, up, down):
    half, rows = up.shape[0] // 2, act.shape[1]

    def work(ins, outs):
        lo, hi, acts, up_ref, down_ref = ins
        hidden = dot(lo[...], up_ref[:half]) + dot(hi[...], up_ref[half:])
        far = (hidden * jax.nn.sigmoid(hidden)).astype(BF16)
        for h in range(2):
            weights = down_ref[:, h * half : (h + 1) * half]
            outs[h][0] = dot(far, weights).astype(BF16)
            outs[h][1] = dot(acts[1 + h], weights).astype(BF16)
        outs[2][...] = jnp.zeros(TOKEN[0], F32)

    outs = [((2, rows, half), BF16)] * 2 + [TOKEN]
    by_x, by_y, token = on_core("a_far", work, outs, *block, act, up, down)
    return (by_x, by_y), token


def a_second_rows(act, down, got, after=()):
    half, rows = down.shape[1] // 2, act.shape[1]

    def work(ins, outs):
        acts, down_ref, by_x, by_y = ins
        outs[0][...] = (dot(acts[1], down_ref[:, half:]) + by_y[0].astype(F32)).astype(BF16)
        outs[1][...] = (dot(acts[2], down_ref[:, :half]) + by_x[0].astype(F32)).astype(BF16)
        outs[2][...] = jnp.zeros(TOKEN[0], F32)

    outs = [((rows, half), BF16)] * 2 + [TOKEN]
    by_x, by_y, token = on_core("a_second", work, outs, act, down, *got, after=after)
    return (by_x, by_y), token


def a_total_rows(act, down, first, second, place, after):
    half = down.shape[1] // 2

    def work(ins, outs):
        acts, down_ref, first_x, first_y, second_x, second_y, place_ref = ins
        parts = []
        for h, (one, two) in enumerate(((first_x, second_y), (first_y, second_x))):
            cols = slice(h * half, (h + 1) * half)
            total = dot(acts[0], down_ref[:, cols]) + one[1].astype(F32) + two[...].astype(F32)
            parts.append(total.astype(BF16))
        outs[0][...] = placed(parts, place_ref)
        outs[1][...] = jnp.zeros(TOKEN[0], F32)

    outs = [((place.shape[1], 2 * half // place.shape[0]), BF16), TOKEN]
    return on_core("a_total", work, outs, act, down, *first, *second, place, after=after)


def b_hidden_rows(blocks, up, col):
    half, units, rows = up.shape[0] // 2, up.shape[1], blocks[0][0].shape[0]

    def work(ins, outs):
        up_ref, col_ref = ins[8:]
        for j in range(4):
            lo, hi = ins[2 * j][...], ins[2 * j + 1][...]
            outs[0][j] = dot(lo, up_ref[:half]) + dot(hi, up_ref[half:])
            outs[1][j] = dot(lo, col_ref[:half]) + dot(hi, col_ref[half:])

        outs[2][...] = jnp.zeros(TOKEN[0], F32)

    flat = [v for block in blocks for v in block]
    outs = [((4, rows, units), F32), ((4, rows, 128), F32), TOKEN]
    hidden, score, token = on_core("b_hidden", work, outs, *flat, up, col)
    return (hidden, score), token


def back_rows(hidden, score, c_lo, c_hi, down_ref):
    half = c_lo.shape[1]
    act_grad = dot(c_lo, down_ref[:half]) + dot(c_hi, down_ref[half:])
    sigma = jax.nn.sigmoid(hidden)
    active = hidden * sigma
    hid_grad = (act_grad * sigma * (1.0 + hidden * (1.0 - sigma))).astype(BF16)
    term = jnp.sum(active * act_grad, axis=1, keepdims=True) * jax.nn.sigmoid(-score[:, :1])
    return active.astype(BF16), hid_grad, term


def grad_rows(hid_grad, term, up_ref, line_ref, cols):
    return dot(hid_grad, up_ref[:, cols]) + term * line_ref[:, cols]


def b_near_rows(cots, early, up, down, line):
    half, units, rows = up.shape[1] // 2, up.shape[0], cots[0][0].shape[0]

    def work(ins, outs):
        hidden, score, up_ref, down_ref, line_ref = ins[6:]
        for j in range(3):
            lo, hi = ins[2 * j][...], ins[2 * j + 1][...]
            act, hid, term = back_rows(hidden[j], score[j], lo, hi, down_ref)
            outs[0][j], outs[1][j] = act, hid
            outs[2][j] = jnp.broadcast_to(term, (rows, 128))
            if j:
                cols = slice((j - 1) * half, j * half)
                outs[2 + j][...] = grad_rows(hid, term, up_ref, line_ref, cols).astype(BF16)

    flat = [v for block in cots for v in block]
    outs = [((3, rows, units), BF16)] * 2 + [((3, rows, 128), F32)]
    outs += [((rows, half), BF16)] * 2
    act, hid, term, by_x, by_y = on_core("b_near", work, outs, *flat, *early, up, down, line)
    return (act, hid, term), (by_x, by_y)


def b_far_rows(cots, early, up, down, line, after):
    half, units, rows = up.shape[1] // 2, up.shape[0], cots[0].shape[0]

    def work(ins, outs):
        lo, hi, hidden, score, up_ref, down_ref, line_ref = ins
        act, hid, term = back_rows(hidden[3], score[3], lo[...], hi[...], down_ref)
        outs[0][...], outs[1][...] = act, hid
        for h in range(2):
            part = grad_rows(hid, term, up_ref, line_ref, slice(h * half, (h + 1) * half))
            outs[2 + h][...] = part.astype(BF16)

    outs = [((rows, units), BF16)] * 2 + [((rows, half), BF16)] * 2
    args = (*cots, *early, up, down, line)
    act, hid, by_x, by_y = on_core("b_far", work, outs, *args, after=after)
    return (act, hid), (by_x, by_y)


def b_second_rows(near, up, line, got, plain):
    half, rows = up.shape[1] // 2, got[0].shape[0]

    def work(ins, outs):
        hids, terms, up_ref, line_ref, by_x, by_y = ins
        for side, ref in enumerate((by_y, by_x)):
            j, cols = 1 + side, slice((1 - side) * half, (2 - side) * half)
            part = grad_rows(hids[j], terms[j][:, :1], up_ref, line_ref, cols)
            outs[side][...] = (part + ref[...].astype(F32)).astype(BF16)

    outs = [((rows, half), BF16)] * 2
    return on_core("b_second", work, outs, near[1], near[2], up, line, *got, after=plain)


def b_total_rows(near, up, line, plain, second, place):
    half = up.shape[1] // 2

    def work(ins, outs):
        hids, terms, up_ref, line_ref, plain_x, plain_y, second_x, second_y, place_ref = ins
        parts = []
        for h, (one, two) in enumerate(((plain_x, second_y), (plain_y, second_x))):
            cols = slice(h * half, (h + 1) * half)
            part = grad_rows(hids[0], terms[0][:, :1], up_ref, line_ref, cols)
            parts.append((part + one[...].astype(F32) + two[...].astype(F32)).astype(BF16))
        outs[0][...] = placed(parts, place_ref)
        outs[1][...] = jnp.zeros(TOKEN[0], F32)

    outs = [((place.shape[1], 2 * half // place.shape[0]), BF16), TOKEN]
    return on_core("b_total", work, outs, near[1], near[2], up, line, *plain, *second, place)


def weight_grads(blocks, cots, near, far, after):
    half, units = blocks[0][0].shape[1], far[0].shape[1]
    tile = 256

    def work(ins, outs):
        xs, cs = ins[0:8], ins[8:16]
        acts = [ins[16][j] for j in range(3)] + [ins[18][...]]
        hids = [ins[17][j] for j in range(3)] + [ins[19][...]]
        for h in range(2):
            for begin in range(0, half, tile):
                cols, out = slice(begin, begin + tile), slice(h * half + begin, h * half + begin + tile)
                up_sum, down_sum = 0.0, 0.0
                for j in range(4):
                    up_sum = up_sum + dot(xs[2 * j + h][:, cols], hids[j], TN)
                    down_sum = down_sum + dot(acts[j], cs[2 * j + h][:, cols], TN)
                outs[0][out, :] = up_sum.astype(BF16)
                outs[1][:, out] = down_sum.astype(BF16)

    flat = [v for block in blocks for v in block] + [v for block in cots for v in block]
    outs = [((2 * half, units), BF16), ((units, 2 * half), BF16)]
    return on_core("weight_grads", work, outs, *flat, near[0], near[1], *far, after=(after,))


def across_planes(rows, layout):
    blocks = rows.reshape(layout.experts, layout.block, rows.shape[1])
    return depth_exchange(blocks, layout.experts).reshape(rows.shape)


def swap_pair(pair, experts):
    return plane_move(pair[0], experts, 1), plane_move(pair[1], experts, 2)


def spread_halves(mine, experts):
    x_lo, y_hi = swap_pair(mine, experts)
    x_hi, y_lo = swap_pair((mine[1], mine[0]), experts)
    return (x_lo, x_hi), (y_lo, y_hi)


def relay_halves(near, experts):
    return plane_move(near[0][0], experts, 2), plane_move(near[1][1], experts, 1)


def body(a_input, a_route, b_saved, b_grad, b_route, up_weight, down_weight, router):
    devices = lax.axis_size("expert")
    experts = router.shape[2]
    group = devices // experts
    tokens, width = a_input.shape[1], a_input.shape[2]
    layout = Layout(experts, tokens * a_route.shape[2] // experts + 2)
    here = lax.axis_index("expert") // group
    up, down, cols_r = up_weight[0], down_weight[0], router[0]
    b_ids = pipe_move(b_route[0].astype(BF16), lambda i, n: n - 1 - i).astype(jnp.int32)
    b_x = pipe_move(b_saved[0], lambda i, n: n - 1 - i)
    b_c = pipe_move(b_grad[0], lambda i, n: n - 1 - i)
    a_ids = a_route[0]
    own = jnp.where(jnp.arange(experts) == here, cols_r.astype(F32), 0.0)
    own = jnp.sum(own, axis=1, keepdims=True)
    line = own.reshape(1, width)
    col = jnp.where(jnp.arange(128)[None, :] == 0, own, 0.0).astype(BF16)
    place, select = layout.places()
    a_target, b_target = target_rows(a_ids[:, 0], layout), target_rows(b_ids[:, 0], layout)

    a_send, a_gate = send_normed(a_input[0], a_ids, cols_r, a_target, layout)
    up_turned, down_turned = up.T, down.T
    a_blocks = across_planes(a_send, layout)
    a_mine, _ = pack_halves(a_blocks, select, (up_turned, down_turned))
    a_near = spread_halves(a_mine, experts)
    a_far = relay_halves(a_near, experts)
    b_send, b_gate = send_normed(b_x, b_ids, cols_r, b_target, layout, (a_near[0][0],))
    b_blocks = across_planes(b_send, layout)

    act = a_near_rows((a_mine,) + a_near, up, b_gate)
    a_first, a_ready = a_far_rows(a_far, act, up, down)
    a_first = swap_pair(a_first, experts)
    b_mine, _ = pack_halves(b_blocks, select, (a_ready,))
    b_near = spread_halves(b_mine, experts)
    b_far = relay_halves(b_near, experts)

    a_second, _ = a_second_rows(act, down, a_first)
    a_second = swap_pair(a_second, experts)
    c_send, _ = send_cotangents(b_c, b_gate, b_target, layout, (b_near[0][0],))
    c_blocks = across_planes(c_send, layout)
    c_mine, _ = pack_halves(c_blocks, select)
    c_near = spread_halves(c_mine, experts)
    c_far = relay_halves(c_near, experts)
    early, b_ready = b_hidden_rows((b_mine,) + b_near + (b_far,), up, col)
    a_total, a_summed = a_total_rows(act, down, a_first, a_second, place, (b_ready,))
    a_back = across_planes(a_total, layout)
    a_out = forward_out(a_input[0], a_gate, a_back, a_target)
    a_next = pipe_move(a_out, lambda i, n: i + 1)

    cots = (c_mine,) + c_near
    near, b_plain = b_near_rows(cots, early, up_turned, down_turned, line)
    b_plain = swap_pair(b_plain, experts)
    far, b_relay = b_far_rows(c_far, early, up_turned, down_turned, line, (near[2], a_summed))
    b_relay = swap_pair(b_relay, experts)
    b_second = b_second_rows(near, up_turned, line, b_relay, b_plain)
    b_second = swap_pair(b_second, experts)
    b_total, b_done = b_total_rows(near, up_turned, line, b_plain, b_second, place)
    b_out = backward_out(b_x, b_c, across_planes(b_total, layout), b_target)
    b_next = pipe_move(b_out, lambda i, n: n - i)
    up_grad, down_grad = weight_grads(
        (b_mine,) + b_near + (b_far,), (c_mine,) + c_near + (c_far,), near, far, b_done
    )
    return (a_next[None], b_next[None], up_grad[None], down_grad[None])


def solution(mesh):
    return jax.shard_map(
        body,
        mesh=mesh,
        in_specs=(
            P("pipe", "expert", None),
            P("pipe", "expert", None),
            P("pipe", "expert", None),
            P("pipe", "expert", None),
            P("pipe", "expert", None),
            P("pipe", None, "expert"),
            P("pipe", "expert", None),
            P("pipe", None, None),
        ),
        out_specs=(
            P("pipe", "expert", None),
            P("pipe", "expert", None),
            P("pipe", None, "expert"),
            P("pipe", "expert", None),
        ),
        check_vma=False,
    )
```

```python
import jax
import jax.numpy as jnp
import numpy as np
from jax import lax
from jax.experimental import pallas as pl
from jax.experimental.pallas import tpu as pltpu
from jax.sharding import PartitionSpec as P

EPS = 1e-06
F32 = jnp.float32
BF16 = jnp.bfloat16


def dot(a, b, dims=((1,), (0,))):
    return lax.dot_general(a, b, (dims, ((), ())), preferred_element_type=F32)


def pipe_move(array, target):
    count = lax.axis_size("pipe")
    pairs = [(i, target(i, count) % count) for i in range(count)]
    if all(a == b for a, b in pairs):
        return array
    return lax.ppermute(array, "pipe", pairs)


def plane_move(array, experts, bit):
    devices = lax.axis_size("expert")
    return lax.ppermute(array, "expert", [(i, i ^ bit) for i in range(devices)])


def depth_exchange(blocks, experts):
    devices = lax.axis_size("expert")
    group = devices // experts
    columns = [[e * group + m for e in range(experts)] for m in range(group)]
    return lax.all_to_all(
        blocks, "expert", split_axis=0, concat_axis=0, tiled=True, axis_index_groups=columns
    )


class Layout:
    cuts = 4

    def __init__(self, experts, capacity):
        self.experts = experts
        self.slots = capacity
        self.block = self.cuts * capacity
        self.sent = experts * self.block
        self.packed = experts * capacity

    def places(self):
        packed = np.arange(self.packed)
        found = np.zeros((self.cuts, self.sent, self.packed), np.float32)
        for c in range(self.cuts):
            row = packed // self.slots * self.block + c * self.slots + packed % self.slots
            found[c, row, packed] = 1.0
        return jnp.asarray(found, BF16), jnp.asarray(found.transpose(0, 2, 1), BF16)


def target_rows(ids, layout):
    onehot = (ids[:, None] == jnp.arange(layout.experts, dtype=jnp.int32)).astype(jnp.int32)
    slot = jnp.sum(onehot * (jnp.cumsum(onehot, axis=0) - 1), axis=1)
    first = (ids * layout.block + slot)[:, None]
    return first + layout.slots * jnp.arange(layout.cuts, dtype=jnp.int32)[None, :]


def on_core(name, work, outs, *args, after=()):
    first_out = len(args) + len(after)

    def kernel(*refs):
        work(refs[: len(args)], refs[first_out:])

    space = pl.BlockSpec(memory_space=pltpu.VMEM)
    return pl.pallas_call(
        kernel,
        out_shape=[jax.ShapeDtypeStruct(shape, kind) for shape, kind in outs],
        in_specs=[space] * len(args) + [pl.BlockSpec(memory_space=pl.ANY)] * len(after),
        out_specs=[space] * len(outs),
        compiler_params=pltpu.CompilerParams(vmem_limit_bytes=16 * 2**20),
        cost_estimate=pl.CostEstimate(flops=10**6, bytes_accessed=10**5, transcendentals=0),
        name=name,
    )(*args, *after)


NT = ((1,), (1,))
TN = ((0,), (0,))


TOKEN = ((8, 128), F32)


def sent_rows(values, target, sent):
    cuts, tokens = target.shape
    part = values.shape[1] // cuts
    rows = lax.broadcasted_iota(jnp.int32, (sent, tokens), 0)
    total = 0.0
    for c in range(cuts):
        pick = jnp.where(rows == target[c : c + 1, :], 1.0, 0.0).astype(BF16)
        total = total + dot(pick, values[:, c * part : (c + 1) * part])
    return total.astype(BF16)


def token_rows(ref, target):
    tokens, cuts = target.shape
    rows = lax.broadcasted_iota(jnp.int32, (tokens, ref.shape[0]), 1)
    parts = []
    for c in range(cuts):
        pick = jnp.where(rows == target[:, c : c + 1], 1.0, 0.0).astype(BF16)
        parts.append(dot(pick, ref[...]))
    return jnp.concatenate(parts, axis=1)


def send_normed(x, ids, router, target, layout, after=()):
    tokens, width = x.shape

    def work(ins, outs):
        x_ref, ids_ref, router_ref, target_ref = ins[:4]
        feat = x_ref[...].astype(F32)
        scale = lax.rsqrt(jnp.mean(feat * feat, axis=1, keepdims=True) + EPS)
        normed = (feat * scale).astype(BF16)
        outs[0][...] = sent_rows(normed, target_ref[...], layout.sent)
        scores = dot(normed, router_ref[...])
        expert = lax.broadcasted_iota(jnp.int32, scores.shape, 1)
        score = jnp.sum(jnp.where(expert == ids_ref[...], scores, 0.0), axis=1, keepdims=True)
        outs[1][...] = jnp.broadcast_to(jax.nn.sigmoid(score), (tokens, 128))

    outs = [((layout.sent, width // layout.cuts), BF16), ((tokens, 128), F32)]
    return on_core("send_normed", work, outs, x, ids, router, target.T, after=after)


def send_cotangents(cot, gate, target, layout, after=()):
    def work(ins, outs):
        values = (ins[1][:, :1] * ins[0][...].astype(F32)).astype(BF16)
        outs[0][...] = sent_rows(values, ins[2][...], layout.sent)
        outs[1][...] = jnp.zeros(TOKEN[0], F32)

    outs = [((layout.sent, cot.shape[1] // layout.cuts), BF16), TOKEN]
    return on_core("send_cotangents", work, outs, cot, gate, target.T, after=after)


def forward_out(x, gate, back, target):
    def work(ins, outs):
        rows = token_rows(ins[2], ins[3][...])
        outs[0][...] = (ins[0][...].astype(F32) + ins[1][:, :1] * rows).astype(BF16)

    return on_core("forward_out", work, [(x.shape, BF16)], x, gate, back, target)[0]


def backward_out(x, cot, back, target):
    width = x.shape[1]

    def work(ins, outs):
        feat = ins[0][...].astype(F32)
        scale = lax.rsqrt(jnp.mean(feat * feat, axis=1, keepdims=True) + EPS)
        normed_grad = token_rows(ins[2], ins[3][...])
        along = jnp.sum(normed_grad * feat, axis=1, keepdims=True) / width
        feature_grad = scale * normed_grad - feat * (scale * scale * scale) * along
        outs[0][...] = (ins[1][...].astype(F32) + feature_grad).astype(BF16)

    return on_core("backward_out", work, [(x.shape, BF16)], x, cot, back, target)[0]


def pack_halves(blocks, select, after=()):
    cuts, rows, _ = select.shape
    part = blocks.shape[1]
    half = cuts * part // 2

    def work(ins, outs):
        for c in range(cuts):
            begin = c * part % half
            outs[c * part // half][:, begin : begin + part] = dot(ins[1][c], ins[0][...]).astype(
                BF16
            )
        outs[2][...] = jnp.zeros(TOKEN[0], F32)

    lo, hi, token = on_core(
        "pack", work, [((rows, half), BF16)] * 2 + [TOKEN], blocks, select, after=after
    )
    return (lo, hi), token


def placed(parts, place_ref):
    cuts = place_ref.shape[0]
    part = 2 * parts[0].shape[1] // cuts
    rows = 0.0
    for c in range(cuts):
        begin = c * part % parts[0].shape[1]
        rows = rows + dot(
            place_ref[c], parts[c * part // parts[0].shape[1]][:, begin : begin + part]
        )
    return rows.astype(BF16)


def a_near_rows(blocks, up, after):
    half, hidden_units = up.shape[0] // 2, up.shape[1]
    rows = blocks[0][0].shape[0]

    def work(ins, outs):
        for j in range(3):
            hidden = dot(ins[2 * j][...], ins[6][:half]) + dot(ins[2 * j + 1][...], ins[6][half:])
            outs[0][j] = (hidden * jax.nn.sigmoid(hidden)).astype(BF16)

    flat = [half_block for block in blocks for half_block in block]
    return on_core("a_near", work, [((3, rows, hidden_units), BF16)], *flat, up, after=(after,))[0]


def a_far_rows(block, act, up, down):
    half, rows = up.shape[0] // 2, act.shape[1]

    def work(ins, outs):
        lo, hi, acts, up_ref, down_ref = ins
        hidden = dot(lo[...], up_ref[:half]) + dot(hi[...], up_ref[half:])
        far = (hidden * jax.nn.sigmoid(hidden)).astype(BF16)
        for h in range(2):
            weights = down_ref[:, h * half : (h + 1) * half]
            outs[h][0] = dot(far, weights).astype(BF16)
            outs[h][1] = dot(acts[1 + h], weights).astype(BF16)
        outs[2][...] = jnp.zeros(TOKEN[0], F32)

    outs = [((2, rows, half), BF16)] * 2 + [TOKEN]
    by_x, by_y, token = on_core("a_far", work, outs, *block, act, up, down)
    return (by_x, by_y), token


def a_second_rows(act, down, got, after=()):
    half, rows = down.shape[1] // 2, act.shape[1]

    def work(ins, outs):
        acts, down_ref, by_x, by_y = ins
        outs[0][...] = (dot(acts[1], down_ref[:, half:]) + by_y[0].astype(F32)).astype(BF16)
        outs[1][...] = (dot(acts[2], down_ref[:, :half]) + by_x[0].astype(F32)).astype(BF16)
        outs[2][...] = jnp.zeros(TOKEN[0], F32)

    outs = [((rows, half), BF16)] * 2 + [TOKEN]
    by_x, by_y, token = on_core("a_second", work, outs, act, down, *got, after=after)
    return (by_x, by_y), token


def a_total_rows(act, down, first, second, place, after):
    half = down.shape[1] // 2

    def work(ins, outs):
        acts, down_ref, first_x, first_y, second_x, second_y, place_ref = ins
        parts = []
        for h, (one, two) in enumerate(((first_x, second_y), (first_y, second_x))):
            cols = slice(h * half, (h + 1) * half)
            total = dot(acts[0], down_ref[:, cols]) + one[1].astype(F32) + two[...].astype(F32)
            parts.append(total.astype(BF16))
        outs[0][...] = placed(parts, place_ref)
        outs[1][...] = jnp.zeros(TOKEN[0], F32)

    outs = [((place.shape[1], 2 * half // place.shape[0]), BF16), TOKEN]
    return on_core("a_total", work, outs, act, down, *first, *second, place, after=after)


def b_hidden_rows(blocks, up, col):
    half, units, rows = up.shape[0] // 2, up.shape[1], blocks[0][0].shape[0]

    def work(ins, outs):
        up_ref, col_ref = ins[8:]
        for j in range(4):
            lo, hi = ins[2 * j][...], ins[2 * j + 1][...]
            outs[0][j] = dot(lo, up_ref[:half]) + dot(hi, up_ref[half:])
            outs[1][j] = dot(lo, col_ref[:half]) + dot(hi, col_ref[half:])

        outs[2][...] = jnp.zeros(TOKEN[0], F32)

    flat = [v for block in blocks for v in block]
    outs = [((4, rows, units), F32), ((4, rows, 128), F32), TOKEN]
    hidden, score, token = on_core("b_hidden", work, outs, *flat, up, col)
    return (hidden, score), token


def back_rows(hidden, score, c_lo, c_hi, down_ref):
    half = c_lo.shape[1]
    act_grad = dot(c_lo, down_ref[:half]) + dot(c_hi, down_ref[half:])
    sigma = jax.nn.sigmoid(hidden)
    active = hidden * sigma
    hid_grad = (act_grad * sigma * (1.0 + hidden * (1.0 - sigma))).astype(BF16)
    term = jnp.sum(active * act_grad, axis=1, keepdims=True) * jax.nn.sigmoid(-score[:, :1])
    return active.astype(BF16), hid_grad, term


def grad_rows(hid_grad, term, up_ref, line_ref, cols):
    return dot(hid_grad, up_ref[:, cols]) + term * line_ref[:, cols]


def b_near_rows(cots, early, up, down, line, after):
    half, units, rows = up.shape[1] // 2, up.shape[0], cots[0][0].shape[0]

    def work(ins, outs):
        hidden, score, up_ref, down_ref, line_ref = ins[6:]
        for j in range(3):
            lo, hi = ins[2 * j][...], ins[2 * j + 1][...]
            act, hid, term = back_rows(hidden[j], score[j], lo, hi, down_ref)
            outs[0][j], outs[1][j] = act, hid
            outs[2][j] = jnp.broadcast_to(term, (rows, 128))
            if j:
                cols = slice((j - 1) * half, j * half)
                outs[2 + j][...] = grad_rows(hid, term, up_ref, line_ref, cols).astype(BF16)

    flat = [v for block in cots for v in block]
    outs = [((3, rows, units), BF16)] * 2 + [((3, rows, 128), F32)]
    outs += [((rows, half), BF16)] * 2
    act, hid, term, by_x, by_y = on_core("b_near", work, outs, *flat, *early, up, down, line, after=after)
    return (act, hid, term), (by_x, by_y)


def b_far_rows(cots, early, near, up, down, line):
    half, units, rows = up.shape[1] // 2, up.shape[0], cots[0].shape[0]

    def work(ins, outs):
        lo, hi, hidden, score, up_ref, down_ref, line_ref = ins
        act, hid, term = back_rows(hidden[3], score[3], lo[...], hi[...], down_ref)
        outs[0][...], outs[1][...] = act, hid
        for h in range(2):
            part = grad_rows(hid, term, up_ref, line_ref, slice(h * half, (h + 1) * half))
            outs[2 + h][...] = part.astype(BF16)

    outs = [((rows, units), BF16)] * 2 + [((rows, half), BF16)] * 2
    args = (*cots, *early, up, down, line)
    act, hid, by_x, by_y = on_core("b_far", work, outs, *args, after=(near[2],))
    return (act, hid), (by_x, by_y)


def b_second_rows(near, up, line, got, plain):
    half, rows = up.shape[1] // 2, got[0].shape[0]

    def work(ins, outs):
        hids, terms, up_ref, line_ref, by_x, by_y = ins
        for side, ref in enumerate((by_y, by_x)):
            j, cols = 1 + side, slice((1 - side) * half, (2 - side) * half)
            part = grad_rows(hids[j], terms[j][:, :1], up_ref, line_ref, cols)
            outs[side][...] = (part + ref[...].astype(F32)).astype(BF16)

    outs = [((rows, half), BF16)] * 2
    return on_core("b_second", work, outs, near[1], near[2], up, line, *got, after=plain)


def b_total_rows(near, up, line, plain, second, place):
    half = up.shape[1] // 2

    def work(ins, outs):
        hids, terms, up_ref, line_ref, plain_x, plain_y, second_x, second_y, place_ref = ins
        parts = []
        for h, (one, two) in enumerate(((plain_x, second_y), (plain_y, second_x))):
            cols = slice(h * half, (h + 1) * half)
            part = grad_rows(hids[0], terms[0][:, :1], up_ref, line_ref, cols)
            parts.append((part + one[...].astype(F32) + two[...].astype(F32)).astype(BF16))
        outs[0][...] = placed(parts, place_ref)
        outs[1][...] = jnp.zeros(TOKEN[0], F32)

    outs = [((place.shape[1], 2 * half // place.shape[0]), BF16), TOKEN]
    return on_core("b_total", work, outs, near[1], near[2], up, line, *plain, *second, place)


def weight_grads(blocks, cots, near, far, after):
    half, units = blocks[0][0].shape[1], far[0].shape[1]
    tile = 256

    def work(ins, outs):
        xs, cs = ins[0:8], ins[8:16]
        acts = [ins[16][j] for j in range(3)] + [ins[18][...]]
        hids = [ins[17][j] for j in range(3)] + [ins[19][...]]
        for h in range(2):
            for begin in range(0, half, tile):
                cols, out = slice(begin, begin + tile), slice(h * half + begin, h * half + begin + tile)
                up_sum, down_sum = 0.0, 0.0
                for j in range(4):
                    up_sum = up_sum + dot(xs[2 * j + h][:, cols], hids[j], TN)
                    down_sum = down_sum + dot(acts[j], cs[2 * j + h][:, cols], TN)
                outs[0][out, :] = up_sum.astype(BF16)
                outs[1][:, out] = down_sum.astype(BF16)

    flat = [v for block in blocks for v in block] + [v for block in cots for v in block]
    outs = [((2 * half, units), BF16), ((units, 2 * half), BF16)]
    return on_core("weight_grads", work, outs, *flat, near[0], near[1], *far, after=(after,))


def across_planes(rows, layout):
    blocks = rows.reshape(layout.experts, layout.block, rows.shape[1])
    return depth_exchange(blocks, layout.experts).reshape(rows.shape)


def swap_pair(pair, experts):
    return plane_move(pair[0], experts, 1), plane_move(pair[1], experts, 2)


def spread_halves(mine, experts):
    x_lo, y_hi = swap_pair(mine, experts)
    x_hi, y_lo = swap_pair((mine[1], mine[0]), experts)
    return (x_lo, x_hi), (y_lo, y_hi)


def relay_halves(near, experts):
    return plane_move(near[0][0], experts, 2), plane_move(near[1][1], experts, 1)


def body(a_input, a_route, b_saved, b_grad, b_route, up_weight, down_weight, router):
    devices = lax.axis_size("expert")
    experts = router.shape[2]
    group = devices // experts
    tokens, width = a_input.shape[1], a_input.shape[2]
    layout = Layout(experts, tokens * a_route.shape[2] // experts + 2)
    here = lax.axis_index("expert") // group
    up, down, cols_r = up_weight[0], down_weight[0], router[0]
    b_ids = pipe_move(b_route[0].astype(BF16), lambda i, n: n - 1 - i).astype(jnp.int32)
    b_x = pipe_move(b_saved[0], lambda i, n: n - 1 - i)
    b_c = pipe_move(b_grad[0], lambda i, n: n - 1 - i)
    a_ids = a_route[0]
    own = jnp.where(jnp.arange(experts) == here, cols_r.astype(F32), 0.0)
    own = jnp.sum(own, axis=1, keepdims=True)
    line = own.reshape(1, width)
    col = jnp.where(jnp.arange(128)[None, :] == 0, own, 0.0).astype(BF16)
    place, select = layout.places()
    a_target, b_target = target_rows(a_ids[:, 0], layout), target_rows(b_ids[:, 0], layout)

    a_send, a_gate = send_normed(a_input[0], a_ids, cols_r, a_target, layout)
    up_turned, down_turned = up.T, down.T
    a_blocks = across_planes(a_send, layout)
    a_mine, _ = pack_halves(a_blocks, select, (up_turned, down_turned))
    a_near = spread_halves(a_mine, experts)
    a_far = relay_halves(a_near, experts)
    b_send, b_gate = send_normed(b_x, b_ids, cols_r, b_target, layout, a_near[0] + a_near[1])
    b_blocks = across_planes(b_send, layout)

    act = a_near_rows((a_mine,) + a_near, up, b_gate)
    a_first, a_ready = a_far_rows(a_far, act, up, down)
    a_first = swap_pair(a_first, experts)
    b_mine, _ = pack_halves(b_blocks, select, (a_ready,))
    b_near = spread_halves(b_mine, experts)
    b_far = relay_halves(b_near, experts)

    a_second, a_done = a_second_rows(act, down, a_first, (b_near[0][0], b_near[1][1]))
    a_second = swap_pair(a_second, experts)
    c_send, _ = send_cotangents(b_c, b_gate, b_target, layout, (a_done,))
    c_blocks = across_planes(c_send, layout)
    c_mine, _ = pack_halves(c_blocks, select)
    c_near = spread_halves(c_mine, experts)
    c_far = relay_halves(c_near, experts)
    early, b_ready = b_hidden_rows((b_mine,) + b_near + (b_far,), up, col)
    a_total, a_summed = a_total_rows(act, down, a_first, a_second, place, (b_ready,))
    a_back = across_planes(a_total, layout)
    a_out = forward_out(a_input[0], a_gate, a_back, a_target)
    a_next = pipe_move(a_out, lambda i, n: i + 1)

    cots = (c_mine,) + c_near
    near, b_plain = b_near_rows(cots, early, up_turned, down_turned, line, (a_summed,))
    b_plain = swap_pair(b_plain, experts)
    far, b_relay = b_far_rows(c_far, early, near, up_turned, down_turned, line)
    b_relay = swap_pair(b_relay, experts)
    b_second = b_second_rows(near, up_turned, line, b_relay, b_plain)
    b_second = swap_pair(b_second, experts)
    b_total, b_done = b_total_rows(near, up_turned, line, b_plain, b_second, place)
    b_out = backward_out(b_x, b_c, across_planes(b_total, layout), b_target)
    b_next = pipe_move(b_out, lambda i, n: n - i)
    up_grad, down_grad = weight_grads(
        (b_mine,) + b_near + (b_far,), (c_mine,) + c_near + (c_far,), near, far, b_done
    )
    return (a_next[None], b_next[None], up_grad[None], down_grad[None])


def solution(mesh):
    return jax.shard_map(
        body,
        mesh=mesh,
        in_specs=(
            P("pipe", "expert", None),
            P("pipe", "expert", None),
            P("pipe", "expert", None),
            P("pipe", "expert", None),
            P("pipe", "expert", None),
            P("pipe", None, "expert"),
            P("pipe", "expert", None),
            P("pipe", None, None),
        ),
        out_specs=(
            P("pipe", "expert", None),
            P("pipe", "expert", None),
            P("pipe", None, "expert"),
            P("pipe", "expert", None),
        ),
        check_vma=False,
    )
```

```python
import jax
import jax.numpy as jnp
import numpy as np
from jax import lax
from jax.experimental import pallas as pl
from jax.experimental.pallas import tpu as pltpu
from jax.sharding import PartitionSpec as P

EPS = 1e-06
F32 = jnp.float32
BF16 = jnp.bfloat16


def dot(a, b, dims=((1,), (0,))):
    return lax.dot_general(a, b, (dims, ((), ())), preferred_element_type=F32)


def pipe_move(array, target):
    count = lax.axis_size("pipe")
    pairs = [(i, target(i, count) % count) for i in range(count)]
    if all(a == b for a, b in pairs):
        return array
    return lax.ppermute(array, "pipe", pairs)


def plane_move(array, experts, bit):
    devices = lax.axis_size("expert")
    return lax.ppermute(array, "expert", [(i, i ^ bit) for i in range(devices)])


def depth_exchange(blocks, experts):
    devices = lax.axis_size("expert")
    group = devices // experts
    columns = [[e * group + m for e in range(experts)] for m in range(group)]
    return lax.all_to_all(
        blocks, "expert", split_axis=0, concat_axis=0, tiled=True, axis_index_groups=columns
    )


class Layout:
    cuts = 4

    def __init__(self, experts, capacity):
        self.experts = experts
        self.slots = capacity
        self.block = self.cuts * capacity
        self.sent = experts * self.block
        self.packed = experts * capacity

    def places(self):
        packed = np.arange(self.packed)
        found = np.zeros((self.cuts, self.sent, self.packed), np.float32)
        for c in range(self.cuts):
            row = packed // self.slots * self.block + c * self.slots + packed % self.slots
            found[c, row, packed] = 1.0
        return jnp.asarray(found, BF16), jnp.asarray(found.transpose(0, 2, 1), BF16)


def on_core(name, work, outs, *args, after=()):
    first_out = len(args) + len(after)

    def kernel(*refs):
        work(refs[: len(args)], refs[first_out:])

    space = pl.BlockSpec(memory_space=pltpu.VMEM)
    return pl.pallas_call(
        kernel,
        out_shape=[jax.ShapeDtypeStruct(shape, kind) for shape, kind in outs],
        in_specs=[space] * len(args) + [pl.BlockSpec(memory_space=pl.ANY)] * len(after),
        out_specs=[space] * len(outs),
        compiler_params=pltpu.CompilerParams(vmem_limit_bytes=16 * 2**20),
        cost_estimate=pl.CostEstimate(flops=10**6, bytes_accessed=10**5, transcendentals=0),
        name=name,
    )(*args, *after)


NT = ((1,), (1,))
TN = ((0,), (0,))


TOKEN = ((8, 128), F32)


def first_rows(ids, layout):
    tokens = ids.shape[0]
    named = lax.broadcasted_iota(jnp.int32, (tokens, 128), 1) == ids
    row = lax.broadcasted_iota(jnp.int32, (tokens, tokens), 0)
    other = lax.broadcasted_iota(jnp.int32, (tokens, tokens), 1)
    earlier = jnp.where(other < row, 1.0, 0.0).astype(BF16)
    count = dot(earlier, jnp.where(named, 1.0, 0.0).astype(BF16))
    slot = jnp.sum(jnp.where(named, count, 0.0), axis=1, keepdims=True)
    return ids * layout.block + slot.astype(jnp.int32)


def picks(ids, layout):
    first = first_rows(ids, layout)
    place = lax.broadcasted_iota(jnp.int32, (ids.shape[0], layout.sent), 1)
    return [
        jnp.where(place == first + c * layout.slots, 1.0, 0.0).astype(BF16)
        for c in range(layout.cuts)
    ]


def sent_rows(values, ids, layout):
    part = values.shape[1] // layout.cuts
    total = 0.0
    for c, pick in enumerate(picks(ids, layout)):
        total = total + dot(pick, values[:, c * part : (c + 1) * part], TN)
    return total.astype(BF16)


def token_rows(ref, ids, layout):
    return jnp.concatenate([dot(pick, ref[...]) for pick in picks(ids, layout)], axis=1)


def normed_rows(x_ref):
    feat = x_ref[...].astype(F32)
    scale = lax.rsqrt(jnp.mean(feat * feat, axis=1, keepdims=True) + EPS)
    return (feat * scale).astype(BF16)


def gate_rows(normed, ids, router_ref):
    scores = dot(normed, router_ref[...])
    expert = lax.broadcasted_iota(jnp.int32, scores.shape, 1)
    score = jnp.sum(jnp.where(expert == ids, scores, 0.0), axis=1, keepdims=True)
    return jax.nn.sigmoid(score)


def send_rows(x, ids, layout):
    def work(ins, outs):
        outs[0][...] = sent_rows(normed_rows(ins[0]), ins[1][...], layout)

    outs = [((layout.sent, x.shape[1] // layout.cuts), BF16)]
    return on_core("send_rows", work, outs, x, ids)[0]


def send_normed(x, ids, router, layout, after=()):
    tokens, width = x.shape

    def work(ins, outs):
        normed, named = normed_rows(ins[0]), ins[1][...]
        outs[0][...] = sent_rows(normed, named, layout)
        outs[1][...] = jnp.broadcast_to(gate_rows(normed, named, ins[2]), (tokens, 128))

    outs = [((layout.sent, width // layout.cuts), BF16), ((tokens, 128), F32)]
    return on_core("send_normed", work, outs, x, ids, router, after=after)


def send_cotangents(cot, gate, ids, layout, after=()):
    def work(ins, outs):
        values = (ins[1][:, :1] * ins[0][...].astype(F32)).astype(BF16)
        outs[0][...] = sent_rows(values, ins[2][...], layout)

    outs = [((layout.sent, cot.shape[1] // layout.cuts), BF16)]
    return on_core("send_cotangents", work, outs, cot, gate, ids, after=after)[0]


def forward_out(x, router, back, ids, layout):
    def work(ins, outs):
        named = ins[3][...]
        gate = gate_rows(normed_rows(ins[0]), named, ins[1])
        rows = token_rows(ins[2], named, layout)
        outs[0][...] = (ins[0][...].astype(F32) + gate * rows).astype(BF16)

    return on_core("forward_out", work, [(x.shape, BF16)], x, router, back, ids)[0]


def backward_out(x, cot, back, ids, layout):
    width = x.shape[1]

    def work(ins, outs):
        feat = ins[0][...].astype(F32)
        scale = lax.rsqrt(jnp.mean(feat * feat, axis=1, keepdims=True) + EPS)
        normed_grad = token_rows(ins[2], ins[3][...], layout)
        along = jnp.sum(normed_grad * feat, axis=1, keepdims=True) / width
        feature_grad = scale * normed_grad - feat * (scale * scale * scale) * along
        outs[0][...] = (ins[1][...].astype(F32) + feature_grad).astype(BF16)

    return on_core("backward_out", work, [(x.shape, BF16)], x, cot, back, ids)[0]


def pack_halves(blocks, select, after=()):
    cuts, rows, _ = select.shape
    part = blocks.shape[1]
    half = cuts * part // 2

    def work(ins, outs):
        for c in range(cuts):
            begin = c * part % half
            outs[c * part // half][:, begin : begin + part] = dot(ins[1][c], ins[0][...]).astype(
                BF16
            )
        outs[2][...] = jnp.zeros(TOKEN[0], F32)

    lo, hi, token = on_core(
        "pack", work, [((rows, half), BF16)] * 2 + [TOKEN], blocks, select, after=after
    )
    return (lo, hi), token


def placed(parts, place_ref):
    cuts = place_ref.shape[0]
    part = 2 * parts[0].shape[1] // cuts
    rows = 0.0
    for c in range(cuts):
        begin = c * part % parts[0].shape[1]
        rows = rows + dot(
            place_ref[c], parts[c * part // parts[0].shape[1]][:, begin : begin + part]
        )
    return rows.astype(BF16)


def a_near_rows(blocks, up, after):
    half, hidden_units = up.shape[0] // 2, up.shape[1]
    rows = blocks[0][0].shape[0]

    def work(ins, outs):
        for j in range(3):
            hidden = dot(ins[2 * j][...], ins[6][:half]) + dot(ins[2 * j + 1][...], ins[6][half:])
            outs[0][j] = (hidden * jax.nn.sigmoid(hidden)).astype(BF16)

    flat = [half_block for block in blocks for half_block in block]
    return on_core("a_near", work, [((3, rows, hidden_units), BF16)], *flat, up, after=(after,))[0]


def a_far_rows(block, act, up, down):
    half, rows = up.shape[0] // 2, act.shape[1]

    def work(ins, outs):
        lo, hi, acts, up_ref, down_ref = ins
        hidden = dot(lo[...], up_ref[:half]) + dot(hi[...], up_ref[half:])
        far = (hidden * jax.nn.sigmoid(hidden)).astype(BF16)
        for h in range(2):
            weights = down_ref[:, h * half : (h + 1) * half]
            outs[h][0] = dot(far, weights).astype(BF16)
            outs[h][1] = dot(acts[1 + h], weights).astype(BF16)
        outs[2][...] = jnp.zeros(TOKEN[0], F32)

    outs = [((2, rows, half), BF16)] * 2 + [TOKEN]
    by_x, by_y, token = on_core("a_far", work, outs, *block, act, up, down)
    return (by_x, by_y), token


def a_second_rows(act, down, got, after=()):
    half, rows = down.shape[1] // 2, act.shape[1]

    def work(ins, outs):
        acts, down_ref, by_x, by_y = ins
        outs[0][...] = (dot(acts[1], down_ref[:, half:]) + by_y[0].astype(F32)).astype(BF16)
        outs[1][...] = (dot(acts[2], down_ref[:, :half]) + by_x[0].astype(F32)).astype(BF16)
        outs[2][...] = jnp.zeros(TOKEN[0], F32)

    outs = [((rows, half), BF16)] * 2 + [TOKEN]
    by_x, by_y, token = on_core("a_second", work, outs, act, down, *got, after=after)
    return (by_x, by_y), token


def a_total_rows(act, down, first, second, place, after):
    half = down.shape[1] // 2

    def work(ins, outs):
        acts, down_ref, first_x, first_y, second_x, second_y, place_ref = ins
        parts = []
        for h, (one, two) in enumerate(((first_x, second_y), (first_y, second_x))):
            cols = slice(h * half, (h + 1) * half)
            total = dot(acts[0], down_ref[:, cols]) + one[1].astype(F32) + two[...].astype(F32)
            parts.append(total.astype(BF16))
        outs[0][...] = placed(parts, place_ref)
        outs[1][...] = jnp.zeros(TOKEN[0], F32)

    outs = [((place.shape[1], 2 * half // place.shape[0]), BF16), TOKEN]
    return on_core("a_total", work, outs, act, down, *first, *second, place, after=after)


def b_hidden_rows(blocks, up, col):
    half, units, rows = up.shape[0] // 2, up.shape[1], blocks[0][0].shape[0]

    def work(ins, outs):
        up_ref, col_ref = ins[8:]
        for j in range(4):
            lo, hi = ins[2 * j][...], ins[2 * j + 1][...]
            outs[0][j] = dot(lo, up_ref[:half]) + dot(hi, up_ref[half:])
            outs[1][j] = dot(lo, col_ref[:half]) + dot(hi, col_ref[half:])

        outs[2][...] = jnp.zeros(TOKEN[0], F32)

    flat = [v for block in blocks for v in block]
    outs = [((4, rows, units), F32), ((4, rows, 128), F32), TOKEN]
    hidden, score, token = on_core("b_hidden", work, outs, *flat, up, col)
    return (hidden, score), token


def back_rows(hidden, score, c_lo, c_hi, down_ref):
    half = c_lo.shape[1]
    act_grad = dot(c_lo, down_ref[:half]) + dot(c_hi, down_ref[half:])
    sigma = jax.nn.sigmoid(hidden)
    active = hidden * sigma
    hid_grad = (act_grad * sigma * (1.0 + hidden * (1.0 - sigma))).astype(BF16)
    term = jnp.sum(active * act_grad, axis=1, keepdims=True) * jax.nn.sigmoid(-score[:, :1])
    return active.astype(BF16), hid_grad, term


def grad_rows(hid_grad, term, up_ref, line_ref, cols):
    return dot(hid_grad, up_ref[:, cols]) + term * line_ref[:, cols]


def b_near_rows(cots, early, up, down, line, after):
    half, units, rows = up.shape[1] // 2, up.shape[0], cots[0][0].shape[0]

    def work(ins, outs):
        hidden, score, up_ref, down_ref, line_ref = ins[6:]
        for j in range(3):
            lo, hi = ins[2 * j][...], ins[2 * j + 1][...]
            act, hid, term = back_rows(hidden[j], score[j], lo, hi, down_ref)
            outs[0][j], outs[1][j] = act, hid
            outs[2][j] = jnp.broadcast_to(term, (rows, 128))
            if j:
                cols = slice((j - 1) * half, j * half)
                outs[2 + j][...] = grad_rows(hid, term, up_ref, line_ref, cols).astype(BF16)

    flat = [v for block in cots for v in block]
    outs = [((3, rows, units), BF16)] * 2 + [((3, rows, 128), F32)]
    outs += [((rows, half), BF16)] * 2
    act, hid, term, by_x, by_y = on_core("b_near", work, outs, *flat, *early, up, down, line, after=after)
    return (act, hid, term), (by_x, by_y)


def b_far_rows(cots, early, near, up, down, line):
    half, units, rows = up.shape[1] // 2, up.shape[0], cots[0].shape[0]

    def work(ins, outs):
        lo, hi, hidden, score, up_ref, down_ref, line_ref = ins
        act, hid, term = back_rows(hidden[3], score[3], lo[...], hi[...], down_ref)
        outs[0][...], outs[1][...] = act, hid
        for h in range(2):
            part = grad_rows(hid, term, up_ref, line_ref, slice(h * half, (h + 1) * half))
            outs[2 + h][...] = part.astype(BF16)

    outs = [((rows, units), BF16)] * 2 + [((rows, half), BF16)] * 2
    args = (*cots, *early, up, down, line)
    act, hid, by_x, by_y = on_core("b_far", work, outs, *args, after=(near[2],))
    return (act, hid), (by_x, by_y)


def b_second_rows(near, up, line, got, plain):
    half, rows = up.shape[1] // 2, got[0].shape[0]

    def work(ins, outs):
        hids, terms, up_ref, line_ref, by_x, by_y = ins
        for side, ref in enumerate((by_y, by_x)):
            j, cols = 1 + side, slice((1 - side) * half, (2 - side) * half)
            part = grad_rows(hids[j], terms[j][:, :1], up_ref, line_ref, cols)
            outs[side][...] = (part + ref[...].astype(F32)).astype(BF16)

    outs = [((rows, half), BF16)] * 2
    return on_core("b_second", work, outs, near[1], near[2], up, line, *got, after=plain)


def b_total_rows(near, up, line, plain, second, place):
    half = up.shape[1] // 2

    def work(ins, outs):
        hids, terms, up_ref, line_ref, plain_x, plain_y, second_x, second_y, place_ref = ins
        parts = []
        for h, (one, two) in enumerate(((plain_x, second_y), (plain_y, second_x))):
            cols = slice(h * half, (h + 1) * half)
            part = grad_rows(hids[0], terms[0][:, :1], up_ref, line_ref, cols)
            parts.append((part + one[...].astype(F32) + two[...].astype(F32)).astype(BF16))
        outs[0][...] = placed(parts, place_ref)
        outs[1][...] = jnp.zeros(TOKEN[0], F32)

    outs = [((place.shape[1], 2 * half // place.shape[0]), BF16), TOKEN]
    return on_core("b_total", work, outs, near[1], near[2], up, line, *plain, *second, place)


def weight_grads(blocks, cots, near, far, after):
    half, units = blocks[0][0].shape[1], far[0].shape[1]
    tile = 256

    def work(ins, outs):
        xs, cs = ins[0:8], ins[8:16]
        acts = [ins[16][j] for j in range(3)] + [ins[18][...]]
        hids = [ins[17][j] for j in range(3)] + [ins[19][...]]
        for h in range(2):
            for begin in range(0, half, tile):
                cols, out = slice(begin, begin + tile), slice(h * half + begin, h * half + begin + tile)
                up_sum, down_sum = 0.0, 0.0
                for j in range(4):
                    up_sum = up_sum + dot(xs[2 * j + h][:, cols], hids[j], TN)
                    down_sum = down_sum + dot(acts[j], cs[2 * j + h][:, cols], TN)
                outs[0][out, :] = up_sum.astype(BF16)
                outs[1][:, out] = down_sum.astype(BF16)

    flat = [v for block in blocks for v in block] + [v for block in cots for v in block]
    outs = [((2 * half, units), BF16), ((units, 2 * half), BF16)]
    return on_core("weight_grads", work, outs, *flat, near[0], near[1], *far, after=(after,))


def across_planes(rows, layout):
    blocks = rows.reshape(layout.experts, layout.block, rows.shape[1])
    return depth_exchange(blocks, layout.experts).reshape(rows.shape)


def swap_pair(pair, experts):
    return plane_move(pair[0], experts, 1), plane_move(pair[1], experts, 2)


def spread_halves(mine, experts):
    x_lo, y_hi = swap_pair(mine, experts)
    x_hi, y_lo = swap_pair((mine[1], mine[0]), experts)
    return (x_lo, x_hi), (y_lo, y_hi)


def relay_halves(near, experts):
    return plane_move(near[0][0], experts, 2), plane_move(near[1][1], experts, 1)


def body(a_input, a_route, b_saved, b_grad, b_route, up_weight, down_weight, router):
    devices = lax.axis_size("expert")
    experts = router.shape[2]
    group = devices // experts
    tokens, width = a_input.shape[1], a_input.shape[2]
    layout = Layout(experts, tokens * a_route.shape[2] // experts + 2)
    here = lax.axis_index("expert") // group
    up, down, cols_r = up_weight[0], down_weight[0], router[0]
    b_ids = pipe_move(b_route[0].astype(BF16), lambda i, n: n - 1 - i).astype(jnp.int32)
    b_x = pipe_move(b_saved[0], lambda i, n: n - 1 - i)
    b_c = pipe_move(b_grad[0], lambda i, n: n - 1 - i)
    a_ids = a_route[0]
    own = jnp.where(jnp.arange(experts) == here, cols_r.astype(F32), 0.0)
    own = jnp.sum(own, axis=1, keepdims=True)
    line = own.reshape(1, width)
    col = jnp.where(jnp.arange(128)[None, :] == 0, own, 0.0).astype(BF16)
    place, select = layout.places()

    a_send = send_rows(a_input[0], a_ids, layout)
    up_turned, down_turned = up.T, down.T
    a_blocks = across_planes(a_send, layout)
    a_mine, _ = pack_halves(a_blocks, select, (up_turned, down_turned))
    a_near = spread_halves(a_mine, experts)
    a_far = relay_halves(a_near, experts)
    b_send, b_gate = send_normed(b_x, b_ids, cols_r, layout, (a_near[0][0],))
    b_blocks = across_planes(b_send, layout)

    act = a_near_rows((a_mine,) + a_near, up, b_gate)
    a_first, a_ready = a_far_rows(a_far, act, up, down)
    a_first = swap_pair(a_first, experts)
    b_mine, _ = pack_halves(b_blocks, select, (a_ready,))
    b_near = spread_halves(b_mine, experts)
    b_far = relay_halves(b_near, experts)

    a_second, a_done = a_second_rows(act, down, a_first)
    a_second = swap_pair(a_second, experts)
    c_send = send_cotangents(b_c, b_gate, b_ids, layout, (a_done,))
    c_blocks = across_planes(c_send, layout)
    c_mine, _ = pack_halves(c_blocks, select)
    c_near = spread_halves(c_mine, experts)
    c_far = relay_halves(c_near, experts)
    early, b_ready = b_hidden_rows((b_mine,) + b_near + (b_far,), up, col)
    a_total, a_summed = a_total_rows(act, down, a_first, a_second, place, (b_ready,))
    a_back = across_planes(a_total, layout)
    a_out = forward_out(a_input[0], cols_r, a_back, a_ids, layout)
    a_next = pipe_move(a_out, lambda i, n: i + 1)

    cots = (c_mine,) + c_near
    near, b_plain = b_near_rows(cots, early, up_turned, down_turned, line, (a_summed,))
    b_plain = swap_pair(b_plain, experts)
    far, b_relay = b_far_rows(c_far, early, near, up_turned, down_turned, line)
    b_relay = swap_pair(b_relay, experts)
    b_second = b_second_rows(near, up_turned, line, b_relay, b_plain)
    b_second = swap_pair(b_second, experts)
    b_total, b_done = b_total_rows(near, up_turned, line, b_plain, b_second, place)
    b_out = backward_out(b_x, b_c, across_planes(b_total, layout), b_ids, layout)
    b_next = pipe_move(b_out, lambda i, n: n - i)
    up_grad, down_grad = weight_grads(
        (b_mine,) + b_near + (b_far,), (c_mine,) + c_near + (c_far,), near, far, b_done
    )
    return (a_next[None], b_next[None], up_grad[None], down_grad[None])


def solution(mesh):
    return jax.shard_map(
        body,
        mesh=mesh,
        in_specs=(
            P("pipe", "expert", None),
            P("pipe", "expert", None),
            P("pipe", "expert", None),
            P("pipe", "expert", None),
            P("pipe", "expert", None),
            P("pipe", None, "expert"),
            P("pipe", "expert", None),
            P("pipe", None, None),
        ),
        out_specs=(
            P("pipe", "expert", None),
            P("pipe", "expert", None),
            P("pipe", None, "expert"),
            P("pipe", "expert", None),
        ),
        check_vma=False,
    )
```

```python
import jax
import jax.numpy as jnp
import numpy as np
from jax import lax
from jax.experimental import pallas as pl
from jax.experimental.pallas import tpu as pltpu
from jax.sharding import PartitionSpec as P

EPS = 1e-06
F32 = jnp.float32
BF16 = jnp.bfloat16


def dot(a, b, dims=((1,), (0,))):
    return lax.dot_general(a, b, (dims, ((), ())), preferred_element_type=F32)


def pipe_move(array, target):
    count = lax.axis_size("pipe")
    pairs = [(i, target(i, count) % count) for i in range(count)]
    if all(a == b for a, b in pairs):
        return array
    return lax.ppermute(array, "pipe", pairs)


def plane_move(array, experts, bit):
    devices = lax.axis_size("expert")
    return lax.ppermute(array, "expert", [(i, i ^ bit) for i in range(devices)])


def depth_exchange(blocks, experts):
    devices = lax.axis_size("expert")
    group = devices // experts
    columns = [[e * group + m for e in range(experts)] for m in range(group)]
    return lax.all_to_all(
        blocks, "expert", split_axis=0, concat_axis=0, tiled=True, axis_index_groups=columns
    )


class Layout:
    cuts = 4

    def __init__(self, experts, capacity):
        self.experts = experts
        self.slots = capacity
        self.block = self.cuts * capacity
        self.sent = experts * self.block
        self.packed = experts * capacity

    def places(self):
        packed = np.arange(self.packed)
        found = np.zeros((self.cuts, self.sent, self.packed), np.float32)
        for c in range(self.cuts):
            row = packed // self.slots * self.block + c * self.slots + packed % self.slots
            found[c, row, packed] = 1.0
        return jnp.asarray(found, BF16), jnp.asarray(found.transpose(0, 2, 1), BF16)


def on_core(name, work, outs, *args, after=()):
    first_out = len(args) + len(after)

    def kernel(*refs):
        work(refs[: len(args)], refs[first_out:])

    space = pl.BlockSpec(memory_space=pltpu.VMEM)
    return pl.pallas_call(
        kernel,
        out_shape=[jax.ShapeDtypeStruct(shape, kind) for shape, kind in outs],
        in_specs=[space] * len(args) + [pl.BlockSpec(memory_space=pl.ANY)] * len(after),
        out_specs=[space] * len(outs),
        compiler_params=pltpu.CompilerParams(vmem_limit_bytes=16 * 2**20),
        cost_estimate=pl.CostEstimate(flops=10**6, bytes_accessed=10**5, transcendentals=0),
        name=name,
    )(*args, *after)


NT = ((1,), (1,))
TN = ((0,), (0,))


TOKEN = ((8, 128), F32)


def first_rows(ids, layout):
    tokens = ids.shape[0]
    named = lax.broadcasted_iota(jnp.int32, (tokens, 128), 1) == ids
    row = lax.broadcasted_iota(jnp.int32, (tokens, tokens), 0)
    other = lax.broadcasted_iota(jnp.int32, (tokens, tokens), 1)
    earlier = jnp.where(other < row, 1.0, 0.0).astype(BF16)
    count = dot(earlier, jnp.where(named, 1.0, 0.0).astype(BF16))
    slot = jnp.sum(jnp.where(named, count, 0.0), axis=1, keepdims=True)
    return ids * layout.block + slot.astype(jnp.int32)


def picks(ids, layout):
    first = first_rows(ids, layout)
    place = lax.broadcasted_iota(jnp.int32, (ids.shape[0], layout.sent), 1)
    return [
        jnp.where(place == first + c * layout.slots, 1.0, 0.0).astype(BF16)
        for c in range(layout.cuts)
    ]


def sent_rows(values, ids, layout):
    part = values.shape[1] // layout.cuts
    total = 0.0
    for c, pick in enumerate(picks(ids, layout)):
        total = total + dot(pick, values[:, c * part : (c + 1) * part], TN)
    return total.astype(BF16)


def token_rows(ref, ids, layout):
    return jnp.concatenate([dot(pick, ref[...]) for pick in picks(ids, layout)], axis=1)


def normed_rows(x_ref):
    feat = x_ref[...].astype(F32)
    scale = lax.rsqrt(jnp.mean(feat * feat, axis=1, keepdims=True) + EPS)
    return (feat * scale).astype(BF16)


def gate_rows(normed, ids, router_ref):
    scores = dot(normed, router_ref[...])
    expert = lax.broadcasted_iota(jnp.int32, scores.shape, 1)
    score = jnp.sum(jnp.where(expert == ids, scores, 0.0), axis=1, keepdims=True)
    return jax.nn.sigmoid(score)


def send_rows(x, ids, layout):
    def work(ins, outs):
        outs[0][...] = sent_rows(normed_rows(ins[0]), ins[1][...], layout)

    outs = [((layout.sent, x.shape[1] // layout.cuts), BF16)]
    return on_core("send_rows", work, outs, x, ids)[0]


def send_normed(x, ids, router, layout, after=()):
    tokens, width = x.shape

    def work(ins, outs):
        normed, named = normed_rows(ins[0]), ins[1][...]
        outs[0][...] = sent_rows(normed, named, layout)
        outs[1][...] = jnp.broadcast_to(gate_rows(normed, named, ins[2]), (tokens, 128))

    outs = [((layout.sent, width // layout.cuts), BF16), ((tokens, 128), F32)]
    return on_core("send_normed", work, outs, x, ids, router, after=after)


def send_cotangents(cot, gate, ids, layout, after=()):
    def work(ins, outs):
        values = (ins[1][:, :1] * ins[0][...].astype(F32)).astype(BF16)
        outs[0][...] = sent_rows(values, ins[2][...], layout)

    outs = [((layout.sent, cot.shape[1] // layout.cuts), BF16)]
    return on_core("send_cotangents", work, outs, cot, gate, ids, after=after)[0]


def forward_out(x, router, back, ids, layout):
    def work(ins, outs):
        named = ins[3][...]
        gate = gate_rows(normed_rows(ins[0]), named, ins[1])
        rows = token_rows(ins[2], named, layout)
        outs[0][...] = (ins[0][...].astype(F32) + gate * rows).astype(BF16)

    return on_core("forward_out", work, [(x.shape, BF16)], x, router, back, ids)[0]


def backward_out(x, cot, back, ids, layout):
    width = x.shape[1]

    def work(ins, outs):
        feat = ins[0][...].astype(F32)
        scale = lax.rsqrt(jnp.mean(feat * feat, axis=1, keepdims=True) + EPS)
        normed_grad = token_rows(ins[2], ins[3][...], layout)
        along = jnp.sum(normed_grad * feat, axis=1, keepdims=True) / width
        feature_grad = scale * normed_grad - feat * (scale * scale * scale) * along
        outs[0][...] = (ins[1][...].astype(F32) + feature_grad).astype(BF16)

    return on_core("backward_out", work, [(x.shape, BF16)], x, cot, back, ids)[0]


def pack_halves(blocks, select, after=()):
    cuts, rows, _ = select.shape
    part = blocks.shape[1]
    half = cuts * part // 2

    def work(ins, outs):
        for c in range(cuts):
            begin = c * part % half
            outs[c * part // half][:, begin : begin + part] = dot(ins[1][c], ins[0][...]).astype(
                BF16
            )
        outs[2][...] = jnp.zeros(TOKEN[0], F32)

    lo, hi, token = on_core(
        "pack", work, [((rows, half), BF16)] * 2 + [TOKEN], blocks, select, after=after
    )
    return (lo, hi), token


def placed(parts, place_ref):
    cuts = place_ref.shape[0]
    part = 2 * parts[0].shape[1] // cuts
    rows = 0.0
    for c in range(cuts):
        begin = c * part % parts[0].shape[1]
        rows = rows + dot(
            place_ref[c], parts[c * part // parts[0].shape[1]][:, begin : begin + part]
        )
    return rows.astype(BF16)


def a_near_rows(blocks, up, after):
    half, hidden_units = up.shape[0] // 2, up.shape[1]
    rows = blocks[0][0].shape[0]

    def work(ins, outs):
        for j in range(3):
            hidden = dot(ins[2 * j][...], ins[6][:half]) + dot(ins[2 * j + 1][...], ins[6][half:])
            outs[0][j] = (hidden * jax.nn.sigmoid(hidden)).astype(BF16)

    flat = [half_block for block in blocks for half_block in block]
    return on_core("a_near", work, [((3, rows, hidden_units), BF16)], *flat, up, after=(after,))[0]


def a_far_rows(block, act, up, down):
    half, rows = up.shape[0] // 2, act.shape[1]

    def work(ins, outs):
        lo, hi, acts, up_ref, down_ref = ins
        hidden = dot(lo[...], up_ref[:half]) + dot(hi[...], up_ref[half:])
        far = (hidden * jax.nn.sigmoid(hidden)).astype(BF16)
        for h in range(2):
            weights = down_ref[:, h * half : (h + 1) * half]
            outs[h][0] = dot(far, weights).astype(BF16)
            outs[h][1] = dot(acts[1 + h], weights).astype(BF16)
        outs[2][...] = jnp.zeros(TOKEN[0], F32)

    outs = [((2, rows, half), BF16)] * 2 + [TOKEN]
    by_x, by_y, token = on_core("a_far", work, outs, *block, act, up, down)
    return (by_x, by_y), token


def a_second_rows(act, down, got, after=()):
    half, rows = down.shape[1] // 2, act.shape[1]

    def work(ins, outs):
        acts, down_ref, by_x, by_y = ins
        outs[0][...] = (dot(acts[1], down_ref[:, half:]) + by_y[0].astype(F32)).astype(BF16)
        outs[1][...] = (dot(acts[2], down_ref[:, :half]) + by_x[0].astype(F32)).astype(BF16)
        outs[2][...] = jnp.zeros(TOKEN[0], F32)

    outs = [((rows, half), BF16)] * 2 + [TOKEN]
    by_x, by_y, token = on_core("a_second", work, outs, act, down, *got, after=after)
    return (by_x, by_y), token


def a_total_rows(act, down, first, second, place, after):
    half = down.shape[1] // 2

    def work(ins, outs):
        acts, down_ref, first_x, first_y, second_x, second_y, place_ref = ins
        parts = []
        for h, (one, two) in enumerate(((first_x, second_y), (first_y, second_x))):
            cols = slice(h * half, (h + 1) * half)
            total = dot(acts[0], down_ref[:, cols]) + one[1].astype(F32) + two[...].astype(F32)
            parts.append(total.astype(BF16))
        outs[0][...] = placed(parts, place_ref)
        outs[1][...] = jnp.zeros(TOKEN[0], F32)

    outs = [((place.shape[1], 2 * half // place.shape[0]), BF16), TOKEN]
    return on_core("a_total", work, outs, act, down, *first, *second, place, after=after)


def b_hidden_rows(blocks, up, col):
    half, units, rows = up.shape[0] // 2, up.shape[1], blocks[0][0].shape[0]

    def work(ins, outs):
        up_ref, col_ref = ins[8:]
        for j in range(4):
            lo, hi = ins[2 * j][...], ins[2 * j + 1][...]
            outs[0][j] = dot(lo, up_ref[:half]) + dot(hi, up_ref[half:])
            outs[1][j] = dot(lo, col_ref[:half]) + dot(hi, col_ref[half:])

        outs[2][...] = jnp.zeros(TOKEN[0], F32)

    flat = [v for block in blocks for v in block]
    outs = [((4, rows, units), F32), ((4, rows, 128), F32), TOKEN]
    hidden, score, token = on_core("b_hidden", work, outs, *flat, up, col)
    return (hidden, score), token


def back_rows(hidden, score, c_lo, c_hi, down_ref):
    half = c_lo.shape[1]
    act_grad = dot(c_lo, down_ref[:half]) + dot(c_hi, down_ref[half:])
    sigma = jax.nn.sigmoid(hidden)
    active = hidden * sigma
    hid_grad = (act_grad * sigma * (1.0 + hidden * (1.0 - sigma))).astype(BF16)
    term = jnp.sum(active * act_grad, axis=1, keepdims=True) * jax.nn.sigmoid(-score[:, :1])
    return active.astype(BF16), hid_grad, term


def grad_rows(hid_grad, term, up_ref, line_ref, cols):
    return dot(hid_grad, up_ref[:, cols]) + term * line_ref[:, cols]


def b_near_rows(cots, early, up, down, line, after):
    half, units, rows = up.shape[1] // 2, up.shape[0], cots[0][0].shape[0]

    def work(ins, outs):
        hidden, score, up_ref, down_ref, line_ref = ins[6:]
        for j in range(3):
            lo, hi = ins[2 * j][...], ins[2 * j + 1][...]
            act, hid, term = back_rows(hidden[j], score[j], lo, hi, down_ref)
            outs[0][j], outs[1][j] = act, hid
            outs[2][j] = jnp.broadcast_to(term, (rows, 128))
            if j:
                cols = slice((j - 1) * half, j * half)
                outs[2 + j][...] = grad_rows(hid, term, up_ref, line_ref, cols).astype(BF16)

    flat = [v for block in cots for v in block]
    outs = [((3, rows, units), BF16)] * 2 + [((3, rows, 128), F32)]
    outs += [((rows, half), BF16)] * 2
    act, hid, term, by_x, by_y = on_core("b_near", work, outs, *flat, *early, up, down, line, after=after)
    return (act, hid, term), (by_x, by_y)


def b_far_rows(cots, early, near, up, down, line):
    half, units, rows = up.shape[1] // 2, up.shape[0], cots[0].shape[0]

    def work(ins, outs):
        lo, hi, hidden, score, up_ref, down_ref, line_ref = ins
        act, hid, term = back_rows(hidden[3], score[3], lo[...], hi[...], down_ref)
        outs[0][...], outs[1][...] = act, hid
        for h in range(2):
            part = grad_rows(hid, term, up_ref, line_ref, slice(h * half, (h + 1) * half))
            outs[2 + h][...] = part.astype(BF16)

    outs = [((rows, units), BF16)] * 2 + [((rows, half), BF16)] * 2
    args = (*cots, *early, up, down, line)
    act, hid, by_x, by_y = on_core("b_far", work, outs, *args, after=(near[2],))
    return (act, hid), (by_x, by_y)


def b_second_rows(near, up, line, got, plain):
    half, rows = up.shape[1] // 2, got[0].shape[0]

    def work(ins, outs):
        hids, terms, up_ref, line_ref, by_x, by_y = ins
        for side, ref in enumerate((by_y, by_x)):
            j, cols = 1 + side, slice((1 - side) * half, (2 - side) * half)
            part = grad_rows(hids[j], terms[j][:, :1], up_ref, line_ref, cols)
            outs[side][...] = (part + ref[...].astype(F32)).astype(BF16)

    outs = [((rows, half), BF16)] * 2
    return on_core("b_second", work, outs, near[1], near[2], up, line, *got, after=plain)


def b_total_rows(near, up, line, plain, second, place):
    half = up.shape[1] // 2

    def work(ins, outs):
        hids, terms, up_ref, line_ref, plain_x, plain_y, second_x, second_y, place_ref = ins
        parts = []
        for h, (one, two) in enumerate(((plain_x, second_y), (plain_y, second_x))):
            cols = slice(h * half, (h + 1) * half)
            part = grad_rows(hids[0], terms[0][:, :1], up_ref, line_ref, cols)
            parts.append((part + one[...].astype(F32) + two[...].astype(F32)).astype(BF16))
        outs[0][...] = placed(parts, place_ref)
        outs[1][...] = jnp.zeros(TOKEN[0], F32)

    outs = [((place.shape[1], 2 * half // place.shape[0]), BF16), TOKEN]
    return on_core("b_total", work, outs, near[1], near[2], up, line, *plain, *second, place)


def weight_grads(blocks, cots, near, far, after):
    half, units = blocks[0][0].shape[1], far[0].shape[1]
    tile = 256

    def work(ins, outs):
        xs, cs = ins[0:8], ins[8:16]
        acts = [ins[16][j] for j in range(3)] + [ins[18][...]]
        hids = [ins[17][j] for j in range(3)] + [ins[19][...]]
        for h in range(2):
            for begin in range(0, half, tile):
                cols, out = slice(begin, begin + tile), slice(h * half + begin, h * half + begin + tile)
                up_sum, down_sum = 0.0, 0.0
                for j in range(4):
                    up_sum = up_sum + dot(xs[2 * j + h][:, cols], hids[j], TN)
                    down_sum = down_sum + dot(acts[j], cs[2 * j + h][:, cols], TN)
                outs[0][out, :] = up_sum.astype(BF16)
                outs[1][:, out] = down_sum.astype(BF16)

    flat = [v for block in blocks for v in block] + [v for block in cots for v in block]
    outs = [((2 * half, units), BF16), ((units, 2 * half), BF16)]
    return on_core("weight_grads", work, outs, *flat, near[0], near[1], *far, after=(after,))


def across_planes(rows, layout):
    blocks = rows.reshape(layout.experts, layout.block, rows.shape[1])
    return depth_exchange(blocks, layout.experts).reshape(rows.shape)


def swap_pair(pair, experts):
    return plane_move(pair[0], experts, 1), plane_move(pair[1], experts, 2)


def spread_halves(mine, experts):
    x_lo, y_hi = swap_pair(mine, experts)
    x_hi, y_lo = swap_pair((mine[1], mine[0]), experts)
    return (x_lo, x_hi), (y_lo, y_hi)


def relay_halves(near, experts):
    return plane_move(near[0][0], experts, 2), plane_move(near[1][1], experts, 1)


def body(a_input, a_route, b_saved, b_grad, b_route, up_weight, down_weight, router):
    devices = lax.axis_size("expert")
    experts = router.shape[2]
    group = devices // experts
    tokens, width = a_input.shape[1], a_input.shape[2]
    layout = Layout(experts, tokens * a_route.shape[2] // experts + 2)
    here = lax.axis_index("expert") // group
    up, down, cols_r = up_weight[0], down_weight[0], router[0]
    b_ids = pipe_move(b_route[0].astype(BF16), lambda i, n: n - 1 - i).astype(jnp.int32)
    b_x = pipe_move(b_saved[0], lambda i, n: n - 1 - i)
    b_c = pipe_move(b_grad[0], lambda i, n: n - 1 - i)
    a_ids = a_route[0]
    own = jnp.where(jnp.arange(experts) == here, cols_r.astype(F32), 0.0)
    own = jnp.sum(own, axis=1, keepdims=True)
    line = own.reshape(1, width)
    col = jnp.where(jnp.arange(128)[None, :] == 0, own, 0.0).astype(BF16)
    place, select = layout.places()

    a_send = send_rows(a_input[0], a_ids, layout)
    up_turned, down_turned = up.T, down.T
    a_blocks = across_planes(a_send, layout)
    a_mine, _ = pack_halves(a_blocks, select, (up_turned, down_turned))
    a_near = spread_halves(a_mine, experts)
    a_far = relay_halves(a_near, experts)
    b_send, b_gate = send_normed(b_x, b_ids, cols_r, layout, (a_near[0][0],))
    b_blocks = across_planes(b_send, layout)

    act = a_near_rows((a_mine,) + a_near, up, b_gate)
    a_first, a_ready = a_far_rows(a_far, act, up, down)
    a_first = swap_pair(a_first, experts)
    b_mine, b_packed = pack_halves(b_blocks, select, (a_ready,))
    b_near = spread_halves(b_mine, experts)
    b_far = relay_halves(b_near, experts)

    a_second, a_done = a_second_rows(act, down, a_first)
    a_second = swap_pair(a_second, experts)
    c_send = send_cotangents(b_c, b_gate, b_ids, layout, (a_done, b_packed))
    c_blocks = across_planes(c_send, layout)
    c_mine, _ = pack_halves(c_blocks, select)
    c_near = spread_halves(c_mine, experts)
    c_far = relay_halves(c_near, experts)
    early, b_ready = b_hidden_rows((b_mine,) + b_near + (b_far,), up, col)
    a_total, a_summed = a_total_rows(act, down, a_first, a_second, place, (b_ready,))
    a_back = across_planes(a_total, layout)
    a_out = forward_out(a_input[0], cols_r, a_back, a_ids, layout)
    a_next = pipe_move(a_out, lambda i, n: i + 1)

    cots = (c_mine,) + c_near
    near, b_plain = b_near_rows(cots, early, up_turned, down_turned, line, (a_summed,))
    b_plain = swap_pair(b_plain, experts)
    far, b_relay = b_far_rows(c_far, early, near, up_turned, down_turned, line)
    b_relay = swap_pair(b_relay, experts)
    b_second = b_second_rows(near, up_turned, line, b_relay, b_plain)
    b_second = swap_pair(b_second, experts)
    b_total, b_done = b_total_rows(near, up_turned, line, b_plain, b_second, place)
    b_out = backward_out(b_x, b_c, across_planes(b_total, layout), b_ids, layout)
    b_next = pipe_move(b_out, lambda i, n: n - i)
    up_grad, down_grad = weight_grads(
        (b_mine,) + b_near + (b_far,), (c_mine,) + c_near + (c_far,), near, far, b_done
    )
    return (a_next[None], b_next[None], up_grad[None], down_grad[None])


def solution(mesh):
    return jax.shard_map(
        body,
        mesh=mesh,
        in_specs=(
            P("pipe", "expert", None),
            P("pipe", "expert", None),
            P("pipe", "expert", None),
            P("pipe", "expert", None),
            P("pipe", "expert", None),
            P("pipe", None, "expert"),
            P("pipe", "expert", None),
            P("pipe", None, None),
        ),
        out_specs=(
            P("pipe", "expert", None),
            P("pipe", "expert", None),
            P("pipe", None, "expert"),
            P("pipe", "expert", None),
        ),
        check_vma=False,
    )
```

```python
import jax
import jax.numpy as jnp
import numpy as np
from jax import lax
from jax.experimental import pallas as pl
from jax.experimental.pallas import tpu as pltpu
from jax.sharding import PartitionSpec as P

EPS = 1e-06
F32 = jnp.float32
BF16 = jnp.bfloat16


def dot(a, b, dims=((1,), (0,))):
    return lax.dot_general(a, b, (dims, ((), ())), preferred_element_type=F32)


def pipe_move(array, target):
    count = lax.axis_size("pipe")
    pairs = [(i, target(i, count) % count) for i in range(count)]
    if all(a == b for a, b in pairs):
        return array
    return lax.ppermute(array, "pipe", pairs)


def plane_move(array, experts, bit):
    devices = lax.axis_size("expert")
    return lax.ppermute(array, "expert", [(i, i ^ bit) for i in range(devices)])


def depth_exchange(blocks, experts):
    devices = lax.axis_size("expert")
    group = devices // experts
    columns = [[e * group + m for e in range(experts)] for m in range(group)]
    return lax.all_to_all(
        blocks, "expert", split_axis=0, concat_axis=0, tiled=True, axis_index_groups=columns
    )


class Layout:
    cuts = 4

    def __init__(self, experts, capacity):
        self.experts = experts
        self.slots = capacity
        self.block = self.cuts * capacity
        self.sent = experts * self.block
        self.packed = experts * capacity

    def places(self):
        packed = np.arange(self.packed)
        found = np.zeros((self.cuts, self.sent, self.packed), np.float32)
        for c in range(self.cuts):
            row = packed // self.slots * self.block + c * self.slots + packed % self.slots
            found[c, row, packed] = 1.0
        return jnp.asarray(found, BF16), jnp.asarray(found.transpose(0, 2, 1), BF16)


def on_core(name, work, outs, *args, after=()):
    first_out = len(args) + len(after)

    def kernel(*refs):
        work(refs[: len(args)], refs[first_out:])

    space = pl.BlockSpec(memory_space=pltpu.VMEM)
    return pl.pallas_call(
        kernel,
        out_shape=[jax.ShapeDtypeStruct(shape, kind) for shape, kind in outs],
        in_specs=[space] * len(args) + [pl.BlockSpec(memory_space=pl.ANY)] * len(after),
        out_specs=[space] * len(outs),
        compiler_params=pltpu.CompilerParams(vmem_limit_bytes=16 * 2**20),
        cost_estimate=pl.CostEstimate(flops=10**6, bytes_accessed=10**5, transcendentals=0),
        name=name,
    )(*args, *after)


NT = ((1,), (1,))
TN = ((0,), (0,))


TOKEN = ((8, 128), F32)


def first_rows(ids, layout):
    tokens = ids.shape[0]
    named = lax.broadcasted_iota(jnp.int32, (tokens, 128), 1) == ids
    row = lax.broadcasted_iota(jnp.int32, (tokens, tokens), 0)
    other = lax.broadcasted_iota(jnp.int32, (tokens, tokens), 1)
    earlier = jnp.where(other < row, 1.0, 0.0).astype(BF16)
    count = dot(earlier, jnp.where(named, 1.0, 0.0).astype(BF16))
    slot = jnp.sum(jnp.where(named, count, 0.0), axis=1, keepdims=True)
    return ids * layout.block + slot.astype(jnp.int32)


def picks(ids, layout):
    first = first_rows(ids, layout)
    place = lax.broadcasted_iota(jnp.int32, (ids.shape[0], layout.sent), 1)
    return [
        jnp.where(place == first + c * layout.slots, 1.0, 0.0).astype(BF16)
        for c in range(layout.cuts)
    ]


def sent_rows(values, ids, layout):
    part = values.shape[1] // layout.cuts
    total = 0.0
    for c, pick in enumerate(picks(ids, layout)):
        total = total + dot(pick, values[:, c * part : (c + 1) * part], TN)
    return total.astype(BF16)


def token_rows(ref, ids, layout):
    return jnp.concatenate([dot(pick, ref[...]) for pick in picks(ids, layout)], axis=1)


def normed_rows(x_ref):
    feat = x_ref[...].astype(F32)
    scale = lax.rsqrt(jnp.mean(feat * feat, axis=1, keepdims=True) + EPS)
    return (feat * scale).astype(BF16)


def gate_rows(normed, ids, router_ref):
    scores = dot(normed, router_ref[...])
    expert = lax.broadcasted_iota(jnp.int32, scores.shape, 1)
    score = jnp.sum(jnp.where(expert == ids, scores, 0.0), axis=1, keepdims=True)
    return jax.nn.sigmoid(score)


def send_rows(x, ids, layout):
    def work(ins, outs):
        outs[0][...] = sent_rows(normed_rows(ins[0]), ins[1][...], layout)

    outs = [((layout.sent, x.shape[1] // layout.cuts), BF16)]
    return on_core("send_rows", work, outs, x, ids)[0]


def send_normed(x, ids, router, layout, after=()):
    tokens, width = x.shape

    def work(ins, outs):
        normed, named = normed_rows(ins[0]), ins[1][...]
        outs[0][...] = sent_rows(normed, named, layout)
        outs[1][...] = jnp.broadcast_to(gate_rows(normed, named, ins[2]), (tokens, 128))

    outs = [((layout.sent, width // layout.cuts), BF16), ((tokens, 128), F32)]
    return on_core("send_normed", work, outs, x, ids, router, after=after)


def send_cotangents(cot, gate, ids, layout, after=()):
    def work(ins, outs):
        values = (ins[1][:, :1] * ins[0][...].astype(F32)).astype(BF16)
        outs[0][...] = sent_rows(values, ins[2][...], layout)

    outs = [((layout.sent, cot.shape[1] // layout.cuts), BF16)]
    return on_core("send_cotangents", work, outs, cot, gate, ids, after=after)[0]


def forward_out(x, router, back, ids, layout):
    def work(ins, outs):
        named = ins[3][...]
        gate = gate_rows(normed_rows(ins[0]), named, ins[1])
        rows = token_rows(ins[2], named, layout)
        outs[0][...] = (ins[0][...].astype(F32) + gate * rows).astype(BF16)

    return on_core("forward_out", work, [(x.shape, BF16)], x, router, back, ids)[0]


def backward_out(x, cot, back, ids, layout):
    width = x.shape[1]

    def work(ins, outs):
        feat = ins[0][...].astype(F32)
        scale = lax.rsqrt(jnp.mean(feat * feat, axis=1, keepdims=True) + EPS)
        normed_grad = token_rows(ins[2], ins[3][...], layout)
        along = jnp.sum(normed_grad * feat, axis=1, keepdims=True) / width
        feature_grad = scale * normed_grad - feat * (scale * scale * scale) * along
        outs[0][...] = (ins[1][...].astype(F32) + feature_grad).astype(BF16)

    return on_core("backward_out", work, [(x.shape, BF16)], x, cot, back, ids)[0]


def pack_halves(blocks, select, after=()):
    cuts, rows, _ = select.shape
    part = blocks.shape[1]
    half = cuts * part // 2

    def work(ins, outs):
        for c in range(cuts):
            begin = c * part % half
            outs[c * part // half][:, begin : begin + part] = dot(ins[1][c], ins[0][...]).astype(
                BF16
            )
        outs[2][...] = jnp.zeros(TOKEN[0], F32)

    lo, hi, token = on_core(
        "pack", work, [((rows, half), BF16)] * 2 + [TOKEN], blocks, select, after=after
    )
    return (lo, hi), token


def placed(parts, place_ref):
    cuts = place_ref.shape[0]
    part = 2 * parts[0].shape[1] // cuts
    rows = 0.0
    for c in range(cuts):
        begin = c * part % parts[0].shape[1]
        rows = rows + dot(
            place_ref[c], parts[c * part // parts[0].shape[1]][:, begin : begin + part]
        )
    return rows.astype(BF16)


def a_near_rows(blocks, up, after):
    half, hidden_units = up.shape[0] // 2, up.shape[1]
    rows = blocks[0][0].shape[0]

    def work(ins, outs):
        for j in range(3):
            hidden = dot(ins[2 * j][...], ins[6][:half]) + dot(ins[2 * j + 1][...], ins[6][half:])
            outs[0][j] = (hidden * jax.nn.sigmoid(hidden)).astype(BF16)

    flat = [half_block for block in blocks for half_block in block]
    return on_core("a_near", work, [((3, rows, hidden_units), BF16)], *flat, up, after=(after,))[0]


def a_far_rows(block, act, up, down):
    half, rows = up.shape[0] // 2, act.shape[1]

    def work(ins, outs):
        lo, hi, acts, up_ref, down_ref = ins
        hidden = dot(lo[...], up_ref[:half]) + dot(hi[...], up_ref[half:])
        far = (hidden * jax.nn.sigmoid(hidden)).astype(BF16)
        for h in range(2):
            weights = down_ref[:, h * half : (h + 1) * half]
            outs[h][0] = dot(far, weights).astype(BF16)
            outs[h][1] = dot(acts[1 + h], weights).astype(BF16)
        outs[2][...] = jnp.zeros(TOKEN[0], F32)

    outs = [((2, rows, half), BF16)] * 2 + [TOKEN]
    by_x, by_y, token = on_core("a_far", work, outs, *block, act, up, down)
    return (by_x, by_y), token


def a_second_rows(act, down, got, after=()):
    half, rows = down.shape[1] // 2, act.shape[1]

    def work(ins, outs):
        acts, down_ref, by_x, by_y = ins
        outs[0][...] = (dot(acts[1], down_ref[:, half:]) + by_y[0].astype(F32)).astype(BF16)
        outs[1][...] = (dot(acts[2], down_ref[:, :half]) + by_x[0].astype(F32)).astype(BF16)
        outs[2][...] = jnp.zeros(TOKEN[0], F32)

    outs = [((rows, half), BF16)] * 2 + [TOKEN]
    by_x, by_y, token = on_core("a_second", work, outs, act, down, *got, after=after)
    return (by_x, by_y), token


def a_total_rows(act, down, first, second, place, after):
    half = down.shape[1] // 2

    def work(ins, outs):
        acts, down_ref, first_x, first_y, second_x, second_y, place_ref = ins
        parts = []
        for h, (one, two) in enumerate(((first_x, second_y), (first_y, second_x))):
            cols = slice(h * half, (h + 1) * half)
            total = dot(acts[0], down_ref[:, cols]) + one[1].astype(F32) + two[...].astype(F32)
            parts.append(total.astype(BF16))
        outs[0][...] = placed(parts, place_ref)
        outs[1][...] = jnp.zeros(TOKEN[0], F32)

    outs = [((place.shape[1], 2 * half // place.shape[0]), BF16), TOKEN]
    return on_core("a_total", work, outs, act, down, *first, *second, place, after=after)


def b_hidden_rows(blocks, up, col):
    half, units, rows = up.shape[0] // 2, up.shape[1], blocks[0][0].shape[0]

    def work(ins, outs):
        up_ref, col_ref = ins[8:]
        for j in range(4):
            lo, hi = ins[2 * j][...], ins[2 * j + 1][...]
            outs[0][j] = dot(lo, up_ref[:half]) + dot(hi, up_ref[half:])
            outs[1][j] = dot(lo, col_ref[:half]) + dot(hi, col_ref[half:])

        outs[2][...] = jnp.zeros(TOKEN[0], F32)

    flat = [v for block in blocks for v in block]
    outs = [((4, rows, units), F32), ((4, rows, 128), F32), TOKEN]
    hidden, score, token = on_core("b_hidden", work, outs, *flat, up, col)
    return (hidden, score), token


def back_rows(hidden, score, c_lo, c_hi, down_ref):
    half = c_lo.shape[1]
    act_grad = dot(c_lo, down_ref[:half]) + dot(c_hi, down_ref[half:])
    sigma = jax.nn.sigmoid(hidden)
    active = hidden * sigma
    hid_grad = (act_grad * sigma * (1.0 + hidden * (1.0 - sigma))).astype(BF16)
    term = jnp.sum(active * act_grad, axis=1, keepdims=True) * jax.nn.sigmoid(-score[:, :1])
    return active.astype(BF16), hid_grad, term


def grad_rows(hid_grad, term, up_ref, line_ref, cols):
    return dot(hid_grad, up_ref[:, cols]) + term * line_ref[:, cols]


def b_near_rows(cots, early, up, down, line, after):
    half, units, rows = up.shape[1] // 2, up.shape[0], cots[0][0].shape[0]

    def work(ins, outs):
        hidden, score, up_ref, down_ref, line_ref = ins[6:]
        for j in range(3):
            lo, hi = ins[2 * j][...], ins[2 * j + 1][...]
            act, hid, term = back_rows(hidden[j], score[j], lo, hi, down_ref)
            outs[0][j], outs[1][j] = act, hid
            outs[2][j] = jnp.broadcast_to(term, (rows, 128))
            if j:
                cols = slice((j - 1) * half, j * half)
                outs[2 + j][...] = grad_rows(hid, term, up_ref, line_ref, cols).astype(BF16)

    flat = [v for block in cots for v in block]
    outs = [((3, rows, units), BF16)] * 2 + [((3, rows, 128), F32)]
    outs += [((rows, half), BF16)] * 2
    act, hid, term, by_x, by_y = on_core("b_near", work, outs, *flat, *early, up, down, line, after=after)
    return (act, hid, term), (by_x, by_y)


def b_far_rows(cots, early, up, down, line, after):
    half, units, rows = up.shape[1] // 2, up.shape[0], cots[0].shape[0]

    def work(ins, outs):
        lo, hi, hidden, score, up_ref, down_ref, line_ref = ins
        act, hid, term = back_rows(hidden[3], score[3], lo[...], hi[...], down_ref)
        outs[0][...], outs[1][...] = act, hid
        for h in range(2):
            part = grad_rows(hid, term, up_ref, line_ref, slice(h * half, (h + 1) * half))
            outs[2 + h][...] = part.astype(BF16)

    outs = [((rows, units), BF16)] * 2 + [((rows, half), BF16)] * 2
    args = (*cots, *early, up, down, line)
    act, hid, by_x, by_y = on_core("b_far", work, outs, *args, after=after)
    return (act, hid), (by_x, by_y)


def b_second_rows(near, up, line, got, plain):
    half, rows = up.shape[1] // 2, got[0].shape[0]

    def work(ins, outs):
        hids, terms, up_ref, line_ref, by_x, by_y = ins
        for side, ref in enumerate((by_y, by_x)):
            j, cols = 1 + side, slice((1 - side) * half, (2 - side) * half)
            part = grad_rows(hids[j], terms[j][:, :1], up_ref, line_ref, cols)
            outs[side][...] = (part + ref[...].astype(F32)).astype(BF16)

    outs = [((rows, half), BF16)] * 2
    return on_core("b_second", work, outs, near[1], near[2], up, line, *got, after=plain)


def b_total_rows(near, up, line, plain, second, place):
    half = up.shape[1] // 2

    def work(ins, outs):
        hids, terms, up_ref, line_ref, plain_x, plain_y, second_x, second_y, place_ref = ins
        parts = []
        for h, (one, two) in enumerate(((plain_x, second_y), (plain_y, second_x))):
            cols = slice(h * half, (h + 1) * half)
            part = grad_rows(hids[0], terms[0][:, :1], up_ref, line_ref, cols)
            parts.append((part + one[...].astype(F32) + two[...].astype(F32)).astype(BF16))
        outs[0][...] = placed(parts, place_ref)
        outs[1][...] = jnp.zeros(TOKEN[0], F32)

    outs = [((place.shape[1], 2 * half // place.shape[0]), BF16), TOKEN]
    return on_core("b_total", work, outs, near[1], near[2], up, line, *plain, *second, place)


def weight_grads(blocks, cots, near, far, after):
    half, units = blocks[0][0].shape[1], far[0].shape[1]
    tile = 256

    def work(ins, outs):
        xs, cs = ins[0:8], ins[8:16]
        acts = [ins[16][j] for j in range(3)] + [ins[18][...]]
        hids = [ins[17][j] for j in range(3)] + [ins[19][...]]
        for h in range(2):
            for begin in range(0, half, tile):
                cols, out = slice(begin, begin + tile), slice(h * half + begin, h * half + begin + tile)
                up_sum, down_sum = 0.0, 0.0
                for j in range(4):
                    up_sum = up_sum + dot(xs[2 * j + h][:, cols], hids[j], TN)
                    down_sum = down_sum + dot(acts[j], cs[2 * j + h][:, cols], TN)
                outs[0][out, :] = up_sum.astype(BF16)
                outs[1][:, out] = down_sum.astype(BF16)

    flat = [v for block in blocks for v in block] + [v for block in cots for v in block]
    outs = [((2 * half, units), BF16), ((units, 2 * half), BF16)]
    return on_core("weight_grads", work, outs, *flat, near[0], near[1], *far, after=(after,))


def across_planes(rows, layout):
    blocks = rows.reshape(layout.experts, layout.block, rows.shape[1])
    return depth_exchange(blocks, layout.experts).reshape(rows.shape)


def swap_pair(pair, experts):
    return plane_move(pair[0], experts, 1), plane_move(pair[1], experts, 2)


def spread_halves(mine, experts):
    x_lo, y_hi = swap_pair(mine, experts)
    x_hi, y_lo = swap_pair((mine[1], mine[0]), experts)
    return (x_lo, x_hi), (y_lo, y_hi)


def relay_halves(near, experts):
    return plane_move(near[0][0], experts, 2), plane_move(near[1][1], experts, 1)


def body(a_input, a_route, b_saved, b_grad, b_route, up_weight, down_weight, router):
    devices = lax.axis_size("expert")
    experts = router.shape[2]
    group = devices // experts
    tokens, width = a_input.shape[1], a_input.shape[2]
    layout = Layout(experts, tokens * a_route.shape[2] // experts + 2)
    here = lax.axis_index("expert") // group
    up, down, cols_r = up_weight[0], down_weight[0], router[0]
    b_ids = pipe_move(b_route[0].astype(BF16), lambda i, n: n - 1 - i).astype(jnp.int32)
    b_x = pipe_move(b_saved[0], lambda i, n: n - 1 - i)
    b_c = pipe_move(b_grad[0], lambda i, n: n - 1 - i)
    a_ids = a_route[0]
    own = jnp.where(jnp.arange(experts) == here, cols_r.astype(F32), 0.0)
    own = jnp.sum(own, axis=1, keepdims=True)
    line = own.reshape(1, width)
    col = jnp.where(jnp.arange(128)[None, :] == 0, own, 0.0).astype(BF16)
    place, select = layout.places()

    a_send = send_rows(a_input[0], a_ids, layout)
    up_turned, down_turned = up.T, down.T
    a_blocks = across_planes(a_send, layout)
    a_mine, _ = pack_halves(a_blocks, select, (up_turned, down_turned))
    a_near = spread_halves(a_mine, experts)
    a_far = relay_halves(a_near, experts)
    b_send, b_gate = send_normed(b_x, b_ids, cols_r, layout, (a_near[0][0],))
    b_blocks = across_planes(b_send, layout)

    act = a_near_rows((a_mine,) + a_near, up, b_gate)
    a_first, a_ready = a_far_rows(a_far, act, up, down)
    a_first = swap_pair(a_first, experts)
    b_mine, _ = pack_halves(b_blocks, select, (a_ready,))
    b_near = spread_halves(b_mine, experts)
    b_far = relay_halves(b_near, experts)

    a_second, a_done = a_second_rows(act, down, a_first)
    a_second = swap_pair(a_second, experts)
    c_send = send_cotangents(b_c, b_gate, b_ids, layout, (a_done,))
    c_blocks = across_planes(c_send, layout)
    c_mine, _ = pack_halves(c_blocks, select)
    c_near = spread_halves(c_mine, experts)
    c_far = relay_halves(c_near, experts)
    early, _ = b_hidden_rows((b_mine,) + b_near + (b_far,), up, col)

    cots = (c_mine,) + c_near
    near, b_plain = b_near_rows(cots, early, up_turned, down_turned, line, ())
    a_total, a_summed = a_total_rows(act, down, a_first, a_second, place, (near[2],))
    a_back = across_planes(a_total, layout)
    a_out = forward_out(a_input[0], cols_r, a_back, a_ids, layout)
    a_next = pipe_move(a_out, lambda i, n: i + 1)
    b_plain = swap_pair(b_plain, experts)
    far, b_relay = b_far_rows(c_far, early, up_turned, down_turned, line, (near[2], a_summed))
    b_relay = swap_pair(b_relay, experts)
    b_second = b_second_rows(near, up_turned, line, b_relay, b_plain)
    b_second = swap_pair(b_second, experts)
    b_total, b_done = b_total_rows(near, up_turned, line, b_plain, b_second, place)
    b_out = backward_out(b_x, b_c, across_planes(b_total, layout), b_ids, layout)
    b_next = pipe_move(b_out, lambda i, n: n - i)
    up_grad, down_grad = weight_grads(
        (b_mine,) + b_near + (b_far,), (c_mine,) + c_near + (c_far,), near, far, b_done
    )
    return (a_next[None], b_next[None], up_grad[None], down_grad[None])


def solution(mesh):
    return jax.shard_map(
        body,
        mesh=mesh,
        in_specs=(
            P("pipe", "expert", None),
            P("pipe", "expert", None),
            P("pipe", "expert", None),
            P("pipe", "expert", None),
            P("pipe", "expert", None),
            P("pipe", None, "expert"),
            P("pipe", "expert", None),
            P("pipe", None, None),
        ),
        out_specs=(
            P("pipe", "expert", None),
            P("pipe", "expert", None),
            P("pipe", None, "expert"),
            P("pipe", "expert", None),
        ),
        check_vma=False,
    )
```
